32 devices in a mesh: lat: 4 (over y, x), lon: 8 (over z, core).
Axes of the slice: x: 2, y: 2, z: 4, core: 2. Of those that a mesh axis runs over, the one named last changes fastest.
Arguments:
- innovation: float32 [64, 2048], P(None, ('lat', 'lon')), may hold values from -6 to 6
- obs_weight: float32 [64, 2048], P(None, ('lat', 'lon')), may hold values from 0.5 to 4
- jacobian: float32 [6144, 64, 128], P(('lat', 'lon')), may hold values from -0.5 to 0.5
- block_list: int32 [2, 6144], P(None, ('lat', 'lon')), may hold values from 0 to 512, as said below
- pass_counts: int32 [2], replicated, may hold values from 3 to 6, as said below
- kappa_h: float32 [64, 256, 128], P('lat', 'lon'), may hold values from 0.03 to 0.24
- kappa_v: float32 [64, 256, 128], P('lat', 'lon'), may hold values from 0.05 to 0.45
Outputs:
- increment: float32 [64, 256, 128], P('lat', 'lon')
- residual: float32 [64, 256, 128], P('lat', 'lon')
The draws below stay inside these ranges and needn't reach their ends.
Inputs may be any that keep to these rules, and one draw needn't show every extreme that they name: `pass_counts`: entry 0 counts lateral passes and entry 1 vertical passes; one of the two is 6 and the other is smaller. `block_list`: on each device the non-empty slots come first among its 192 slots, and in every latitude band some device has all 192 slots non-empty; an empty slot has block row 512.
All inputs are finite; a program needn't handle non-finite values.
Results may differ from the reference program's by a relative error of at most 0.0003.
Values sent between devices are 32-bit elements; how exact they have to be, the bound alone decides.
No kernel may reach another device: no remote copies, remote signals or barrier semaphores. Data moves between devices by JAX's collectives and lax.ppermute only.
A program may use at most 64 MiB of HBM per device.

```python
import math
import jax
import jax.numpy as jnp
from jax import lax

CLAT = 16
CLON = 32
LEVELS = 128
OBSB = 64
ROWS_DEV = 64
CAP = 192
PASS_MIN = 3
PASS_MAX = 6
ITERS = 2
NLAT = 64
NLON = 256
ROWS_LAT = 512
OBSROWS = 2048
BLOCKS = 6144
N_LAT = 4
N_LON = 8


def draw_block_list(key, part):
    subkeys = jax.random.split(jax.random.fold_in(key, 41), 4)
    device_count = BLOCKS // CAP
    lon_count = ROWS_LAT // ROWS_DEV
    band_count = device_count // lon_count
    loaded = jax.random.randint(subkeys[0], (device_count,), CAP // 8, CAP // 2 + 1)
    busiest = jax.random.randint(subkeys[1], (band_count, 1), 0, lon_count)
    position = jnp.arange(lon_count, dtype=jnp.int32)[None, :]
    crowded = ((position == busiest) | (position == (busiest + 1) % lon_count)).reshape(-1)
    loaded = jnp.where(crowded, CAP, loaded)
    slot_ids = jnp.arange(CAP, dtype=jnp.int32)[None, :]
    active = slot_ids < loaded[:, None]
    row_ids = jax.random.randint(subkeys[2], (device_count, CAP), 0, ROWS_LAT)
    row_ids = jnp.where(active, row_ids, ROWS_LAT)
    col_ids = jax.random.randint(subkeys[3], (device_count, CAP), 0, CLAT * CLON)
    return jnp.stack([row_ids.reshape(-1), col_ids.reshape(-1)]).astype(jnp.int32)


def draw_pass_counts(key, part):
    subkeys = jax.random.split(jax.random.fold_in(key, 23), 2)
    drawn = jax.random.randint(subkeys[0], (2,), PASS_MIN, PASS_MAX)
    chosen = jax.random.randint(subkeys[1], (), 0, 2)
    return jnp.where(jnp.arange(2) == chosen, PASS_MAX, drawn).astype(jnp.int32)


def block_scale(rng, dims, cuts, smallest, high):
    factor_of, own = 1.0, jax.random.fold_in(rng, 6)
    for axis_at, blocks in cuts:
        heights = jnp.exp(jax.random.uniform(jax.random.fold_in(own, axis_at), (blocks,), jnp.float32, smallest / len(cuts), high / len(cuts)))
        factor_of = factor_of * jnp.repeat(heights, dims[axis_at] // blocks).reshape([-1 if axis == axis_at else 1 for axis in range(len(dims))])
    return factor_of


def scatter_about(key, extent, scale, most, cuts=(), kind=jnp.bfloat16):
    entries = scale * jax.random.normal(key, extent, jnp.float32)
    if cuts:
        entries = entries * block_scale(key, extent, cuts, -0.22, 0.18)
    return jnp.clip(entries, -most, most).astype(kind)


def setup_inputs(seed: int = 0) -> dict:
    key_of = jax.random.split(jax.random.key(seed), 8)
    innovation = scatter_about(key_of[0], (OBSB, OBSROWS), 1.0, 6.0, ((1, 32),), jnp.float32)
    obs_weight = jnp.clip(jnp.exp(math.log(4.0) - 2.0794415 * jax.random.uniform(key_of[1], (OBSB, OBSROWS), jnp.float32) ** block_scale(key_of[1], (OBSB, OBSROWS), ((1, 32),), -0.2, 0.2)), 0.5, 4.0)
    jacobian = scatter_about(key_of[2], (BLOCKS, OBSB, LEVELS), LEVELS ** -0.5, 0.5, ((0, 32),), jnp.float32)
    block_list = draw_block_list(jax.random.fold_in(key_of[7], 71), 0)
    pass_counts = draw_pass_counts(jax.random.fold_in(key_of[7], 71), 0)
    kappa_h = jnp.clip(jnp.exp(math.log(0.24) - 2.0794415 * jax.random.uniform(key_of[5], (NLAT, NLON, LEVELS), jnp.float32) ** block_scale(key_of[5], (NLAT, NLON, LEVELS), ((0, 4), (1, 8)), -0.2, 0.2)), 0.03, 0.24)
    kappa_v = jnp.clip(jnp.exp(math.log(0.45) - 2.1972245 * jax.random.uniform(key_of[6], (NLAT, NLON, LEVELS), jnp.float32) ** block_scale(key_of[6], (NLAT, NLON, LEVELS), ((0, 4), (1, 8)), -0.2, 0.2)), 0.05, 0.45)
    return {"innovation": innovation, "obs_weight": obs_weight, "jacobian": jacobian, "block_list": block_list, "pass_counts": pass_counts, "kappa_h": kappa_h, "kappa_v": kappa_v}


def vertical_faces(kappa_v):
    upper_face = jnp.sqrt(kappa_v[..., :-1] * kappa_v[..., 1:])
    zero_face = jnp.zeros(kappa_v.shape[:-1] + (1,), jnp.float32)
    return (jnp.concatenate([upper_face, zero_face], -1), jnp.concatenate([zero_face, upper_face], -1))

def vertical_pass(current, face_below, face_above):
    zero_face = jnp.zeros(current.shape[:-1] + (1,), jnp.float32)
    higher = jnp.concatenate([current[..., 1:], zero_face], -1)
    lower_level = jnp.concatenate([zero_face, current[..., :-1]], -1)
    return current + face_below * (higher - current) + face_above * (lower_level - current)

def lateral_faces(kappa_h):
    padded = jnp.pad(kappa_h, ((1, 1), (0, 0), (0, 0)))
    return (jnp.sqrt(kappa_h * padded[:-2]), jnp.sqrt(kappa_h * padded[2:]), jnp.sqrt(kappa_h * jnp.roll(kappa_h, 1, axis=1)), jnp.sqrt(kappa_h * jnp.roll(kappa_h, -1, axis=1)))

def lateral_pass(current, face_set):
    padded = jnp.pad(current, ((1, 1), (0, 0), (0, 0)))
    return current + face_set[0] * (padded[:-2] - current) + face_set[1] * (padded[2:] - current) + face_set[2] * (jnp.roll(current, 1, axis=1) - current) + face_set[3] * (jnp.roll(current, -1, axis=1) - current)

def reference(innovation, obs_weight, jacobian, block_list, pass_counts, kappa_h, kappa_v):
    lateral_count = pass_counts[0]
    vertical_count = pass_counts[1]
    face_set = lateral_faces(kappa_h)
    face_below, face_above = vertical_faces(kappa_v)

    def vertical(current):
        return lax.fori_loop(0, vertical_count, lambda counter, running: vertical_pass(running, face_below, face_above), current)

    def lateral(current):
        return lax.fori_loop(0, lateral_count, lambda counter, running: lateral_pass(running, face_set), current)

    def spread(current):
        return lateral(vertical(current))

    def spread_adjoint(current):
        return vertical(lateral(current))
    device_count = N_LAT * N_LON
    column_count = CLAT * CLON

    def to_columns(current):
        return current.reshape(N_LAT, CLAT, N_LON, CLON, LEVELS).transpose(0, 2, 1, 3, 4).reshape(device_count * column_count, LEVELS)

    def from_columns(columns):
        return columns.reshape(N_LAT, N_LON, CLAT, CLON, LEVELS).transpose(0, 2, 1, 3, 4).reshape(NLAT, NLON, LEVELS)
    block_rows = block_list[0].reshape(device_count, CAP)
    block_cols = block_list[1].reshape(device_count, CAP)
    active = block_rows < ROWS_LAT
    band_index = (jnp.arange(device_count, dtype=jnp.int32) // N_LON)[:, None]
    obs_ids = jnp.where(active, band_index * ROWS_LAT + block_rows, 0).astype(jnp.int32).reshape(-1)
    cell_ids = (jnp.arange(device_count, dtype=jnp.int32)[:, None] * column_count + block_cols).astype(jnp.int32).reshape(-1)
    active_mask = active.reshape(-1).astype(jnp.float32)[:, None]

    def observe(current):
        picked = to_columns(current)[cell_ids]
        block_obs = jnp.einsum('bok,bk->bo', jacobian, picked, precision=lax.Precision.HIGHEST) * active_mask
        return jax.ops.segment_sum(block_obs, obs_ids, num_segments=OBSROWS).T

    def observe_adjoint(weighted):
        taken = weighted.T[obs_ids] * active_mask
        contrib = jnp.einsum('bok,bo->bk', jacobian, taken, precision=lax.Precision.HIGHEST)
        return from_columns(jax.ops.segment_sum(contrib, cell_ids, num_segments=device_count * column_count))
    gradient = spread_adjoint(observe_adjoint(obs_weight * innovation))
    solution = jnp.zeros_like(gradient)
    residual = gradient
    direction = gradient
    norm_now = jnp.sum(residual * residual)
    for iteration in range(ITERS):
        image_vec = direction + spread_adjoint(observe_adjoint(obs_weight * observe(spread(direction))))
        alpha_step = norm_now / jnp.sum(direction * image_vec)
        solution = solution + alpha_step * direction
        residual = residual - alpha_step * image_vec
        if iteration + 1 < ITERS:
            norm_next = jnp.sum(residual * residual)
            direction = residual + norm_next / norm_now * direction
            norm_now = norm_next
    return (spread(solution), residual)
```

```python
import functools

import jax
import jax.numpy as jnp
from jax import lax
from jax.experimental import pallas as pl
from jax.experimental.pallas import tpu as pltpu
from jax.sharding import PartitionSpec as P

LANES = 128
VMEM_LIMIT = 48 * 1024 * 1024
REACH = 6
FRAME = 2 * REACH


def split3(x):
    high = x.astype(jnp.bfloat16)
    rest = x - high.astype(jnp.float32)
    mid = rest.astype(jnp.bfloat16)
    low = (rest - mid.astype(jnp.float32)).astype(jnp.bfloat16)
    return high, mid, low


def fold_sum(x):
    total = None
    for i in range(x.shape[0] // 8):
        for j in range(x.shape[1] // LANES):
            tile = x[8 * i:8 * i + 8, LANES * j:LANES * j + LANES]
            total = tile if total is None else total + tile
    return total


def copies(pairs, sems):
    started = [pltpu.make_async_copy(src, dst, sems.at[i]) for i, (src, dst) in enumerate(pairs)]
    for copy in started:
        copy.start()
    return started


def lateral_pass(buf, face_lat, face_lon, first, last, left, right):
    cols = slice(left, right)
    width = right - left

    def body(step, carry):
        current, flux_above = carry
        row = first + 2 * step
        for k in range(2):
            below = buf[row + k + 1, cols]
            flux = face_lat[row + k, cols] * (below - current)
            side = face_lon[row + k, cols] * (pltpu.roll(current, width - 1, 0) - current)
            buf[row + k, cols] = current + ((flux - flux_above) + (side - pltpu.roll(side, 1, 0)))
            current, flux_above = below, flux
        return current, flux_above

    start = buf[first, cols]
    flux_start = face_lat[first - 1, cols] * (start - buf[first - 1, cols])
    lax.fori_loop(0, (last - first) // 2, body, (start, flux_start))


def lateral_passes(buf, face_lat, face_lon, nh, begin, end, left, right):
    rows, lost = buf.shape[0], FRAME - 2 * nh

    def body(p, c):
        lateral_pass(buf, face_lat, face_lon, lost + p, rows - lost - p, left, right)
        return c

    lax.fori_loop(begin + 1, end + 1, body, 0)


def last_lateral(buf, face_lat, face_lon, nh, lon_cells):
    close = jnp.minimum(nh, 4)
    lateral_passes(buf, face_lat, face_lon, nh, nh, 2 * nh - close, 0, buf.shape[1])
    left = (FRAME - 4) // 8 * 8
    right = -(-(FRAME + lon_cells + 4) // 8) * 8
    lateral_passes(buf, face_lat, face_lon, nh, 2 * nh - close, 2 * nh, left, right)


def vertical_passes(buf, keep, up, down, first, last, tile, offset, nv, left, right):
    cols = slice(left, right)

    def sweep(p, c):
        def rows(t, c):
            at = [first + t * tile + k for k in range(tile)]
            values = [buf[i, cols] for i in at]
            values = [
                keep[i - offset, cols] * w
                + (up[i - offset, cols] * pltpu.roll(w, LANES - 1, 1)
                   + down[i - offset, cols] * pltpu.roll(w, 1, 1))
                for i, w in zip(at, values)
            ]
            for i, w in zip(at, values):
                buf[i, cols] = w
            return c
        return lax.fori_loop(0, (last - first) // tile, rows, c)

    lax.fori_loop(0, nv, sweep, 0)


def place_halos(flags, buf, own, strips, sides, reach, dims):
    lat_cells, lon_cells = dims
    from_a, from_b = strips
    from_x, from_s = sides
    base = FRAME - reach
    lat_even, lon_even = flags[0] == 0, flags[1] == 0
    south = FRAME + lat_cells
    row_a = jnp.where(lat_even, south, base)
    row_b = jnp.where(lat_even, base, south)
    cols = slice(FRAME, FRAME + lon_cells)

    def put_own(i, c):
        buf[FRAME + i, cols] = own[pl.ds(pl.multiple_of(i * lon_cells, lon_cells), lon_cells)]
        return c

    def put_strips(i, c):
        buf[row_a + i, cols] = from_a(i)
        buf[row_b + i, cols] = from_b(i)
        return c

    lax.fori_loop(0, lat_cells, put_own, 0)
    lax.fori_loop(0, reach, put_strips, 0)
    west = slice(base, FRAME)
    east = slice(FRAME + lon_cells, FRAME + lon_cells + reach)

    def put_sides(first, second):
        def put(i, c):
            for k in range(2):
                buf[base + 2 * i + k, first] = from_x(i, k)
                buf[base + 2 * i + k, second] = from_s(i, k)
            return c
        lax.fori_loop(0, (lat_cells + 2 * reach) // 2, put, 0)

    pl.when(lon_even)(lambda: put_sides(east, west))
    pl.when(jnp.logical_not(lon_even))(lambda: put_sides(west, east))


def strip_of(ref, lon_cells, skip=0):
    return lambda i: ref[pl.ds(pl.multiple_of((skip + i) * lon_cells, lon_cells), lon_cells)]


def side_of(ref):
    return lambda i, k: ref[2 * i + k]


def folded_side_of(ref, skip, reach):
    return lambda i, k: ref[skip + i, k * reach:k * reach + reach]


def faces_kernel(dims, flags, root_h, root_v, from_a, from_b, from_x, from_s, *refs):
    lat_cells, lon_cells = dims
    out, (face_lat, face_lon, keep, up, down, buf, sems) = refs[:5], refs[5:]
    rows = lat_cells + 2 * FRAME
    width = buf.shape[1]
    place_halos(
        flags, buf, root_h, (strip_of(from_a, lon_cells), strip_of(from_b, lon_cells)),
        (side_of(from_x), side_of(from_s)), FRAME, dims,
    )

    def clear(first):
        def body(i, c):
            buf[first + i] = jnp.zeros((width, LANES), jnp.float32)
            return c
        lax.fori_loop(0, FRAME, body, 0)

    pl.when(flags[2] == 1)(lambda: clear(0))
    pl.when(flags[3] == 1)(lambda: clear(FRAME + lat_cells))

    def lateral(i, c):
        here = buf[i]
        face_lat[i] = here * buf[i + 1]
        face_lon[i] = here * pltpu.roll(here, width - 1, 0)
        return c

    lax.fori_loop(0, rows - 1, lateral, 0)
    here = buf[rows - 1]
    face_lat[rows - 1] = jnp.zeros((width, LANES), jnp.float32)
    face_lon[rows - 1] = here * pltpu.roll(here, width - 1, 0)
    side = copies([(face_lat, out[0]), (face_lon, out[1])], sems)
    place_halos(
        flags, buf, root_v, (strip_of(from_a, lon_cells, FRAME), strip_of(from_b, lon_cells, FRAME)),
        (folded_side_of(from_x, rows, REACH), folded_side_of(from_s, rows, REACH)), REACH, dims,
    )
    top = lax.broadcasted_iota(jnp.int32, (width, LANES), 1) == LANES - 1

    def vertical(i, c):
        here = buf[FRAME - REACH + i]
        face = jnp.where(top, 0.0, here * pltpu.roll(here, LANES - 1, 1))
        below = pltpu.roll(face, 1, 1)
        up[i] = face
        down[i] = below
        keep[i] = 1.0 - (face + below)
        return c

    lax.fori_loop(0, lat_cells + 2 * REACH, vertical, 0)
    level = copies([(keep, out[2]), (up, out[3]), (down, out[4])], sems.at[pl.ds(2, 3)])
    for copy in side + level:
        copy.wait()


def observe(cells, jac, field, out):
    slots, obs, _ = jac.shape
    lane = lax.broadcasted_iota(jnp.int32, (obs, LANES), 1)

    def part(first, count):
        def body(step, acc):
            for k in range(8):
                slot = first + step * 8 + k
                row = field[pl.ds(cells[slot], 1), :]
                value = jnp.sum(jac[slot] * row, axis=1, keepdims=True)
                acc = jnp.where(lane == step * 8 + k, value, acc)
            return acc
        return lax.fori_loop(0, count // 8, body, jnp.zeros((obs, LANES), jnp.float32))

    out[0:obs] = part(0, LANES)
    rest = part(LANES, slots - LANES)
    out[obs:obs + obs // 2] = rest[:obs // 2] + pltpu.roll(rest[obs // 2:], LANES // 2, 1)


def pack_kernel(innovation, obs_weight, rows, out):
    obs, own = innovation.shape
    weight = obs_weight[...]
    out[0:obs, 0:own] = weight * innovation[...]
    out[0:obs, own:2 * own] = weight
    out[obs:obs + 8] = rows[...]


def adjoint_kernel(first_call, parts, *refs):
    pieces, refs = refs[:2 * parts], refs[2 * parts:]
    if first_call:
        own_hot, cell_hot, jac_hbm, field, weight, band, jac, taken, contrib, sems = refs
    else:
        row_hot, weight, own_hot, cell_hot, jac_hbm, field, sums, jac, taken, contrib, sems = refs
    slots, obs, _ = jac.shape
    group = 32
    groups = slots // group

    def chunk(g):
        place = pl.ds(g * group, group)
        return pltpu.make_async_copy(jac_hbm.at[place], jac.at[place], sems.at[g])

    for g in range(groups):
        chunk(g).start()
    if first_call:
        own = weight.shape[1] // (2 * parts)
        for d, piece in enumerate(pieces):
            band[:, d * own:d * own + own] = piece[0:obs, 0:own]
            weight[:, d * own:d * own + own] = piece[0:obs, own:2 * own]
        weighted = band[...]
    else:
        total = None
        scal = None
        for d, piece in enumerate(pieces):
            fold = piece[obs:obs + obs // 2]
            rest = jnp.concatenate([fold, pltpu.roll(fold, LANES // 2, 1)], axis=0)
            values = jnp.concatenate([piece[0:obs], rest], axis=1)
            stack = jnp.concatenate(split3(values), axis=0)
            prod = jnp.dot(stack, row_hot[d], preferred_element_type=jnp.float32)
            total = prod if total is None else total + prod
            tail = piece[obs + obs // 2:obs + obs // 2 + 8]
            scal = tail if scal is None else scal + tail
        total = total[:obs] + (total[obs:2 * obs] + total[2 * obs:])
        weighted = weight[...] * total
        sums[0:8] = scal
        sums[8:16] = fold_sum(weighted * total)
    stack = jnp.concatenate(split3(weighted), axis=0)
    picked = jnp.dot(stack, own_hot[...], preferred_element_type=jnp.float32)
    picked = picked[:obs] + (picked[obs:2 * obs] + picked[2 * obs:])
    taken[0] = picked[:, :LANES]
    taken[1] = picked[:, LANES:]

    def body(g, c):
        chunk(g).wait()
        per = LANES // group
        values = pltpu.roll(taken[g // per], LANES - (g % per) * group, 1)
        for k in range(group):
            slot = g * group + k
            contrib[pl.ds(slot, 1), :] = jnp.sum(jac[slot] * values[:, k:k + 1], axis=0, keepdims=True)
        return c

    lax.fori_loop(0, groups, body, 0)
    out = None
    for piece in split3(contrib[...]):
        prod = jnp.dot(cell_hot[...], piece, preferred_element_type=jnp.float32)
        out = prod if out is None else out + prod
    field[...] = out


def spread_kernel(dims, first_call, *refs):
    lat_cells, lon_cells = dims
    flags, cells, own, from_a, from_b, from_x, from_s = refs[:7]
    refs = refs[7:]
    if not first_call:
        scal, refs = refs[0], refs[1:]
    faces_hbm, jac_hbm, refs = refs[:5], refs[5], refs[6:]
    if not first_call:
        grad_hbm, spread_hbm, refs = refs[0], refs[1], refs[2:]
    one_hbm, two_hbm, message = refs[:3]
    refs = refs[3:]
    face_lat, face_lon, keep, up, down, jac, one, two, grad, buf, mid, sems = refs
    loads = copies(
        list(zip(faces_hbm, (face_lat, face_lon, keep, up, down))) + [(jac_hbm, jac)], sems
    )
    if not first_call:
        old_loads = copies([(grad_hbm, grad), (spread_hbm, two)], sems.at[pl.ds(6, 2)])
    nh, nv = flags[4], flags[5]
    rows = lat_cells + 2 * FRAME
    width = buf.shape[1]
    place_halos(
        flags, buf, own, (strip_of(from_a, lon_cells), strip_of(from_b, lon_cells)),
        (side_of(from_x), side_of(from_s)), FRAME, dims,
    )
    for load in loads[:2]:
        load.wait()
    lateral_passes(buf, face_lat, face_lon, nh, 0, nh, 0, width)
    border = FRAME - REACH
    tall = lat_cells + 2 * REACH
    vertical = functools.partial(
        vertical_passes, buf, keep, up, down, border, border + tall, tall // 2, border, nv, 0, width
    )
    for load in loads[2:5]:
        load.wait()
    vertical()

    def save(i, c):
        mid[i] = buf[FRAME + i]
        return c

    lax.fori_loop(0, lat_cells, save, 0)
    vertical()
    last_lateral(buf, face_lat, face_lon, nh, lon_cells)
    cols = slice(FRAME, FRAME + lon_cells)
    if not first_call:
        rr = jnp.sum(scal[0:8])
        alpha = rr / (rr + jnp.sum(scal[8:16]))
        for load in old_loads:
            load.wait()

    def finish(i, acc):
        place = pl.ds(pl.multiple_of(i * lon_cells, lon_cells), lon_cells)
        vector = mid[i, cols]
        after = buf[FRAME + i, cols]
        if first_call:
            one[place] = vector
            two[place] = after
        else:
            old = two[place]
            base = grad[place]
            applied = base + vector
            one[place] = applied
            two[place] = old - alpha * (old + after)
            vector = base - alpha * applied
        square = vector * vector
        for j in range(lon_cells // 8):
            acc = acc + square[8 * j:8 * j + 8]
        return acc

    norm = lax.fori_loop(0, lat_cells, finish, jnp.zeros((8, LANES), jnp.float32))
    stores = copies([(one, one_hbm), (two, two_hbm)], sems.at[pl.ds(8, 2)])
    loads[5].wait()
    obs = jac.shape[1]
    observe(cells, jac, two, message)
    message[obs + obs // 2:] = norm
    for store in stores:
        store.wait()


def final_kernel(dims, *refs):
    lat_cells, lon_cells = dims
    flags, own, from_a, from_b, from_x, from_s, scal0, scal1 = refs[:8]
    hbm, (increment, residual), refs = refs[8:17], refs[17:19], refs[19:]
    face_lat, face_lon, keep, up, down, grad, spread, image, spread_next, buf, sems = refs
    loads = copies(list(zip(hbm, refs[:9])), sems)
    nh, nv = flags[4], flags[5]
    place_halos(
        flags, buf, own, (strip_of(from_a, lon_cells), strip_of(from_b, lon_cells)),
        (side_of(from_x), side_of(from_s)), REACH, dims,
    )
    for load in loads[:2]:
        load.wait()
    last_lateral(buf, face_lat, face_lon, nh, lon_cells)
    left = FRAME // 8 * 8
    right = -(-(FRAME + lon_cells) // 8) * 8
    for load in loads[2:]:
        load.wait()
    vertical_passes(
        buf, keep, up, down, FRAME, FRAME + lat_cells, lat_cells, FRAME - REACH, nv, left, right
    )
    rr0 = jnp.sum(scal0[0:8])
    alpha0 = rr0 / (rr0 + jnp.sum(scal0[8:16]))
    rr1 = jnp.sum(scal1[0:8])
    beta = rr1 / rr0
    alpha1 = rr1 / ((rr1 + jnp.sum(scal1[8:16])) - beta * (rr1 / alpha0))
    cols = slice(FRAME, FRAME + lon_cells)

    def finish(i, c):
        place = pl.ds(pl.multiple_of(i * lon_cells, lon_cells), lon_cells)
        applied = image[place]
        rest = grad[place] - alpha0 * applied
        residual[place] = rest - alpha1 * ((rest + buf[FRAME + i, cols]) + beta * applied)
        old = spread[place]
        increment[place] = alpha0 * old + alpha1 * (spread_next[place] + beta * old)
        return c

    lax.fori_loop(0, lat_cells, finish, 0)


def local(innovation, obs_weight, jacobian, block_list, pass_counts, kappa_h, kappa_v):
    lat_cells, lon_cells, levels = kappa_h.shape
    cells_n = lat_cells * lon_cells
    slots, obs, _ = jacobian.shape
    own_rows = innovation.shape[1]
    n_lat, n_lon = lax.axis_size("lat"), lax.axis_size("lon")
    parts = n_lon // 2
    lat, lon = lax.axis_index("lat"), lax.axis_index("lon")
    lat_even, lon_even = lat % 2 == 0, lon % 2 == 0
    f32 = jnp.float32

    def swap(n, k):
        return [(i, i ^ k) for i in range(n)]

    def odd_pairs(n):
        return [(i, (i + 1) % n if i % 2 else (i - 1) % n) for i in range(n)]

    def send(x, axis, pairs):
        return lax.ppermute(x, axis, pairs)

    def gather_band(x):
        near = [x] + [send(x, "lon", swap(n_lon, 2 * k)) for k in range(1, parts)]
        return near + [send(piece, "lon", swap(n_lon, 1)) for piece in near]

    def lat_strips(top, bottom, tail=None):
        to_a = jnp.where(lat_even, bottom, top)
        to_b = jnp.where(lat_even, top, bottom)
        if tail is not None:
            to_a = jnp.concatenate([to_a, tail], 0)
            to_b = jnp.concatenate([to_b, tail], 0)
        return send(to_a, "lat", swap(n_lat, 1)), send(to_b, "lat", odd_pairs(n_lat))

    def side_strips(ext, reach):
        west, east = ext[:, :reach], ext[:, lon_cells - reach:]
        return jnp.where(lon_even, east, west), jnp.where(lon_even, west, east)

    def lon_send(to_x, to_s):
        return send(to_x, "lon", swap(n_lon, 1)), send(to_s, "lon", odd_pairs(n_lon))

    def stacked(own, from_a, from_b, reach):
        shape = (reach, lon_cells, levels)
        from_a, from_b = from_a.reshape(shape), from_b.reshape(shape)
        north = jnp.where(lat_even, from_b, from_a)
        south = jnp.where(lat_even, from_a, from_b)
        return jnp.concatenate([north, own.reshape(lat_cells, lon_cells, levels), south], 0)

    def halo(own, reach, tail=None):
        count = reach * lon_cells
        from_a, from_b = lat_strips(own[:count], own[cells_n - count:], tail)
        sums = None
        if tail is not None:
            if n_lat == 4:
                sums = (tail + send(tail, "lat", swap(n_lat, 2))) + (from_a[count:] + from_b[count:])
            else:
                sums = lax.psum(tail, "lat")
            from_a, from_b = from_a[:count], from_b[:count]
        ext = stacked(own, from_a, from_b, reach)
        from_x, from_s = lon_send(*side_strips(ext, reach))
        return (from_a, from_b, from_x, from_s), sums

    vmem = pl.BlockSpec(memory_space=pltpu.VMEM)
    smem = pl.BlockSpec(memory_space=pltpu.SMEM)
    hbm = pl.BlockSpec(memory_space=pl.ANY)
    params = pltpu.CompilerParams(vmem_limit_bytes=VMEM_LIMIT)
    shape = lambda *dims: jax.ShapeDtypeStruct(dims, f32)
    scratch = lambda *dims: pltpu.VMEM(dims, f32)
    rows_h = lat_cells + 2 * FRAME
    rows_v = lat_cells + 2 * REACH
    width = lon_cells + 2 * FRAME
    band_rows = n_lon * own_rows
    dims = (lat_cells, lon_cells)
    field = shape(cells_n, levels)
    msg = shape(obs + obs // 2 + 8, LANES)
    wide, tall = shape(rows_h, width, levels), shape(rows_v, width, levels)
    wide_vmem, tall_vmem = scratch(rows_h, width, levels), scratch(rows_v, width, levels)
    field_vmem = scratch(cells_n, levels)
    jac_vmem = scratch(slots, obs, levels)
    faces_vmem = [wide_vmem] * 2 + [tall_vmem] * 3
    sems = lambda count: pltpu.SemaphoreType.DMA((count,))

    def call(kernel, name, outs, ins, scalars=0, far_in=(), far_out=False, scratches=()):
        out_specs = jax.tree.map(lambda _: vmem, outs)
        if far_out:
            out_specs = (hbm,) * far_out + out_specs[far_out:]
        specs = [smem] * scalars + [vmem] * (len(ins) - scalars) + [hbm] * len(far_in)
        return pl.pallas_call(
            kernel, out_shape=outs, in_specs=specs, out_specs=out_specs,
            scratch_shapes=list(scratches), compiler_params=params, name=name,
        )(*ins, *far_in)

    rows_own = jnp.pad(block_list[0].astype(f32), (0, 2 * LANES - slots), constant_values=-1.0)
    first = call(pack_kernel, "pack", shape(obs + 8, LANES),
                 (innovation, obs_weight, jnp.pad(rows_own.reshape(2, LANES), ((0, 6), (0, 0)))))
    band = gather_band(first)

    kh_lat = FRAME * lon_cells
    kv_lat = REACH * lon_cells
    kh2, kv2 = (jnp.sqrt(v).reshape(cells_n, levels) for v in (kappa_h, kappa_v))
    k_strips = lat_strips(
        jnp.concatenate([kh2[:kh_lat], kv2[:kv_lat]], 0),
        jnp.concatenate([kh2[cells_n - kh_lat:], kv2[cells_n - kv_lat:]], 0),
    )
    hx, hs = side_strips(stacked(kh2, k_strips[0][:kh_lat], k_strips[1][:kh_lat], FRAME), FRAME)
    vx, vs = side_strips(stacked(kv2, k_strips[0][kh_lat:], k_strips[1][kh_lat:], REACH), REACH)
    fold = lambda v: v.reshape(rows_v // 2, 2 * REACH, levels)
    k_messages = [jnp.concatenate([hx, fold(vx)], 0), jnp.concatenate([hs, fold(vs)], 0)]

    def place_of(row):
        row = row.astype(jnp.int32)
        key = (row // own_rows) ^ lon
        at = (key // 2 + parts * (key % 2)) * own_rows + row % own_rows
        return jnp.where((row >= 0) & (row < band_rows), at, -1)

    all_at = place_of(jnp.stack([piece[obs:obs + 2] for piece in band]).reshape(n_lon, 2 * LANES))
    row_iota = jnp.arange(band_rows, dtype=jnp.int32)
    row_hot = (all_at[:, :, None] == row_iota[None, None, :]).astype(jnp.bfloat16)
    own_at = place_of(rows_own)
    own_hot = (row_iota[:, None] == own_at[None, :]).astype(jnp.bfloat16)
    cells = jnp.clip(block_list[1], 0, cells_n - 1)
    cell_hot = (jnp.arange(cells_n, dtype=jnp.int32)[:, None] == cells[None, :]).astype(jnp.bfloat16)
    flags = jnp.stack([
        lat % 2, lon % 2, (lat == 0).astype(jnp.int32), (lat == n_lat - 1).astype(jnp.int32),
        pass_counts[0], pass_counts[1],
    ]).astype(jnp.int32)

    adj_scratch = [jac_vmem, scratch(2, obs, LANES), scratch(slots, levels), sems(slots // 32)]
    band[0], k_messages = lax.optimization_barrier((band[0], k_messages))
    k_sides = lon_send(*k_messages)
    own, weight = call(
        functools.partial(adjoint_kernel, True, parts), "adjoint_first",
        (field, shape(obs, band_rows)), (*band, own_hot, cell_hot), far_in=(jacobian,),
        scratches=[scratch(obs, band_rows)] + adj_scratch)
    faces = call(
        functools.partial(faces_kernel, dims), "faces", (wide, wide, tall, tall, tall),
        (flags, kh2, kv2, *k_strips, *k_sides), 1, far_out=5,
        scratches=faces_vmem + [wide_vmem, sems(5)])
    halos, _ = halo(own, FRAME)
    spread_scratch = faces_vmem + [jac_vmem] + [field_vmem] * 3 + [
        wide_vmem, scratch(lat_cells, width, levels), sems(10)]
    grad, spread, message = call(
        functools.partial(spread_kernel, dims, True), "spread_first", (field, field, msg),
        (flags, cells, own, *halos), 2, (*faces, jacobian), 2, spread_scratch)

    def adjoint(message):
        return call(
            functools.partial(adjoint_kernel, False, parts), "adjoint_next",
            (field, shape(16, LANES)), (*gather_band(message), row_hot, weight, own_hot, cell_hot),
            far_in=(jacobian,), scratches=adj_scratch)

    own, sums = adjoint(message)
    halos, scal0 = halo(own, FRAME, sums)
    image, spread_next, message = call(
        functools.partial(spread_kernel, dims, False), "spread_next", (field, field, msg),
        (flags, cells, own, *halos, scal0), 2, (*faces, jacobian, grad, spread), 2, spread_scratch)
    own, sums = adjoint(message)
    halos, scal1 = halo(own, REACH, sums)
    increment, residual = call(
        functools.partial(final_kernel, dims), "final", (field, field),
        (flags, own, *halos, scal0, scal1), 1,
        (*faces, grad, spread, image, spread_next), 0,
        faces_vmem + [field_vmem] * 4 + [wide_vmem, sems(9)])
    block = (lat_cells, lon_cells, levels)
    return increment.reshape(block), residual.reshape(block)


def solution(mesh):
    return jax.shard_map(
        local,
        mesh=mesh,
        in_specs=(
            P(None, ("lat", "lon")),
            P(None, ("lat", "lon")),
            P(("lat", "lon"), None, None),
            P(None, ("lat", "lon")),
            P(),
            P("lat", "lon", None),
            P("lat", "lon", None),
        ),
        out_specs=(P("lat", "lon", None), P("lat", "lon", None)),
        check_vma=False,
    )
```

```python
import functools

import jax
import jax.numpy as jnp
from jax import lax
from jax.experimental import pallas as pl
from jax.experimental.pallas import tpu as pltpu
from jax.sharding import PartitionSpec as P

LANES = 128
VMEM_LIMIT = 48 * 1024 * 1024
REACH = 6
FRAME = 2 * REACH


def split3(x):
    high = x.astype(jnp.bfloat16)
    rest = x - high.astype(jnp.float32)
    mid = rest.astype(jnp.bfloat16)
    low = (rest - mid.astype(jnp.float32)).astype(jnp.bfloat16)
    return high, mid, low


def fold_sum(x):
    total = None
    for i in range(x.shape[0] // 8):
        for j in range(x.shape[1] // LANES):
            tile = x[8 * i:8 * i + 8, LANES * j:LANES * j + LANES]
            total = tile if total is None else total + tile
    return total


def copies(pairs, sems):
    started = [pltpu.make_async_copy(src, dst, sems.at[i]) for i, (src, dst) in enumerate(pairs)]
    for copy in started:
        copy.start()
    return started


def lateral_pass(buf, face_lat, face_lon, first, last, left, right):
    cols = slice(left, right)
    width = right - left

    def body(step, carry):
        current, flux_above = carry
        row = first + 2 * step
        for k in range(2):
            below = buf[row + k + 1, cols]
            flux = face_lat[row + k, cols] * (below - current)
            side = face_lon[row + k, cols] * (pltpu.roll(current, width - 1, 0) - current)
            buf[row + k, cols] = current + ((flux - flux_above) + (side - pltpu.roll(side, 1, 0)))
            current, flux_above = below, flux
        return current, flux_above

    start = buf[first, cols]
    flux_start = face_lat[first - 1, cols] * (start - buf[first - 1, cols])
    lax.fori_loop(0, (last - first) // 2, body, (start, flux_start))


def lateral_passes(buf, face_lat, face_lon, nh, begin, end, left, right):
    rows, lost = buf.shape[0], FRAME - 2 * nh

    def body(p, c):
        lateral_pass(buf, face_lat, face_lon, lost + p, rows - lost - p, left, right)
        return c

    lax.fori_loop(begin + 1, end + 1, body, 0)


def last_lateral(buf, face_lat, face_lon, nh, lon_cells):
    close = jnp.minimum(nh, 4)
    lateral_passes(buf, face_lat, face_lon, nh, nh, 2 * nh - close, 0, buf.shape[1])
    left = (FRAME - 4) // 8 * 8
    right = -(-(FRAME + lon_cells + 4) // 8) * 8
    lateral_passes(buf, face_lat, face_lon, nh, 2 * nh - close, 2 * nh, left, right)


def vertical_passes(buf, keep, up, down, first, last, tile, offset, nv, left, right):
    cols = slice(left, right)

    def sweep(p, c):
        def rows(t, c):
            at = [first + t * tile + k for k in range(tile)]
            values = [buf[i, cols] for i in at]
            values = [
                keep[i - offset, cols] * w
                + (up[i - offset, cols] * pltpu.roll(w, LANES - 1, 1)
                   + down[i - offset, cols] * pltpu.roll(w, 1, 1))
                for i, w in zip(at, values)
            ]
            for i, w in zip(at, values):
                buf[i, cols] = w
            return c
        return lax.fori_loop(0, (last - first) // tile, rows, c)

    lax.fori_loop(0, nv, sweep, 0)


def side_rows(reach, lat_cells):
    plan, first = [], 0
    for i in range(lat_cells + 2 * reach):
        outside = max(reach - i, i - (reach + lat_cells - 1), 0)
        plan.append((first, reach - outside))
        first += reach - outside
    return plan, -(-first // 8) * 8


def even(axis):
    return lax.axis_index(axis) % 2 == 0


def place_halos(buf, own, strips, sides, reach, dims):
    lat_cells, lon_cells = dims
    (from_a, skip_a), (from_b, skip_b) = strips
    (from_x, skip_x), (from_s, skip_s) = sides
    base = FRAME - reach
    lat_even, lon_even = even("lat"), even("lon")
    south = FRAME + lat_cells
    row_a = jnp.where(lat_even, south, base)
    row_b = jnp.where(lat_even, base, south)
    cols = slice(FRAME, FRAME + lon_cells)
    for i in range(lat_cells):
        buf[FRAME + i, cols] = own[i * lon_cells:(i + 1) * lon_cells]
    for i in range(reach):
        place = i * lon_cells
        buf[row_a + i, cols] = from_a[skip_a + place:skip_a + place + lon_cells]
        buf[row_b + i, cols] = from_b[skip_b + place:skip_b + place + lon_cells]

    def put_sides(west, skip_west, east, skip_east):
        for i, (first, count) in enumerate(side_rows(reach, lat_cells)[0]):
            if count:
                buf[base + i, FRAME - count:FRAME] = west[skip_west + first:skip_west + first + count]
                buf[base + i, FRAME + lon_cells:FRAME + lon_cells + count] = (
                    east[skip_east + first:skip_east + first + count])

    pl.when(lon_even)(lambda: put_sides(from_s, skip_s, from_x, skip_x))
    pl.when(jnp.logical_not(lon_even))(lambda: put_sides(from_x, skip_x, from_s, skip_s))


def pack_sides(own, strips, outs, reach, dims):
    lat_cells, lon_cells = dims
    (from_a, skip_a), (from_b, skip_b) = strips
    (to_x, skip_x), (to_s, skip_s) = outs
    plan, _ = side_rows(reach, lat_cells)

    def write(north, skip_north, south, skip_south, west, skip_west, east, skip_east):
        for i, (first, count) in enumerate(plan):
            if not count:
                continue
            if i < reach:
                ref, row = north, skip_north + i * lon_cells
            elif i < reach + lat_cells:
                ref, row = own, (i - reach) * lon_cells
            else:
                ref, row = south, skip_south + (i - reach - lat_cells) * lon_cells
            west[skip_west + first:skip_west + first + count] = ref[row:row + count]
            east[skip_east + first:skip_east + first + count] = (
                ref[row + lon_cells - count:row + lon_cells])

    lat_even, lon_even = even("lat"), even("lon")
    for even_lat in (True, False):
        for even_lon in (True, False):
            poles = (from_b, skip_b, from_a, skip_a) if even_lat else (from_a, skip_a, from_b, skip_b)
            edges = (to_s, skip_s, to_x, skip_x) if even_lon else (to_x, skip_x, to_s, skip_s)
            pl.when((lat_even == even_lat) & (lon_even == even_lon))(
                functools.partial(write, *poles, *edges))


def cells_at(rows, slots):
    return jnp.concatenate([rows[0:1], rows[1:2, :slots - LANES]], axis=1).astype(jnp.int32)


def add_into(cells, parts, count):
    hot = lax.broadcasted_iota(jnp.int32, (count, cells.shape[1]), 0) == cells
    both = jnp.dot(hot.astype(jnp.bfloat16), jnp.concatenate(parts, axis=1),
                   preferred_element_type=jnp.float32)
    return both[:, :LANES] + (both[:, LANES:2 * LANES] + both[:, 2 * LANES:])


def scatter_kernel(slots, cells_n, message, cells, own):
    own[...] = add_into(cells[...], split3(message[0:slots]), cells_n)


def sides_kernel(dims, slots, reach, own, from_a, from_b, cells_a, cells_b,
                 strip_a, strip_b, to_x, to_s):
    lat_cells, lon_cells = dims
    skip = (lat_cells - reach) * lon_cells
    for message, cells, strip, north in (
        (from_a, cells_a, strip_a, jnp.logical_not(even("lat"))),
        (from_b, cells_b, strip_b, even("lat")),
    ):
        at = cells_at(cells, slots) - jnp.where(north, skip, 0)
        strip[...] = add_into(at, split3(message[0:slots]), reach * lon_cells)
    pack_sides(own, ((strip_a, 0), (strip_b, 0)), ((to_x, 0), (to_s, 0)), reach, dims)


def face_sides_kernel(dims, root_h, root_v, from_a, from_b, to_x, to_s):
    skip = FRAME * dims[1]
    rows = side_rows(FRAME, dims[0])[1]
    pack_sides(root_h, ((from_a, 0), (from_b, 0)), ((to_x, 0), (to_s, 0)), FRAME, dims)
    pack_sides(root_v, ((from_a, skip), (from_b, skip)), ((to_x, rows), (to_s, rows)), REACH, dims)


def start_kernel(dims, *refs):
    lat_cells, lon_cells = dims
    sources, (first, root_h, root_v, to_a, to_b), refs = refs[:5], refs[5:10], refs[10:]
    (innovation, obs_weight, block_list, kappa_h, kappa_v), sems = refs[:5], refs[5]
    loads = copies(list(zip(sources, refs[:5])), sems)
    obs, own = innovation.shape
    slots = block_list.shape[1]
    for load in loads:
        load.wait()
    weight = obs_weight[...]
    first[0:obs, 0:own] = weight * innovation[...]
    first[0:obs, own:2 * own] = weight
    places = block_list[...].astype(jnp.float32)
    tail = to_a.shape[0] - 8
    cells = jnp.clip(places[1:2], 0.0, lat_cells * lon_cells - 1.0)
    for ref, base, row in ((first, obs, places[0:1]), (to_a, tail, cells), (to_b, tail, cells)):
        ref[base:base + 8] = jnp.full((8, LANES), -1.0, jnp.float32)
        ref[base:base + 1] = row[:, :LANES]
        ref[base + 1:base + 2, 0:slots - LANES] = row[:, LANES:]
    root_h[...] = jnp.sqrt(kappa_h[...])
    root_v[...] = jnp.sqrt(kappa_v[...])

    def write(south, north):
        skip = 0
        for ref, reach in ((root_h, FRAME), (root_v, REACH)):
            count = reach * lon_cells
            north[skip:skip + count] = ref[0:count]
            south[skip:skip + count] = ref[lat_cells * lon_cells - count:]
            skip += count

    pl.when(even("lat"))(lambda: write(to_a, to_b))
    pl.when(jnp.logical_not(even("lat")))(lambda: write(to_b, to_a))


def faces_kernel(dims, root_h, root_v, from_a, from_b, from_x, from_s, *refs):
    lat_cells, lon_cells = dims
    out, (face_lat, face_lon, keep, up, down, buf, sems) = refs[:5], refs[5:]
    rows = lat_cells + 2 * FRAME
    width = buf.shape[1]
    place_halos(
        buf, root_h, ((from_a, 0), (from_b, 0)), ((from_x, 0), (from_s, 0)), FRAME, dims
    )

    def clear(first):
        def body(i, c):
            buf[first + i] = jnp.zeros((width, LANES), jnp.float32)
            return c
        lax.fori_loop(0, FRAME, body, 0)

    lat = lax.axis_index("lat")
    pl.when(lat == 0)(lambda: clear(0))
    pl.when(lat == lax.axis_size("lat") - 1)(lambda: clear(FRAME + lat_cells))

    buf[rows] = jnp.zeros((width, LANES), jnp.float32)

    def lateral(step, c):
        for k in range(4):
            i = 4 * step + k
            here = buf[i]
            face_lat[i] = here * buf[i + 1]
            face_lon[i] = here * pltpu.roll(here, width - 1, 0)
        return c

    lax.fori_loop(0, rows // 4, lateral, 0)
    side = copies([(face_lat, out[0]), (face_lon, out[1])], sems)
    skip, skip_side = FRAME * lon_cells, side_rows(FRAME, lat_cells)[1]
    place_halos(
        buf, root_v, ((from_a, skip), (from_b, skip)),
        ((from_x, skip_side), (from_s, skip_side)), REACH, dims,
    )
    top = lax.broadcasted_iota(jnp.int32, (width, LANES), 1) == LANES - 1

    def vertical(step, c):
        at = [4 * step + k for k in range(4)]
        here = [buf[FRAME - REACH + i] for i in at]
        face = [jnp.where(top, 0.0, v * pltpu.roll(v, LANES - 1, 1)) for v in here]
        below = [pltpu.roll(v, 1, 1) for v in face]
        for i, f, g in zip(at, face, below):
            up[i] = f
            down[i] = g
            keep[i] = 1.0 - (f + g)
        return c

    lax.fori_loop(0, (lat_cells + 2 * REACH) // 4, vertical, 0)
    level = copies([(keep, out[2]), (up, out[3]), (down, out[4])], sems.at[pl.ds(2, 3)])
    for copy in side + level:
        copy.wait()


def observe(cells, jac, field, out):
    slots, obs, _ = jac.shape
    lane = lax.broadcasted_iota(jnp.int32, (obs, LANES), 1)

    ones = jnp.ones((2 * LANES, LANES), jnp.bfloat16)
    group = 16

    def part(first, count):
        def body(step, acc):
            at = [first + step * group + k for k in range(group)]
            prods = [jac[slot] * field[pl.ds(cells[slot], 1), :] for slot in at]
            half = jnp.concatenate(prods[:group // 2], axis=0)
            high = half.astype(jnp.bfloat16)
            low = (half - high.astype(jnp.float32)).astype(jnp.bfloat16)
            sums = jnp.dot(jnp.concatenate([high, low], axis=1), ones, preferred_element_type=jnp.float32)
            for k in range(group):
                if k < group // 2:
                    value = sums[obs * k:obs * k + obs]
                else:
                    value = jnp.sum(prods[k], axis=1, keepdims=True)
                acc = jnp.where(lane == step * group + k, value, acc)
            return acc
        return lax.fori_loop(0, count // group, body, jnp.zeros((obs, LANES), jnp.float32))

    out[0:obs] = part(0, LANES)
    rest = part(LANES, slots - LANES)
    out[obs:obs + obs // 2] = rest[:obs // 2] + pltpu.roll(rest[obs // 2:], LANES // 2, 1)


def adjoint_kernel(first_call, parts, *refs):
    pieces, refs = refs[:2 * parts], refs[2 * parts:]
    if first_call:
        own_hot, jac_hbm, out, weight, band, jac, taken, sems = refs
    else:
        row_hot, weight, own_hot, jac_hbm, out, jac, taken, sems = refs
    slots, obs, _ = jac.shape
    group = 32
    groups = slots // group

    def chunk(g):
        place = pl.ds(g * group, group)
        return pltpu.make_async_copy(jac_hbm.at[place], jac.at[place], sems.at[g])

    for g in range(groups):
        chunk(g).start()
    if first_call:
        own = weight.shape[1] // (2 * parts)
        for d, piece in enumerate(pieces):
            band[:, d * own:d * own + own] = piece[0:obs, 0:own]
            weight[:, d * own:d * own + own] = piece[0:obs, own:2 * own]
        weighted = band[...]
    else:
        total = None
        scal = None
        for d, piece in enumerate(pieces):
            fold = piece[obs:obs + obs // 2]
            rest = jnp.concatenate([fold, pltpu.roll(fold, LANES // 2, 1)], axis=0)
            values = jnp.concatenate([piece[0:obs], rest], axis=1)
            stack = jnp.concatenate(split3(values), axis=0)
            prod = jnp.dot(stack, row_hot[d], preferred_element_type=jnp.float32)
            total = prod if total is None else total + prod
            tail = piece[obs + obs // 2:obs + obs // 2 + 8]
            scal = tail if scal is None else scal + tail
        total = total[:obs] + (total[obs:2 * obs] + total[2 * obs:])
        weighted = weight[...] * total
        out[slots:slots + 8] = scal
        out[slots + 8:slots + 16] = fold_sum(weighted * total)
    stack = jnp.concatenate(split3(weighted), axis=0)
    picked = jnp.dot(stack, own_hot[...], preferred_element_type=jnp.float32)
    picked = picked[:obs] + (picked[obs:2 * obs] + picked[2 * obs:])
    taken[0] = picked[:, :LANES]
    taken[1] = picked[:, LANES:]

    ones = jnp.ones((2 * LANES, LANES), jnp.bfloat16)
    lane = lax.broadcasted_iota(jnp.int32, (obs, LANES), 1)

    def body(g, c):
        chunk(g).wait()
        per = LANES // group
        base = (g % per) * group
        values = taken[g // per]
        high = values.astype(jnp.bfloat16)
        low = (values - high.astype(jnp.float32)).astype(jnp.bfloat16)
        none = jnp.zeros_like(high)
        stack = jnp.concatenate([
            jnp.concatenate([jnp.where(lane == base + k, high, none),
                             jnp.where(lane == base + k, low, none)], axis=1)
            for k in range(group // 2)
        ], axis=0)
        spread = jnp.dot(stack, ones, preferred_element_type=jnp.float32)
        values = pltpu.roll(values, LANES - base, 1)
        for k in range(group):
            slot = g * group + k
            wide = spread[obs * k:obs * k + obs] if k < group // 2 else values[:, k:k + 1]
            out[pl.ds(slot, 1), :] = jnp.sum(jac[slot] * wide, axis=0, keepdims=True)
        return c

    lax.fori_loop(0, groups, body, 0)


def spread_kernel(dims, first_call, *refs):
    lat_cells, lon_cells = dims
    counts, cells, own, from_a, from_b, from_x, from_s = refs[:7]
    refs = refs[7:]
    if not first_call:
        scal, refs = refs[0], refs[1:]
    faces_hbm, jac_hbm, refs = refs[:5], refs[5], refs[6:]
    if not first_call:
        grad_hbm, spread_hbm, refs = refs[0], refs[1], refs[2:]
    one_hbm, two_hbm, message = refs[:3]
    refs = refs[3:]
    face_lat, face_lon, keep, up, down, jac, one, two, grad, buf, mid, sems = refs
    loads = copies(
        list(zip(faces_hbm, (face_lat, face_lon, keep, up, down))) + [(jac_hbm, jac)], sems
    )
    if not first_call:
        old_loads = copies([(grad_hbm, grad), (spread_hbm, two)], sems.at[pl.ds(6, 2)])
    nh, nv = counts[0], counts[1]
    rows = lat_cells + 2 * FRAME
    width = buf.shape[1]
    place_halos(
        buf, own, ((from_a, 0), (from_b, 0)), ((from_x, 0), (from_s, 0)), FRAME, dims
    )
    for load in loads[:2]:
        load.wait()
    lateral_passes(buf, face_lat, face_lon, nh, 0, nh, 0, width)
    border = FRAME - REACH
    tall = lat_cells + 2 * REACH
    vertical = functools.partial(
        vertical_passes, buf, keep, up, down, border, border + tall, tall // 2, border, nv, 0, width
    )
    for load in loads[2:5]:
        load.wait()
    vertical()

    def save(i, c):
        mid[i] = buf[FRAME + i]
        return c

    lax.fori_loop(0, lat_cells, save, 0)
    vertical()
    last_lateral(buf, face_lat, face_lon, nh, lon_cells)
    cols = slice(FRAME, FRAME + lon_cells)
    if not first_call:
        rr = jnp.sum(scal[0:8])
        alpha = rr / (rr + jnp.sum(scal[8:16]))
        for load in old_loads:
            load.wait()

    def finish(i, acc):
        place = pl.ds(pl.multiple_of(i * lon_cells, lon_cells), lon_cells)
        vector = mid[i, cols]
        after = buf[FRAME + i, cols]
        if first_call:
            one[place] = vector
            two[place] = after
        else:
            old = two[place]
            base = grad[place]
            applied = base + vector
            one[place] = applied
            two[place] = old - alpha * (old + after)
            vector = base - alpha * applied
        square = vector * vector
        for j in range(lon_cells // 8):
            acc = acc + square[8 * j:8 * j + 8]
        return acc

    norm = lax.fori_loop(0, lat_cells, finish, jnp.zeros((8, LANES), jnp.float32))
    stores = copies([(one, one_hbm), (two, two_hbm)], sems.at[pl.ds(8, 2)])
    loads[5].wait()
    obs = jac.shape[1]
    observe(cells, jac, two, message)
    message[obs + obs // 2:] = norm
    for store in stores:
        store.wait()


def final_kernel(dims, *refs):
    lat_cells, lon_cells = dims
    counts, own, from_a, from_b, from_x, from_s, scal0, scal1 = refs[:8]
    hbm, (increment, residual), refs = refs[8:17], refs[17:19], refs[19:]
    face_lat, face_lon, keep, up, down, grad, spread, image, spread_next, buf, sems = refs
    inner = pl.ds(FRAME - REACH, lat_cells + 2 * REACH)
    block = pl.ds(REACH, lat_cells)
    loads = copies(
        [(src.at[inner], dst.at[inner]) for src, dst in zip(hbm[:2], refs[:2])]
        + [(src.at[block], dst.at[block]) for src, dst in zip(hbm[2:5], refs[2:5])]
        + list(zip(hbm[5:], refs[5:9])), sems)
    nh, nv = counts[0], counts[1]
    place_halos(
        buf, own, ((from_a, 0), (from_b, 0)), ((from_x, 0), (from_s, 0)), REACH, dims
    )
    for load in loads[:2]:
        load.wait()
    last_lateral(buf, face_lat, face_lon, nh, lon_cells)
    left = FRAME // 8 * 8
    right = -(-(FRAME + lon_cells) // 8) * 8
    for load in loads[2:5]:
        load.wait()
    vertical_passes(
        buf, keep, up, down, FRAME, FRAME + lat_cells, lat_cells, FRAME - REACH, nv, left, right
    )
    rr0 = jnp.sum(scal0[0:8])
    alpha0 = rr0 / (rr0 + jnp.sum(scal0[8:16]))
    rr1 = jnp.sum(scal1[0:8])
    beta = rr1 / rr0
    alpha1 = rr1 / ((rr1 + jnp.sum(scal1[8:16])) - beta * (rr1 / alpha0))
    cols = slice(FRAME, FRAME + lon_cells)
    for load in loads[5:]:
        load.wait()

    def finish(i, c):
        place = pl.ds(pl.multiple_of(i * lon_cells, lon_cells), lon_cells)
        applied = image[place]
        rest = grad[place] - alpha0 * applied
        residual[place] = rest - alpha1 * ((rest + buf[FRAME + i, cols]) + beta * applied)
        old = spread[place]
        increment[place] = alpha0 * old + alpha1 * (spread_next[place] + beta * old)
        return c

    lax.fori_loop(0, lat_cells, finish, 0)


def local(innovation, obs_weight, jacobian, block_list, pass_counts, kappa_h, kappa_v):
    lat_cells, lon_cells, levels = kappa_h.shape
    cells_n = lat_cells * lon_cells
    slots, obs, _ = jacobian.shape
    own_rows = innovation.shape[1]
    n_lat, n_lon = lax.axis_size("lat"), lax.axis_size("lon")
    parts = n_lon // 2
    lon = lax.axis_index("lon")
    f32 = jnp.float32

    def swap(n, k):
        return [(i, i ^ k) for i in range(n)]

    def odd_pairs(n):
        return [(i, (i + 1) % n if i % 2 else (i - 1) % n) for i in range(n)]

    def send(x, axis, pairs):
        return lax.ppermute(x, axis, pairs)

    def gather_band(x):
        near = [x] + [send(x, "lon", swap(n_lon, 2 * k)) for k in range(1, parts)]
        return near + [send(piece, "lon", swap(n_lon, 1)) for piece in near]

    def lon_send(to_x, to_s):
        return send(to_x, "lon", swap(n_lon, 1)), send(to_s, "lon", odd_pairs(n_lon))

    def lat_send(to_a, to_b):
        return send(to_a, "lat", swap(n_lat, 1)), send(to_b, "lat", odd_pairs(n_lat))

    def lat_sum(message, from_a, from_b):
        tail = message[slots:]
        if n_lat != 4:
            return lax.psum(tail, "lat")
        return (tail + send(tail, "lat", swap(n_lat, 2))) + (from_a[slots:] + from_b[slots:])

    def scatter(message):
        return call(functools.partial(scatter_kernel, slots, cells_n), "scatter", field, (message, cells))

    def sides_of(own, from_a, from_b, reach):
        side = shape(side_rows(reach, lat_cells)[1], levels)
        strip = shape(reach * lon_cells, levels)
        strip_a, strip_b, to_x, to_s = call(
            functools.partial(sides_kernel, dims, slots, reach), "sides", (strip, strip, side, side),
            (own, from_a, from_b, *cells_near))
        return (strip_a, strip_b), (to_x, to_s)

    def halo(message, reach):
        from_a, from_b = lat_send(message, message)
        own = scatter(message)
        strips, sides = sides_of(own, from_a, from_b, reach)
        return (own, *strips, *lon_send(*sides)), lat_sum(message, from_a, from_b)

    vmem = pl.BlockSpec(memory_space=pltpu.VMEM)
    smem = pl.BlockSpec(memory_space=pltpu.SMEM)
    hbm = pl.BlockSpec(memory_space=pl.ANY)
    params = pltpu.CompilerParams(vmem_limit_bytes=VMEM_LIMIT)
    shape = lambda *dims: jax.ShapeDtypeStruct(dims, f32)
    scratch = lambda *dims: pltpu.VMEM(dims, f32)
    rows_h = lat_cells + 2 * FRAME
    rows_v = lat_cells + 2 * REACH
    width = lon_cells + 2 * FRAME
    band_rows = n_lon * own_rows
    dims = (lat_cells, lon_cells)
    field = shape(cells_n, levels)
    msg = shape(obs + obs // 2 + 8, LANES)
    wide, tall = shape(rows_h, width, levels), shape(rows_v, width, levels)
    wide_vmem, tall_vmem = scratch(rows_h, width, levels), scratch(rows_v, width, levels)
    field_vmem = scratch(cells_n, levels)
    jac_vmem = scratch(slots, obs, levels)
    faces_vmem = [wide_vmem] * 2 + [tall_vmem] * 3
    sems = lambda count: pltpu.SemaphoreType.DMA((count,))

    def call(kernel, name, outs, ins, scalars=0, far_in=(), far_out=False, scratches=()):
        out_specs = jax.tree.map(lambda _: vmem, outs)
        if far_out:
            out_specs = (hbm,) * far_out + out_specs[far_out:]
        specs = [smem] * scalars + [vmem] * (len(ins) - scalars) + [hbm] * len(far_in)
        return pl.pallas_call(
            kernel, out_shape=outs, in_specs=specs, out_specs=out_specs,
            scratch_shapes=list(scratches), compiler_params=params, name=name,
        )(*ins, *far_in)

    strip = shape((FRAME + REACH) * lon_cells + 8, levels)
    start_in = (innovation, obs_weight, block_list,
                kappa_h.reshape(cells_n, levels), kappa_v.reshape(cells_n, levels))
    first, root_h, root_v, to_a, to_b = call(
        functools.partial(start_kernel, dims), "start", (shape(obs + 8, LANES), field, field, strip, strip),
        (), far_in=start_in, scratches=[pltpu.VMEM(v.shape, v.dtype) for v in start_in] + [sems(5)])
    k_strips = lat_send(to_a, to_b)
    band = gather_band(first)
    cells_near = [v[(FRAME + REACH) * lon_cells:] for v in k_strips]

    def place_of(row):
        row = row.astype(jnp.int32)
        key = (row // own_rows) ^ lon
        at = (key // 2 + parts * (key % 2)) * own_rows + row % own_rows
        return jnp.where((row >= 0) & (row < band_rows), at, -1)

    all_at = place_of(jnp.stack([piece[obs:obs + 2] for piece in band]).reshape(n_lon, 2 * LANES))
    row_iota = jnp.arange(band_rows, dtype=jnp.int32)
    row_hot = (all_at[:, :, None] == row_iota[None, None, :]).astype(jnp.bfloat16)
    own_at = jnp.pad(place_of(block_list[0]), (0, 2 * LANES - slots), constant_values=-1)
    own_hot = (row_iota[:, None] == own_at[None, :]).astype(jnp.bfloat16)
    cells = jnp.clip(block_list[1:], 0, cells_n - 1)
    cells_flat = cells.reshape(slots)

    adj_scratch = [jac_vmem, scratch(2, obs, LANES), sems(slots // 32)]
    message, weight = call(
        functools.partial(adjoint_kernel, True, parts), "adjoint_first",
        (shape(slots, levels), shape(obs, band_rows)), (*band, own_hot), far_in=(jacobian,),
        scratches=[scratch(obs, band_rows)] + adj_scratch)

    from_a, from_b = lat_send(message, message)
    own = scatter(message)
    side = shape(sum(side_rows(reach, lat_cells)[1] for reach in (FRAME, REACH)), levels)
    k_messages = call(functools.partial(face_sides_kernel, dims), "face_sides", (side, side),
                      (root_h, root_v, *k_strips))
    k_sides = lon_send(*k_messages)
    k_messages, from_a, from_b = lax.optimization_barrier((k_messages, from_a, from_b))
    strips, sides = sides_of(own, from_a, from_b, FRAME)
    halos = (own, *strips, *lon_send(*sides))
    faces = call(
        functools.partial(faces_kernel, dims), "faces", (wide, wide, tall, tall, tall),
        (root_h, root_v, *k_strips, *k_sides), far_out=5,
        scratches=faces_vmem + [scratch(rows_h + 1, width, levels), sems(5)])
    spread_scratch = faces_vmem + [jac_vmem] + [field_vmem] * 3 + [
        wide_vmem, scratch(lat_cells, width, levels), sems(10)]
    grad, spread, message = call(
        functools.partial(spread_kernel, dims, True), "spread_first", (field, field, msg),
        (pass_counts, cells_flat, *halos), 2, (*faces, jacobian), 2, spread_scratch)

    def adjoint(message):
        return call(
            functools.partial(adjoint_kernel, False, parts), "adjoint_next",
            shape(slots + 16, levels), (*gather_band(message), row_hot, weight, own_hot),
            far_in=(jacobian,), scratches=adj_scratch)

    halos, scal0 = halo(adjoint(message), FRAME)
    image, spread_next, message = call(
        functools.partial(spread_kernel, dims, False), "spread_next", (field, field, msg),
        (pass_counts, cells_flat, *halos, scal0), 2, (*faces, jacobian, grad, spread), 2, spread_scratch)
    halos, scal1 = halo(adjoint(message), REACH)
    increment, residual = call(
        functools.partial(final_kernel, dims), "final", (field, field),
        (pass_counts, *halos, scal0, scal1), 1,
        (*faces, grad, spread, image, spread_next), 0,
        faces_vmem + [field_vmem] * 4 + [wide_vmem, sems(9)])
    block = (lat_cells, lon_cells, levels)
    return increment.reshape(block), residual.reshape(block)


def solution(mesh):
    return jax.shard_map(
        local,
        mesh=mesh,
        in_specs=(
            P(None, ("lat", "lon")),
            P(None, ("lat", "lon")),
            P(("lat", "lon"), None, None),
            P(None, ("lat", "lon")),
            P(),
            P("lat", "lon", None),
            P("lat", "lon", None),
        ),
        out_specs=(P("lat", "lon", None), P("lat", "lon", None)),
        check_vma=False,
    )
```

```python
import functools

import jax
import jax.numpy as jnp
from jax import lax
from jax.experimental import pallas as pl
from jax.experimental.pallas import tpu as pltpu
from jax.sharding import PartitionSpec as P

LANES = 128
VMEM_LIMIT = 48 * 1024 * 1024
START_LIMIT = 60 * 1024 * 1024
REACH = 6
FRAME = 2 * REACH


def split3(x):
    high = x.astype(jnp.bfloat16)
    rest = x - high.astype(jnp.float32)
    mid = rest.astype(jnp.bfloat16)
    low = (rest - mid.astype(jnp.float32)).astype(jnp.bfloat16)
    return high, mid, low


def fold_sum(x):
    total = None
    for i in range(x.shape[0] // 8):
        for j in range(x.shape[1] // LANES):
            tile = x[8 * i:8 * i + 8, LANES * j:LANES * j + LANES]
            total = tile if total is None else total + tile
    return total


def copies(pairs, sems):
    started = [pltpu.make_async_copy(src, dst, sems.at[i]) for i, (src, dst) in enumerate(pairs)]
    for copy in started:
        copy.start()
    return started


def lateral_pass(buf, face_lat, face_lon, first, last, left, right):
    cols = slice(left, right)
    width = right - left

    def body(step, carry):
        current, flux_above = carry
        row = first + 2 * step
        for k in range(2):
            below = buf[row + k + 1, cols]
            flux = face_lat[row + k, cols] * (below - current)
            side = face_lon[row + k, cols] * (pltpu.roll(current, width - 1, 0) - current)
            buf[row + k, cols] = current + ((flux - flux_above) + (side - pltpu.roll(side, 1, 0)))
            current, flux_above = below, flux
        return current, flux_above

    start = buf[first, cols]
    flux_start = face_lat[first - 1, cols] * (start - buf[first - 1, cols])
    lax.fori_loop(0, (last - first) // 2, body, (start, flux_start))


def lateral_passes(buf, face_lat, face_lon, nh, begin, end, left, right):
    rows, lost = buf.shape[0], FRAME - 2 * nh

    def body(p, c):
        lateral_pass(buf, face_lat, face_lon, lost + p, rows - lost - p, left, right)
        return c

    lax.fori_loop(begin + 1, end + 1, body, 0)


def last_lateral(buf, face_lat, face_lon, nh, lon_cells):
    close = jnp.minimum(nh, 4)
    lateral_passes(buf, face_lat, face_lon, nh, nh, 2 * nh - close, 0, buf.shape[1])
    left = (FRAME - 4) // 8 * 8
    right = -(-(FRAME + lon_cells + 4) // 8) * 8
    lateral_passes(buf, face_lat, face_lon, nh, 2 * nh - close, 2 * nh, left, right)


def shift_matrix():
    source = lax.broadcasted_iota(jnp.int32, (2 * LANES, 2 * LANES), 0) % LANES
    target = lax.broadcasted_iota(jnp.int32, (2 * LANES, 2 * LANES), 1)
    wanted = jnp.where(target < LANES, target + 1, target - LANES - 1)
    return (source == wanted).astype(jnp.bfloat16)


def vertical_passes(buf, keep, up, down, first, last, offset, nv, left, right):
    cols = slice(left, right)
    width = right - left
    shifts = shift_matrix()
    at = list(range(first, last))
    half = (last - first) // 2

    def sweep(p, c):
        values = [buf[i, cols] for i in at]
        stack = jnp.concatenate(values[:half], axis=0)
        high = stack.astype(jnp.bfloat16)
        low = (stack - high.astype(jnp.float32)).astype(jnp.bfloat16)
        moved = jnp.dot(jnp.concatenate([high, low], axis=1), shifts, preferred_element_type=jnp.float32)
        for n, (i, w) in enumerate(zip(at, values)):
            if n < half:
                here = moved[width * n:width * n + width]
                above, below = here[:, :LANES], here[:, LANES:]
            else:
                above, below = pltpu.roll(w, LANES - 1, 1), pltpu.roll(w, 1, 1)
            buf[i, cols] = keep[i - offset, cols] * w + (
                up[i - offset, cols] * above + down[i - offset, cols] * below)
        return c

    lax.fori_loop(0, nv, sweep, 0)


def side_rows(reach, lat_cells):
    plan, first = [], 0
    for i in range(lat_cells + 2 * reach):
        outside = max(reach - i, i - (reach + lat_cells - 1), 0)
        plan.append((first, reach - outside))
        first += reach - outside
    return plan, -(-first // 8) * 8


def even(axis):
    return lax.axis_index(axis) % 2 == 0


def place_halos(buf, own, strips, sides, reach, dims):
    lat_cells, lon_cells = dims
    (from_a, skip_a), (from_b, skip_b) = strips
    (from_x, skip_x), (from_s, skip_s) = sides
    base = FRAME - reach
    lat_even, lon_even = even("lat"), even("lon")
    south = FRAME + lat_cells
    row_a = jnp.where(lat_even, south, base)
    row_b = jnp.where(lat_even, base, south)
    cols = slice(FRAME, FRAME + lon_cells)
    for i in range(lat_cells):
        buf[FRAME + i, cols] = own[i * lon_cells:(i + 1) * lon_cells]
    for i in range(reach):
        place = i * lon_cells
        buf[row_a + i, cols] = from_a[skip_a + place:skip_a + place + lon_cells]
        buf[row_b + i, cols] = from_b[skip_b + place:skip_b + place + lon_cells]

    def put_sides(west, skip_west, east, skip_east):
        for i, (first, count) in enumerate(side_rows(reach, lat_cells)[0]):
            if count:
                buf[base + i, FRAME - count:FRAME] = west[skip_west + first:skip_west + first + count]
                buf[base + i, FRAME + lon_cells:FRAME + lon_cells + count] = (
                    east[skip_east + first:skip_east + first + count])

    pl.when(lon_even)(lambda: put_sides(from_s, skip_s, from_x, skip_x))
    pl.when(jnp.logical_not(lon_even))(lambda: put_sides(from_x, skip_x, from_s, skip_s))


def pack_sides(own, strips, outs, reach, dims):
    lat_cells, lon_cells = dims
    (from_a, skip_a), (from_b, skip_b) = strips
    (to_x, skip_x), (to_s, skip_s) = outs
    plan, _ = side_rows(reach, lat_cells)

    def write(north, skip_north, south, skip_south, west, skip_west, east, skip_east):
        for i, (first, count) in enumerate(plan):
            if not count:
                continue
            if i < reach:
                ref, row = north, skip_north + i * lon_cells
            elif i < reach + lat_cells:
                ref, row = own, (i - reach) * lon_cells
            else:
                ref, row = south, skip_south + (i - reach - lat_cells) * lon_cells
            west[skip_west + first:skip_west + first + count] = ref[row:row + count]
            east[skip_east + first:skip_east + first + count] = (
                ref[row + lon_cells - count:row + lon_cells])

    lat_even, lon_even = even("lat"), even("lon")
    for even_lat in (True, False):
        for even_lon in (True, False):
            poles = (from_b, skip_b, from_a, skip_a) if even_lat else (from_a, skip_a, from_b, skip_b)
            edges = (to_s, skip_s, to_x, skip_x) if even_lon else (to_x, skip_x, to_s, skip_s)
            pl.when((lat_even == even_lat) & (lon_even == even_lon))(
                functools.partial(write, *poles, *edges))


def cells_at(rows, slots):
    return jnp.concatenate([rows[0:1], rows[1:2, :slots - LANES]], axis=1).astype(jnp.int32)


def add_into(cells, parts, count):
    hot = lax.broadcasted_iota(jnp.int32, (count, cells.shape[1]), 0) == cells
    both = jnp.dot(hot.astype(jnp.bfloat16), jnp.concatenate(parts, axis=1),
                   preferred_element_type=jnp.float32)
    return both[:, :LANES] + (both[:, LANES:2 * LANES] + both[:, 2 * LANES:])


def scatter_kernel(slots, cells_n, message, cells, own):
    own[...] = add_into(cells[...], split3(message[0:slots]), cells_n)


def sides_kernel(dims, slots, reach, own, from_a, from_b, cells_a, cells_b,
                 strip_a, strip_b, to_x, to_s):
    lat_cells, lon_cells = dims
    skip = (lat_cells - reach) * lon_cells
    for message, cells, strip, north in (
        (from_a, cells_a, strip_a, jnp.logical_not(even("lat"))),
        (from_b, cells_b, strip_b, even("lat")),
    ):
        at = cells_at(cells, slots) - jnp.where(north, skip, 0)
        strip[...] = add_into(at, split3(message[0:slots]), reach * lon_cells)
    pack_sides(own, ((strip_a, 0), (strip_b, 0)), ((to_x, 0), (to_s, 0)), reach, dims)


def face_sides_kernel(dims, root_h, root_v, from_a, from_b, to_x, to_s):
    skip = FRAME * dims[1]
    rows = side_rows(FRAME, dims[0])[1]
    pack_sides(root_h, ((from_a, 0), (from_b, 0)), ((to_x, 0), (to_s, 0)), FRAME, dims)
    pack_sides(root_v, ((from_a, skip), (from_b, skip)), ((to_x, rows), (to_s, rows)), REACH, dims)


def start_kernel(dims, *refs):
    lat_cells, lon_cells = dims
    sources, (first, root_h, root_v, to_a, to_b), refs = refs[:5], refs[5:10], refs[10:]
    (innovation, obs_weight, block_list, kappa_h, kappa_v), sems = refs[:5], refs[5]
    loads = copies(list(zip(sources, refs[:5])), sems)
    obs, own = innovation.shape
    slots = block_list.shape[1]
    for load in loads:
        load.wait()
    weight = obs_weight[...]
    first[0:obs, 0:own] = weight * innovation[...]
    first[0:obs, own:2 * own] = weight
    places = block_list[...].astype(jnp.float32)
    tail = to_a.shape[0] - 8
    cells = jnp.clip(places[1:2], 0.0, lat_cells * lon_cells - 1.0)
    for ref, base, row in ((first, obs, places[0:1]), (to_a, tail, cells), (to_b, tail, cells)):
        ref[base:base + 8] = jnp.full((8, LANES), -1.0, jnp.float32)
        ref[base:base + 1] = row[:, :LANES]
        ref[base + 1:base + 2, 0:slots - LANES] = row[:, LANES:]
    root_h[...] = jnp.sqrt(kappa_h[...])
    root_v[...] = jnp.sqrt(kappa_v[...])

    def write(south, north):
        skip = 0
        for ref, reach in ((root_h, FRAME), (root_v, REACH)):
            count = reach * lon_cells
            north[skip:skip + count] = ref[0:count]
            south[skip:skip + count] = ref[lat_cells * lon_cells - count:]
            skip += count

    pl.when(even("lat"))(lambda: write(to_a, to_b))
    pl.when(jnp.logical_not(even("lat")))(lambda: write(to_b, to_a))


def faces_kernel(dims, root_h, root_v, from_a, from_b, from_x, from_s, *refs):
    lat_cells, lon_cells = dims
    out, (face_lat, face_lon, keep, up, down, buf, sems) = refs[:5], refs[5:]
    rows = lat_cells + 2 * FRAME
    width = buf.shape[1]
    place_halos(
        buf, root_h, ((from_a, 0), (from_b, 0)), ((from_x, 0), (from_s, 0)), FRAME, dims
    )

    def clear(first):
        def body(i, c):
            buf[first + i] = jnp.zeros((width, LANES), jnp.float32)
            return c
        lax.fori_loop(0, FRAME, body, 0)

    lat = lax.axis_index("lat")
    pl.when(lat == 0)(lambda: clear(0))
    pl.when(lat == lax.axis_size("lat") - 1)(lambda: clear(FRAME + lat_cells))

    buf[rows] = jnp.zeros((width, LANES), jnp.float32)

    def lateral(step, c):
        for k in range(4):
            i = 4 * step + k
            here = buf[i]
            face_lat[i] = here * buf[i + 1]
            face_lon[i] = here * pltpu.roll(here, width - 1, 0)
        return c

    lax.fori_loop(0, rows // 4, lateral, 0)
    side = copies([(face_lat, out[0]), (face_lon, out[1])], sems)
    skip, skip_side = FRAME * lon_cells, side_rows(FRAME, lat_cells)[1]
    place_halos(
        buf, root_v, ((from_a, skip), (from_b, skip)),
        ((from_x, skip_side), (from_s, skip_side)), REACH, dims,
    )
    top = lax.broadcasted_iota(jnp.int32, (width, LANES), 1) == LANES - 1

    def vertical(step, c):
        at = [4 * step + k for k in range(4)]
        here = [buf[FRAME - REACH + i] for i in at]
        face = [jnp.where(top, 0.0, v * pltpu.roll(v, LANES - 1, 1)) for v in here]
        below = [pltpu.roll(v, 1, 1) for v in face]
        for i, f, g in zip(at, face, below):
            up[i] = f
            down[i] = g
            keep[i] = 1.0 - (f + g)
        return c

    lax.fori_loop(0, (lat_cells + 2 * REACH) // 4, vertical, 0)
    level = copies([(keep, out[2]), (up, out[3]), (down, out[4])], sems.at[pl.ds(2, 3)])
    for copy in side + level:
        copy.wait()


def observe(cells, jac, field, out):
    slots, obs, _ = jac.shape
    lane = lax.broadcasted_iota(jnp.int32, (obs, LANES), 1)

    ones = jnp.ones((2 * LANES, LANES), jnp.bfloat16)
    group = 64

    def part(first, count):
        def body(step, acc):
            at = [first + step * group + k for k in range(group)]
            prods = [jac[slot] * field[pl.ds(cells[slot], 1), :] for slot in at]
            half = jnp.concatenate(prods[:group // 2], axis=0)
            high = half.astype(jnp.bfloat16)
            low = (half - high.astype(jnp.float32)).astype(jnp.bfloat16)
            sums = jnp.dot(jnp.concatenate([high, low], axis=1), ones, preferred_element_type=jnp.float32)
            for k in range(group):
                if k < group // 2:
                    value = sums[obs * k:obs * k + obs]
                else:
                    value = jnp.sum(prods[k], axis=1, keepdims=True)
                acc = jnp.where(lane == step * group + k, value, acc)
            return acc
        return lax.fori_loop(0, count // group, body, jnp.zeros((obs, LANES), jnp.float32))

    out[0:obs] = part(0, LANES)
    rest = part(LANES, slots - LANES)
    out[obs:obs + obs // 2] = rest[:obs // 2] + pltpu.roll(rest[obs // 2:], LANES // 2, 1)


def adjoint_kernel(first_call, parts, *refs):
    pieces, refs = refs[:2 * parts], refs[2 * parts:]
    if first_call:
        own_hot, jac_hbm, out, weight, band, jac, taken, sems = refs
    else:
        row_hot, weight, own_hot, jac_hbm, out, jac, taken, sems = refs
    slots, obs, _ = jac.shape
    group = 64
    groups = slots // group

    def chunk(g):
        place = pl.ds(g * group, group)
        return pltpu.make_async_copy(jac_hbm.at[place], jac.at[place], sems.at[g])

    for g in range(groups):
        chunk(g).start()
    if first_call:
        own = weight.shape[1] // (2 * parts)
        for d, piece in enumerate(pieces):
            band[:, d * own:d * own + own] = piece[0:obs, 0:own]
            weight[:, d * own:d * own + own] = piece[0:obs, own:2 * own]
        weighted = band[...]
    else:
        total = None
        scal = None
        for d, piece in enumerate(pieces):
            fold = piece[obs:obs + obs // 2]
            rest = jnp.concatenate([fold, pltpu.roll(fold, LANES // 2, 1)], axis=0)
            values = jnp.concatenate([piece[0:obs], rest], axis=1)
            stack = jnp.concatenate(split3(values), axis=0)
            prod = jnp.dot(stack, row_hot[d], preferred_element_type=jnp.float32)
            total = prod if total is None else total + prod
            tail = piece[obs + obs // 2:obs + obs // 2 + 8]
            scal = tail if scal is None else scal + tail
        total = total[:obs] + (total[obs:2 * obs] + total[2 * obs:])
        weighted = weight[...] * total
        out[slots:slots + 8] = scal
        out[slots + 8:slots + 16] = fold_sum(weighted * total)
    stack = jnp.concatenate(split3(weighted), axis=0)
    picked = jnp.dot(stack, own_hot[...], preferred_element_type=jnp.float32)
    picked = picked[:obs] + (picked[obs:2 * obs] + picked[2 * obs:])
    taken[0] = picked[:, :LANES]
    taken[1] = picked[:, LANES:]

    ones = jnp.ones((2 * LANES, LANES), jnp.bfloat16)
    lane = lax.broadcasted_iota(jnp.int32, (obs, LANES), 1)

    def body(g, c):
        chunk(g).wait()
        per = LANES // group
        base = (g % per) * group
        values = taken[g // per]
        high = values.astype(jnp.bfloat16)
        low = (values - high.astype(jnp.float32)).astype(jnp.bfloat16)
        none = jnp.zeros_like(high)
        stack = jnp.concatenate([
            jnp.concatenate([jnp.where(lane == base + k, high, none),
                             jnp.where(lane == base + k, low, none)], axis=1)
            for k in range(group // 2)
        ], axis=0)
        spread = jnp.dot(stack, ones, preferred_element_type=jnp.float32)
        values = pltpu.roll(values, LANES - base, 1)
        for k in range(group):
            slot = g * group + k
            wide = spread[obs * k:obs * k + obs] if k < group // 2 else values[:, k:k + 1]
            out[pl.ds(slot, 1), :] = jnp.sum(jac[slot] * wide, axis=0, keepdims=True)
        return c

    lax.fori_loop(0, groups, body, 0)


def spread_kernel(dims, first_call, *refs):
    lat_cells, lon_cells = dims
    counts, cells, own, from_a, from_b, from_x, from_s = refs[:7]
    refs = refs[7:]
    if not first_call:
        scal, refs = refs[0], refs[1:]
    faces_hbm, jac_hbm, refs = refs[:5], refs[5], refs[6:]
    if not first_call:
        grad_hbm, spread_hbm, refs = refs[0], refs[1], refs[2:]
    one_hbm, two_hbm, message = refs[:3]
    refs = refs[3:]
    face_lat, face_lon, keep, up, down, jac, one, two, grad, buf, mid, sems = refs
    loads = copies(list(zip(faces_hbm[:2], (face_lat, face_lon))), sems)
    nh, nv = counts[0], counts[1]
    rows = lat_cells + 2 * FRAME
    width = buf.shape[1]
    place_halos(
        buf, own, ((from_a, 0), (from_b, 0)), ((from_x, 0), (from_s, 0)), FRAME, dims
    )
    for load in loads:
        load.wait()
    loads = copies(
        list(zip(faces_hbm[2:], (keep, up, down))) + [(jac_hbm, jac)], sems.at[pl.ds(2, 4)]
    )
    if not first_call:
        old_loads = copies([(grad_hbm, grad), (spread_hbm, two)], sems.at[pl.ds(6, 2)])
    lateral_passes(buf, face_lat, face_lon, nh, 0, nh, 0, width)
    border = FRAME - REACH
    tall = lat_cells + 2 * REACH
    vertical = functools.partial(
        vertical_passes, buf, keep, up, down, border, border + tall, border, nv, 0, width
    )
    for load in loads[:3]:
        load.wait()
    vertical()

    def save(i, c):
        mid[i] = buf[FRAME + i]
        return c

    lax.fori_loop(0, lat_cells, save, 0)
    vertical()
    last_lateral(buf, face_lat, face_lon, nh, lon_cells)
    cols = slice(FRAME, FRAME + lon_cells)
    if not first_call:
        rr = jnp.sum(scal[0:8])
        alpha = rr / (rr + jnp.sum(scal[8:16]))
        for load in old_loads:
            load.wait()

    def finish(i, acc):
        place = pl.ds(pl.multiple_of(i * lon_cells, lon_cells), lon_cells)
        vector = mid[i, cols]
        after = buf[FRAME + i, cols]
        if first_call:
            one[place] = vector
            two[place] = after
        else:
            old = two[place]
            base = grad[place]
            applied = base + vector
            one[place] = applied
            two[place] = old - alpha * (old + after)
            vector = base - alpha * applied
        square = vector * vector
        for j in range(lon_cells // 8):
            acc = acc + square[8 * j:8 * j + 8]
        return acc

    norm = lax.fori_loop(0, lat_cells, finish, jnp.zeros((8, LANES), jnp.float32))
    stores = copies([(one, one_hbm), (two, two_hbm)], sems.at[pl.ds(8, 2)])
    loads[3].wait()
    obs = jac.shape[1]
    observe(cells, jac, two, message)
    message[obs + obs // 2:] = norm
    for store in stores:
        store.wait()


def final_kernel(dims, *refs):
    lat_cells, lon_cells = dims
    counts, own, from_a, from_b, from_x, from_s, scal0, scal1 = refs[:8]
    hbm, (increment, residual), refs = refs[8:17], refs[17:19], refs[19:]
    face_lat, face_lon, keep, up, down, grad, spread, image, spread_next, buf, sems = refs
    inner = pl.ds(FRAME - REACH, lat_cells + 2 * REACH)
    block = pl.ds(REACH, lat_cells)
    loads = copies(
        [(src.at[inner], dst.at[inner]) for src, dst in zip(hbm[:2], refs[:2])]
        + [(src.at[block], dst.at[block]) for src, dst in zip(hbm[2:5], refs[2:5])]
        + list(zip(hbm[5:], refs[5:9])), sems)
    nh, nv = counts[0], counts[1]
    place_halos(
        buf, own, ((from_a, 0), (from_b, 0)), ((from_x, 0), (from_s, 0)), REACH, dims
    )
    for load in loads[:2]:
        load.wait()
    last_lateral(buf, face_lat, face_lon, nh, lon_cells)
    left = FRAME // 8 * 8
    right = -(-(FRAME + lon_cells) // 8) * 8
    for load in loads[2:5]:
        load.wait()
    vertical_passes(
        buf, keep, up, down, FRAME, FRAME + lat_cells, FRAME - REACH, nv, left, right
    )
    rr0 = jnp.sum(scal0[0:8])
    alpha0 = rr0 / (rr0 + jnp.sum(scal0[8:16]))
    rr1 = jnp.sum(scal1[0:8])
    beta = rr1 / rr0
    alpha1 = rr1 / ((rr1 + jnp.sum(scal1[8:16])) - beta * (rr1 / alpha0))
    cols = slice(FRAME, FRAME + lon_cells)
    for load in loads[5:]:
        load.wait()

    def finish(i, c):
        place = pl.ds(pl.multiple_of(i * lon_cells, lon_cells), lon_cells)
        applied = image[place]
        rest = grad[place] - alpha0 * applied
        residual[place] = rest - alpha1 * ((rest + buf[FRAME + i, cols]) + beta * applied)
        old = spread[place]
        increment[place] = alpha0 * old + alpha1 * (spread_next[place] + beta * old)
        return c

    lax.fori_loop(0, lat_cells, finish, 0)


def local(innovation, obs_weight, jacobian, block_list, pass_counts, kappa_h, kappa_v):
    lat_cells, lon_cells, levels = kappa_h.shape
    cells_n = lat_cells * lon_cells
    slots, obs, _ = jacobian.shape
    own_rows = innovation.shape[1]
    n_lat, n_lon = lax.axis_size("lat"), lax.axis_size("lon")
    parts = n_lon // 2
    lon = lax.axis_index("lon")
    f32 = jnp.float32

    def swap(n, k):
        return [(i, i ^ k) for i in range(n)]

    def odd_pairs(n):
        return [(i, (i + 1) % n if i % 2 else (i - 1) % n) for i in range(n)]

    inner_pairs = [(0, 0), (n_lat - 1, n_lat - 1)] + [
        pair for i in range(1, n_lat - 1, 2) for pair in ((i, i + 1), (i + 1, i))]

    def send(x, axis, pairs):
        return lax.ppermute(x, axis, pairs)

    def gather_band(x):
        near = [x] + [send(x, "lon", swap(n_lon, 2 * k)) for k in range(1, parts)]
        return near + [send(piece, "lon", swap(n_lon, 1)) for piece in near]

    def lon_send(to_x, to_s):
        return send(to_x, "lon", swap(n_lon, 1)), send(to_s, "lon", odd_pairs(n_lon))

    def lat_send(to_a, to_b, pairs):
        return send(to_a, "lat", swap(n_lat, 1)), send(to_b, "lat", pairs)

    def lat_sum(tail, from_a, from_b):
        if n_lat != 4:
            return lax.psum(tail, "lat")
        return (tail + send(tail, "lat", swap(n_lat, 2))) + (from_a[slots:] + from_b[slots:])

    def scatter(message):
        return call(functools.partial(scatter_kernel, slots, cells_n), "scatter", field, (message, cells))

    def sides_of(own, from_a, from_b, reach):
        side = shape(side_rows(reach, lat_cells)[1], levels)
        strip = shape(reach * lon_cells, levels)
        strip_a, strip_b, to_x, to_s = call(
            functools.partial(sides_kernel, dims, slots, reach), "sides", (strip, strip, side, side),
            (own, from_a, from_b, *cells_near))
        return (strip_a, strip_b), (to_x, to_s)

    def halo(message, reach):
        from_a, from_b = lat_send(message, message, odd_pairs(n_lat))
        own = scatter(message)
        strips, sides = sides_of(own, from_a, from_b, reach)
        return (own, *strips, *lon_send(*sides)), lat_sum(message[slots:], from_a, from_b)

    vmem = pl.BlockSpec(memory_space=pltpu.VMEM)
    smem = pl.BlockSpec(memory_space=pltpu.SMEM)
    hbm = pl.BlockSpec(memory_space=pl.ANY)
    params = pltpu.CompilerParams(vmem_limit_bytes=VMEM_LIMIT)
    shape = lambda *dims: jax.ShapeDtypeStruct(dims, f32)
    scratch = lambda *dims: pltpu.VMEM(dims, f32)
    rows_h = lat_cells + 2 * FRAME
    rows_v = lat_cells + 2 * REACH
    width = lon_cells + 2 * FRAME
    band_rows = n_lon * own_rows
    dims = (lat_cells, lon_cells)
    field = shape(cells_n, levels)
    msg = shape(obs + obs // 2 + 8, LANES)
    wide, tall = shape(rows_h, width, levels), shape(rows_v, width, levels)
    wide_vmem, tall_vmem = scratch(rows_h, width, levels), scratch(rows_v, width, levels)
    field_vmem = scratch(cells_n, levels)
    jac_vmem = scratch(slots, obs, levels)
    faces_vmem = [wide_vmem] * 2 + [tall_vmem] * 3
    sems = lambda count: pltpu.SemaphoreType.DMA((count,))

    def call(kernel, name, outs, ins, scalars=0, far_in=(), far_out=False, scratches=(), params=params):
        out_specs = jax.tree.map(lambda _: vmem, outs)
        if far_out:
            out_specs = (hbm,) * far_out + out_specs[far_out:]
        specs = [smem] * scalars + [vmem] * (len(ins) - scalars) + [hbm] * len(far_in)
        return pl.pallas_call(
            kernel, out_shape=outs, in_specs=specs, out_specs=out_specs,
            scratch_shapes=list(scratches), compiler_params=params, name=name,
        )(*ins, *far_in)

    strip = shape((FRAME + REACH) * lon_cells + 8, levels)
    start_in = (innovation, obs_weight, block_list,
                kappa_h.reshape(cells_n, levels), kappa_v.reshape(cells_n, levels))
    first, root_h, root_v, to_a, to_b = call(
        functools.partial(start_kernel, dims), "start", (shape(obs + 8, LANES), field, field, strip, strip),
        (), far_in=start_in, scratches=[pltpu.VMEM(v.shape, v.dtype) for v in start_in] + [sems(5)],
        params=pltpu.CompilerParams(vmem_limit_bytes=START_LIMIT))
    k_strips = lat_send(to_a, to_b, inner_pairs)
    band = gather_band(first)
    cells_near = [v[(FRAME + REACH) * lon_cells:] for v in k_strips]

    def place_of(row):
        row = row.astype(jnp.int32)
        key = (row // own_rows) ^ lon
        at = (key // 2 + parts * (key % 2)) * own_rows + row % own_rows
        return jnp.where((row >= 0) & (row < band_rows), at, -1)

    all_at = place_of(jnp.stack([piece[obs:obs + 2] for piece in band]).reshape(n_lon, 2 * LANES))
    row_iota = jnp.arange(band_rows, dtype=jnp.int32)
    row_hot = (all_at[:, :, None] == row_iota[None, None, :]).astype(jnp.bfloat16)
    own_at = jnp.pad(place_of(block_list[0]), (0, 2 * LANES - slots), constant_values=-1)
    own_hot = (row_iota[:, None] == own_at[None, :]).astype(jnp.bfloat16)
    cells = jnp.clip(block_list[1:], 0, cells_n - 1)
    cells_flat = cells.reshape(slots)

    adj_scratch = [jac_vmem, scratch(2, obs, LANES), sems(slots // 64)]
    message, weight = call(
        functools.partial(adjoint_kernel, True, parts), "adjoint_first",
        (shape(slots, levels), shape(obs, band_rows)), (*band, own_hot), far_in=(jacobian,),
        scratches=[scratch(obs, band_rows)] + adj_scratch)

    from_a, from_b = lat_send(message, message, inner_pairs)
    own = scatter(message)
    side = shape(sum(side_rows(reach, lat_cells)[1] for reach in (FRAME, REACH)), levels)
    k_messages = call(functools.partial(face_sides_kernel, dims), "face_sides", (side, side),
                      (root_h, root_v, *k_strips))
    k_sides = lon_send(*k_messages)
    k_messages, from_a, from_b = lax.optimization_barrier((k_messages, from_a, from_b))
    strips, sides = sides_of(own, from_a, from_b, FRAME)
    halos = (own, *strips, *lon_send(*sides))
    faces = call(
        functools.partial(faces_kernel, dims), "faces", (wide, wide, tall, tall, tall),
        (root_h, root_v, *k_strips, *k_sides), far_out=5,
        scratches=faces_vmem + [scratch(rows_h + 1, width, levels), sems(5)])
    spread_scratch = faces_vmem + [jac_vmem] + [field_vmem] * 3 + [
        wide_vmem, scratch(lat_cells, width, levels), sems(10)]
    grad, spread, message = call(
        functools.partial(spread_kernel, dims, True), "spread_first", (field, field, msg),
        (pass_counts, cells_flat, *halos), 2, (*faces, jacobian), 2, spread_scratch)

    def adjoint(message):
        return call(
            functools.partial(adjoint_kernel, False, parts), "adjoint_next",
            shape(slots + 16, levels), (*gather_band(message), row_hot, weight, own_hot),
            far_in=(jacobian,), scratches=adj_scratch)

    halos, scal0 = halo(adjoint(message), FRAME)
    image, spread_next, message = call(
        functools.partial(spread_kernel, dims, False), "spread_next", (field, field, msg),
        (pass_counts, cells_flat, *halos, scal0), 2, (*faces, jacobian, grad, spread), 2, spread_scratch)
    halos, scal1 = halo(adjoint(message), REACH)
    increment, residual = call(
        functools.partial(final_kernel, dims), "final", (field, field),
        (pass_counts, *halos, scal0, scal1), 1,
        (*faces, grad, spread, image, spread_next), 0,
        faces_vmem + [field_vmem] * 4 + [wide_vmem, sems(9)])
    block = (lat_cells, lon_cells, levels)
    return increment.reshape(block), residual.reshape(block)


def solution(mesh):
    return jax.shard_map(
        local,
        mesh=mesh,
        in_specs=(
            P(None, ("lat", "lon")),
            P(None, ("lat", "lon")),
            P(("lat", "lon"), None, None),
            P(None, ("lat", "lon")),
            P(),
            P("lat", "lon", None),
            P("lat", "lon", None),
        ),
        out_specs=(P("lat", "lon", None), P("lat", "lon", None)),
        check_vma=False,
    )
```

```python
import functools

import jax
import jax.numpy as jnp
from jax import lax
from jax.experimental import pallas as pl
from jax.experimental.pallas import tpu as pltpu
from jax.sharding import PartitionSpec as P

LANES = 128
VMEM_LIMIT = 48 * 1024 * 1024
START_LIMIT = 60 * 1024 * 1024
REACH = 6
FRAME = 2 * REACH


def split3(x):
    high = x.astype(jnp.bfloat16)
    rest = x - high.astype(jnp.float32)
    mid = rest.astype(jnp.bfloat16)
    low = (rest - mid.astype(jnp.float32)).astype(jnp.bfloat16)
    return high, mid, low


def fold_sum(x):
    total = None
    for i in range(x.shape[0] // 8):
        for j in range(x.shape[1] // LANES):
            tile = x[8 * i:8 * i + 8, LANES * j:LANES * j + LANES]
            total = tile if total is None else total + tile
    return total


def copies(pairs, sems):
    started = [pltpu.make_async_copy(src, dst, sems.at[i]) for i, (src, dst) in enumerate(pairs)]
    for copy in started:
        copy.start()
    return started


def to_strided(natural, buf, rows):
    count = natural.shape[1] // 8
    for i in rows:
        for v in range(count):
            buf[i, 8 * v:8 * v + 8] = natural[i, pl.ds(v, 8, stride=count)]


def to_natural(buf, natural, rows, skip=0):
    count = natural.shape[1] // 8
    for i in rows:
        for v in range(count):
            natural[i - skip, pl.ds(v, 8, stride=count)] = buf[i, 8 * v:8 * v + 8]


def eastern(tiles):
    return tiles[1:] + [pltpu.roll(tiles[0], 7, 0)]


def western(tiles):
    return [pltpu.roll(tiles[-1], 1, 0)] + tiles[:-1]


def lateral_pass(buf, face_lat, face_lon, first, last):
    def tiles(ref, row):
        return [ref[row, 8 * v:8 * v + 8] for v in range(buf.shape[1] // 8)]

    def advance(row, carry):
        current, flux_above = carry
        below = tiles(buf, row + 1)
        flux = [f * (b - w) for f, b, w in zip(tiles(face_lat, row), below, current)]
        side = [f * (e - w) for f, e, w in zip(tiles(face_lon, row), eastern(current), current)]
        for v, (w, f, g, e, h) in enumerate(zip(current, flux, flux_above, side, western(side))):
            buf[row, 8 * v:8 * v + 8] = w + ((f - g) + (e - h))
        return below, flux

    def four(step, carry):
        for k in range(4):
            carry = advance(first + 4 * step + k, carry)
        return carry

    def two(step, carry):
        for k in range(2):
            carry = advance(last - 2 + k, carry)
        return carry

    start = tiles(buf, first)
    flux = [f * (w - a) for f, w, a in zip(tiles(face_lat, first - 1), start, tiles(buf, first - 1))]
    count = last - first
    carry = lax.fori_loop(0, count // 4, four, (start, flux))
    lax.fori_loop(0, (count % 4) // 2, two, carry)


def lateral_passes(buf, face_lat, face_lon, nh, begin, end):
    rows, lost = buf.shape[0], FRAME - 2 * nh

    def body(p, c):
        lateral_pass(buf, face_lat, face_lon, lost + p, rows - lost - p)
        return c

    lax.fori_loop(begin + 1, end + 1, body, 0)


def shift_matrix():
    source = lax.broadcasted_iota(jnp.int32, (2 * LANES, 2 * LANES), 0) % LANES
    target = lax.broadcasted_iota(jnp.int32, (2 * LANES, 2 * LANES), 1)
    wanted = jnp.where(target < LANES, target + 1, target - LANES - 1)
    return (source == wanted).astype(jnp.bfloat16)


def vertical_passes(buf, keep, up, down, first, last, offset, nv):
    width = buf.shape[1]
    shifts = shift_matrix()
    at = list(range(first, last))
    half = (last - first) // 2

    def sweep(p, c):
        values = [buf[i] for i in at]
        stack = jnp.concatenate(values[:half], axis=0)
        high = stack.astype(jnp.bfloat16)
        low = (stack - high.astype(jnp.float32)).astype(jnp.bfloat16)
        moved = jnp.dot(jnp.concatenate([high, low], axis=1), shifts, preferred_element_type=jnp.float32)
        for n, (i, w) in enumerate(zip(at, values)):
            if n < half:
                here = moved[width * n:width * n + width]
                above, below = here[:, :LANES], here[:, LANES:]
            else:
                above, below = pltpu.roll(w, LANES - 1, 1), pltpu.roll(w, 1, 1)
            buf[i] = keep[i - offset] * w + (up[i - offset] * above + down[i - offset] * below)
        return c

    lax.fori_loop(0, nv, sweep, 0)


def side_rows(reach, lat_cells):
    plan, first = [], 0
    for i in range(lat_cells + 2 * reach):
        outside = max(reach - i, i - (reach + lat_cells - 1), 0)
        if outside:
            plan.append((first, reach - outside))
            first += reach - outside
        else:
            plan.append(((i - reach) * reach, reach))
    return plan, (lat_cells * reach, -(-first // 8) * 8)


def even(axis):
    return lax.axis_index(axis) % 2 == 0


def place_halos(buf, own, strips, sides, reach, dims):
    lat_cells, lon_cells = dims
    (from_a, skip_a), (from_b, skip_b) = strips
    from_x, from_s = sides
    base = FRAME - reach
    lat_even, lon_even = even("lat"), even("lon")
    south = FRAME + lat_cells
    row_a = jnp.where(lat_even, south, base)
    row_b = jnp.where(lat_even, base, south)
    cols = slice(FRAME, FRAME + lon_cells)
    for i in range(lat_cells):
        buf[FRAME + i, cols] = own[i * lon_cells:(i + 1) * lon_cells]
    for i in range(reach):
        place = i * lon_cells
        buf[row_a + i, cols] = from_a[skip_a + place:skip_a + place + lon_cells]
        buf[row_b + i, cols] = from_b[skip_b + place:skip_b + place + lon_cells]

    def put_sides(west, east):
        for i, (first, count) in enumerate(side_rows(reach, lat_cells)[0]):
            part = 0 if reach <= i < reach + lat_cells else 1
            for (ref, skip), place in ((west[part], FRAME - count), (east[part], FRAME + lon_cells)):
                if count:
                    buf[base + i, place:place + count] = ref[skip + first:skip + first + count]

    pl.when(lon_even)(lambda: put_sides(from_s, from_x))
    pl.when(jnp.logical_not(lon_even))(lambda: put_sides(from_x, from_s))


def pack_own_sides(own, outs, reach, dims):
    lat_cells, lon_cells = dims

    def write(west, east):
        for i in range(lat_cells):
            row = i * lon_cells
            for (ref, skip), place in ((west, row), (east, row + lon_cells - reach)):
                ref[skip + i * reach:skip + (i + 1) * reach] = own[place:place + reach]

    to_x, to_s = outs
    pl.when(even("lon"))(lambda: write(to_s, to_x))
    pl.when(jnp.logical_not(even("lon")))(lambda: write(to_x, to_s))


def pack_corners(strips, outs, reach, dims):
    lat_cells, lon_cells = dims
    from_a, from_b = strips
    to_x, to_s = outs
    plan, _ = side_rows(reach, lat_cells)

    def write(north, south, west, east):
        for i, (first, count) in enumerate(plan):
            if reach <= i < reach + lat_cells or not count:
                continue
            ref, skip = north if i < reach else south
            row = skip + (i if i < reach else i - reach - lat_cells) * lon_cells
            for (out, base), place in ((west, row), (east, row + lon_cells - count)):
                out[base + first:base + first + count] = ref[place:place + count]

    for even_lat in (True, False):
        for even_lon in (True, False):
            poles = (from_b, from_a) if even_lat else (from_a, from_b)
            edges = (to_s, to_x) if even_lon else (to_x, to_s)
            pl.when((even("lat") == even_lat) & (even("lon") == even_lon))(
                functools.partial(write, *poles, *edges))


def cells_at(rows, slots):
    return jnp.concatenate([rows[0:1], rows[1:2, :slots - LANES]], axis=1).astype(jnp.int32)


def add_into(cells, parts, count):
    hot = lax.broadcasted_iota(jnp.int32, (count, cells.shape[1]), 0) == cells
    both = jnp.dot(hot.astype(jnp.bfloat16), jnp.concatenate(parts, axis=1),
                   preferred_element_type=jnp.float32)
    return both[:, :LANES] + (both[:, LANES:2 * LANES] + both[:, 2 * LANES:])


def scatter_kernel(dims, slots, reach, message, cells, own, *outs):
    own[...] = add_into(cells[...], split3(message[0:slots]), dims[0] * dims[1])
    if outs:
        pack_own_sides(own, [(out, 0) for out in outs], reach, dims)


def sides_kernel(dims, slots, reach, joined, *refs):
    lat_cells, lon_cells = dims
    own, refs = (refs[0], refs[1:]) if joined else (None, refs)
    from_a, from_b, cells_a, cells_b, strip_a, strip_b, to_x, to_s = refs
    skip = (lat_cells - reach) * lon_cells
    for message, cells, strip, north in (
        (from_a, cells_a, strip_a, jnp.logical_not(even("lat"))),
        (from_b, cells_b, strip_b, even("lat")),
    ):
        at = cells_at(cells, slots) - jnp.where(north, skip, 0)
        strip[...] = add_into(at, split3(message[0:slots]), reach * lon_cells)
    base = 0
    if joined:
        pack_own_sides(own, ((to_x, 0), (to_s, 0)), reach, dims)
        base = side_rows(reach, lat_cells)[1][0]
    pack_corners(((strip_a, 0), (strip_b, 0)), ((to_x, base), (to_s, base)), reach, dims)


def face_places(lat_cells):
    (own_h, corner_h), (own_v, _) = (side_rows(reach, lat_cells)[1] for reach in (FRAME, REACH))
    return (0, own_h + own_v), (own_h, own_h + own_v + corner_h)


def face_sides_kernel(dims, root_h, root_v, from_a, from_b, to_x, to_s):
    skip = 0
    for root, reach, (own, corner) in zip((root_h, root_v), (FRAME, REACH), face_places(dims[0])):
        pack_own_sides(root, ((to_x, own), (to_s, own)), reach, dims)
        pack_corners(((from_a, skip), (from_b, skip)), ((to_x, corner), (to_s, corner)), reach, dims)
        skip += reach * dims[1]


def start_kernel(dims, *refs):
    lat_cells, lon_cells = dims
    sources, (first, root_h, root_v, to_a, to_b), refs = refs[:5], refs[5:10], refs[10:]
    (innovation, obs_weight, block_list, kappa_h, kappa_v), sems = refs[:5], refs[5]
    loads = copies(list(zip(sources, refs[:5])), sems)
    obs, own = innovation.shape
    slots = block_list.shape[1]
    for load in loads:
        load.wait()
    weight = obs_weight[...]
    first[0:obs, 0:own] = weight * innovation[...]
    first[0:obs, own:2 * own] = weight
    places = block_list[...].astype(jnp.float32)
    tail = to_a.shape[0] - 8
    cells = jnp.clip(places[1:2], 0.0, lat_cells * lon_cells - 1.0)
    for ref, base, row in ((first, obs, places[0:1]), (to_a, tail, cells), (to_b, tail, cells)):
        ref[base:base + 8] = jnp.full((8, LANES), -1.0, jnp.float32)
        ref[base:base + 1] = row[:, :LANES]
        ref[base + 1:base + 2, 0:slots - LANES] = row[:, LANES:]
    root_h[...] = jnp.sqrt(kappa_h[...])
    root_v[...] = jnp.sqrt(kappa_v[...])

    def write(south, north):
        skip = 0
        for ref, reach in ((root_h, FRAME), (root_v, REACH)):
            count = reach * lon_cells
            north[skip:skip + count] = ref[0:count]
            south[skip:skip + count] = ref[lat_cells * lon_cells - count:]
            skip += count

    pl.when(even("lat"))(lambda: write(to_a, to_b))
    pl.when(jnp.logical_not(even("lat")))(lambda: write(to_b, to_a))


def faces_kernel(dims, root_h, root_v, from_a, from_b, from_x, from_s, *refs):
    lat_cells, lon_cells = dims
    out, (face_lat, face_lon, keep, up, down, natural, buf, sems) = refs[:5], refs[5:]
    rows = lat_cells + 2 * FRAME
    width = buf.shape[1]
    places = face_places(lat_cells)
    place_halos(
        natural, root_h, ((from_a, 0), (from_b, 0)),
        [[(ref, place) for place in places[0]] for ref in (from_x, from_s)], FRAME, dims,
    )

    def clear(first):
        def body(i, c):
            natural[first + i] = jnp.zeros((width, LANES), jnp.float32)
            return c
        lax.fori_loop(0, FRAME, body, 0)

    lat = lax.axis_index("lat")
    pl.when(lat == 0)(lambda: clear(0))
    pl.when(lat == lax.axis_size("lat") - 1)(lambda: clear(FRAME + lat_cells))

    to_strided(natural, buf, range(rows))
    buf[rows] = jnp.zeros((width, LANES), jnp.float32)

    def lateral(step, c):
        for k in range(4):
            i = 4 * step + k
            here = [buf[i, 8 * v:8 * v + 8] for v in range(width // 8)]
            face_lat[i] = buf[i] * buf[i + 1]
            for v, (w, e) in enumerate(zip(here, eastern(here))):
                face_lon[i, 8 * v:8 * v + 8] = w * e
        return c

    lax.fori_loop(0, rows // 4, lateral, 0)
    side = copies([(face_lat, out[0]), (face_lon, out[1])], sems)
    skip = FRAME * lon_cells
    place_halos(
        natural, root_v, ((from_a, skip), (from_b, skip)),
        [[(ref, place) for place in places[1]] for ref in (from_x, from_s)], REACH, dims,
    )
    to_strided(natural, buf, range(FRAME - REACH, rows - FRAME + REACH))
    top = lax.broadcasted_iota(jnp.int32, (width, LANES), 1) == LANES - 1

    def vertical(step, c):
        at = [4 * step + k for k in range(4)]
        here = [buf[FRAME - REACH + i] for i in at]
        face = [jnp.where(top, 0.0, v * pltpu.roll(v, LANES - 1, 1)) for v in here]
        below = [pltpu.roll(v, 1, 1) for v in face]
        for i, f, g in zip(at, face, below):
            up[i] = f
            down[i] = g
            keep[i] = 1.0 - (f + g)
        return c

    lax.fori_loop(0, (lat_cells + 2 * REACH) // 4, vertical, 0)
    level = copies([(keep, out[2]), (up, out[3]), (down, out[4])], sems.at[pl.ds(2, 3)])
    for copy in side + level:
        copy.wait()


def observe(cells, jac, field, out):
    slots, obs, _ = jac.shape
    lane = lax.broadcasted_iota(jnp.int32, (obs, LANES), 1)

    ones = jnp.ones((2 * LANES, LANES), jnp.bfloat16)
    group = 64

    def part(first, count):
        def body(step, acc):
            at = [first + step * group + k for k in range(group)]
            prods = [jac[slot] * field[pl.ds(cells[slot], 1), :] for slot in at]
            half = jnp.concatenate(prods[:group // 2], axis=0)
            high = half.astype(jnp.bfloat16)
            low = (half - high.astype(jnp.float32)).astype(jnp.bfloat16)
            sums = jnp.dot(jnp.concatenate([high, low], axis=1), ones, preferred_element_type=jnp.float32)
            for k in range(group):
                if k < group // 2:
                    value = sums[obs * k:obs * k + obs]
                else:
                    value = jnp.sum(prods[k], axis=1, keepdims=True)
                acc = jnp.where(lane == step * group + k, value, acc)
            return acc
        return lax.fori_loop(0, count // group, body, jnp.zeros((obs, LANES), jnp.float32))

    out[0:obs] = part(0, LANES)
    rest = part(LANES, slots - LANES)
    out[obs:obs + obs // 2] = rest[:obs // 2] + pltpu.roll(rest[obs // 2:], LANES // 2, 1)


def adjoint_kernel(first_call, parts, *refs):
    pieces, refs = refs[:2 * parts], refs[2 * parts:]
    if first_call:
        own_hot, jac_hbm, out, weight, band, jac, taken, sems = refs
    else:
        row_hot, weight, own_hot, jac_hbm, out, jac, taken, sems = refs
    slots, obs, _ = jac.shape
    group = 64
    groups = slots // group

    def chunk(g):
        place = pl.ds(g * group, group)
        return pltpu.make_async_copy(jac_hbm.at[place], jac.at[place], sems.at[g])

    for g in range(groups):
        chunk(g).start()
    if first_call:
        own = weight.shape[1] // (2 * parts)
        for d, piece in enumerate(pieces):
            band[:, d * own:d * own + own] = piece[0:obs, 0:own]
            weight[:, d * own:d * own + own] = piece[0:obs, own:2 * own]
        weighted = band[...]
    else:
        total = None
        scal = None
        for d, piece in enumerate(pieces):
            fold = piece[obs:obs + obs // 2]
            rest = jnp.concatenate([fold, pltpu.roll(fold, LANES // 2, 1)], axis=0)
            values = jnp.concatenate([piece[0:obs], rest], axis=1)
            stack = jnp.concatenate(split3(values), axis=0)
            prod = jnp.dot(stack, row_hot[d], preferred_element_type=jnp.float32)
            total = prod if total is None else total + prod
            tail = piece[obs + obs // 2:obs + obs // 2 + 8]
            scal = tail if scal is None else scal + tail
        total = total[:obs] + (total[obs:2 * obs] + total[2 * obs:])
        weighted = weight[...] * total
        out[slots:slots + 8] = scal
        out[slots + 8:slots + 16] = fold_sum(weighted * total)
    stack = jnp.concatenate(split3(weighted), axis=0)
    picked = jnp.dot(stack, own_hot[...], preferred_element_type=jnp.float32)
    picked = picked[:obs] + (picked[obs:2 * obs] + picked[2 * obs:])
    taken[0] = picked[:, :LANES]
    taken[1] = picked[:, LANES:]

    ones = jnp.ones((2 * LANES, LANES), jnp.bfloat16)
    lane = lax.broadcasted_iota(jnp.int32, (obs, LANES), 1)

    def body(g, c):
        chunk(g).wait()
        per = LANES // group
        base = (g % per) * group
        values = taken[g // per]
        high = values.astype(jnp.bfloat16)
        low = (values - high.astype(jnp.float32)).astype(jnp.bfloat16)
        none = jnp.zeros_like(high)
        stack = jnp.concatenate([
            jnp.concatenate([jnp.where(lane == base + k, high, none),
                             jnp.where(lane == base + k, low, none)], axis=1)
            for k in range(group // 2)
        ], axis=0)
        spread = jnp.dot(stack, ones, preferred_element_type=jnp.float32)
        values = pltpu.roll(values, LANES - base, 1)
        for k in range(group):
            slot = g * group + k
            wide = spread[obs * k:obs * k + obs] if k < group // 2 else values[:, k:k + 1]
            out[pl.ds(slot, 1), :] = jnp.sum(jac[slot] * wide, axis=0, keepdims=True)
        return c

    lax.fori_loop(0, groups, body, 0)


def spread_kernel(dims, first_call, *refs):
    lat_cells, lon_cells = dims
    counts, cells, own, from_a, from_b = refs[:5]
    if first_call:
        (from_x, from_s), refs = refs[5:7], refs[7:]
        corner = side_rows(FRAME, lat_cells)[1][0]
        sides = [[(ref, 0), (ref, corner)] for ref in (from_x, from_s)]
    else:
        (own_x, own_s, corner_x, corner_s), refs = refs[5:9], refs[9:]
        sides = [[(own_x, 0), (corner_x, 0)], [(own_s, 0), (corner_s, 0)]]
    if not first_call:
        scal, refs = refs[0], refs[1:]
    faces_hbm, jac_hbm, refs = refs[:5], refs[5], refs[6:]
    if not first_call:
        grad_hbm, spread_hbm, refs = refs[0], refs[1], refs[2:]
    one_hbm, two_hbm, message = refs[:3]
    refs = refs[3:]
    face_lat, face_lon, keep, up, down, jac, one, two, grad, natural, buf, mid, sems = refs
    loads = copies(list(zip(faces_hbm[:2], (face_lat, face_lon))), sems)
    nh, nv = counts[0], counts[1]
    rows = lat_cells + 2 * FRAME
    place_halos(
        natural, own, ((from_a, 0), (from_b, 0)), sides, FRAME, dims
    )
    to_strided(natural, buf, range(rows))
    for load in loads:
        load.wait()
    loads = copies(
        list(zip(faces_hbm[2:], (keep, up, down))) + [(jac_hbm, jac)], sems.at[pl.ds(2, 4)]
    )
    if not first_call:
        old_loads = copies([(grad_hbm, grad), (spread_hbm, two)], sems.at[pl.ds(6, 2)])
    lateral_passes(buf, face_lat, face_lon, nh, 0, nh)
    border = FRAME - REACH
    tall = lat_cells + 2 * REACH
    vertical = functools.partial(
        vertical_passes, buf, keep, up, down, border, border + tall, border, nv
    )
    for load in loads[:3]:
        load.wait()
    vertical()

    block = range(FRAME, FRAME + lat_cells)
    to_natural(buf, mid, block, FRAME)
    vertical()
    lateral_passes(buf, face_lat, face_lon, nh, nh, 2 * nh)
    to_natural(buf, natural, block)
    cols = slice(FRAME, FRAME + lon_cells)
    if not first_call:
        rr = jnp.sum(scal[0:8])
        alpha = rr / (rr + jnp.sum(scal[8:16]))
        for load in old_loads:
            load.wait()

    def finish(i, acc):
        place = pl.ds(pl.multiple_of(i * lon_cells, lon_cells), lon_cells)
        vector = mid[i, cols]
        after = natural[FRAME + i, cols]
        if first_call:
            one[place] = vector
            two[place] = after
        else:
            old = two[place]
            base = grad[place]
            applied = base + vector
            one[place] = applied
            two[place] = old - alpha * (old + after)
            vector = base - alpha * applied
        square = vector * vector
        for j in range(lon_cells // 8):
            acc = acc + square[8 * j:8 * j + 8]
        return acc

    norm = lax.fori_loop(0, lat_cells, finish, jnp.zeros((8, LANES), jnp.float32))
    stores = copies([(one, one_hbm), (two, two_hbm)], sems.at[pl.ds(8, 2)])
    loads[3].wait()
    obs = jac.shape[1]
    observe(cells, jac, two, message)
    message[obs + obs // 2:] = norm
    for store in stores:
        store.wait()


def final_kernel(dims, *refs):
    lat_cells, lon_cells = dims
    counts, own, from_a, from_b, own_x, own_s, corner_x, corner_s, scal0, scal1 = refs[:10]
    hbm, (increment, residual), refs = refs[10:19], refs[19:21], refs[21:]
    face_lat, face_lon, keep, up, down, grad, spread, image, spread_next, natural, buf, sems = refs
    inner = pl.ds(FRAME - REACH, lat_cells + 2 * REACH)
    block = pl.ds(REACH, lat_cells)
    loads = copies(
        [(src.at[inner], dst.at[inner]) for src, dst in zip(hbm[:2], refs[:2])]
        + [(src.at[block], dst.at[block]) for src, dst in zip(hbm[2:5], refs[2:5])]
        + list(zip(hbm[5:], refs[5:9])), sems)
    nh, nv = counts[0], counts[1]
    place_halos(
        natural, own, ((from_a, 0), (from_b, 0)),
        (((own_x, 0), (corner_x, 0)), ((own_s, 0), (corner_s, 0))), REACH, dims,
    )
    to_strided(natural, buf, range(FRAME - REACH, FRAME + lat_cells + REACH))
    for load in loads[:2]:
        load.wait()
    lateral_passes(buf, face_lat, face_lon, nh, nh, 2 * nh)
    for load in loads[2:5]:
        load.wait()
    vertical_passes(
        buf, keep, up, down, FRAME, FRAME + lat_cells, FRAME - REACH, nv
    )
    to_natural(buf, natural, range(FRAME, FRAME + lat_cells))
    rr0 = jnp.sum(scal0[0:8])
    alpha0 = rr0 / (rr0 + jnp.sum(scal0[8:16]))
    rr1 = jnp.sum(scal1[0:8])
    beta = rr1 / rr0
    alpha1 = rr1 / ((rr1 + jnp.sum(scal1[8:16])) - beta * (rr1 / alpha0))
    cols = slice(FRAME, FRAME + lon_cells)
    for load in loads[5:]:
        load.wait()

    def finish(i, c):
        place = pl.ds(pl.multiple_of(i * lon_cells, lon_cells), lon_cells)
        applied = image[place]
        rest = grad[place] - alpha0 * applied
        residual[place] = rest - alpha1 * ((rest + natural[FRAME + i, cols]) + beta * applied)
        old = spread[place]
        increment[place] = alpha0 * old + alpha1 * (spread_next[place] + beta * old)
        return c

    lax.fori_loop(0, lat_cells, finish, 0)


def local(innovation, obs_weight, jacobian, block_list, pass_counts, kappa_h, kappa_v):
    lat_cells, lon_cells, levels = kappa_h.shape
    cells_n = lat_cells * lon_cells
    slots, obs, _ = jacobian.shape
    own_rows = innovation.shape[1]
    n_lat, n_lon = lax.axis_size("lat"), lax.axis_size("lon")
    parts = n_lon // 2
    lon = lax.axis_index("lon")
    f32 = jnp.float32

    def swap(n, k):
        return [(i, i ^ k) for i in range(n)]

    def odd_pairs(n):
        return [(i, (i + 1) % n if i % 2 else (i - 1) % n) for i in range(n)]

    inner_pairs = [(0, 0), (n_lat - 1, n_lat - 1)] + [
        pair for i in range(1, n_lat - 1, 2) for pair in ((i, i + 1), (i + 1, i))]

    def send(x, axis, pairs):
        return lax.ppermute(x, axis, pairs)

    def gather_band(x):
        near = [x] + [send(x, "lon", swap(n_lon, 2 * k)) for k in range(1, parts)]
        return near + [send(piece, "lon", swap(n_lon, 1)) for piece in near]

    def lon_send(to_x, to_s):
        return send(to_x, "lon", swap(n_lon, 1)), send(to_s, "lon", odd_pairs(n_lon))

    def lat_send(to_a, to_b, pairs):
        return send(to_a, "lat", swap(n_lat, 1)), send(to_b, "lat", pairs)

    def lat_sum(tail, from_a, from_b):
        if n_lat != 4:
            return lax.psum(tail, "lat")
        return (tail + send(tail, "lat", swap(n_lat, 2))) + (from_a[slots:] + from_b[slots:])

    def side_shapes(reach):
        return [shape(size, levels) for size in side_rows(reach, lat_cells)[1]]

    def joined_shape(*reaches):
        return shape(sum(sum(side_rows(reach, lat_cells)[1]) for reach in reaches), levels)

    def scatter(message, reach):
        side = side_shapes(reach)[0]
        own, to_x, to_s = call(
            functools.partial(scatter_kernel, dims, slots, reach), "scatter", (field, side, side),
            (message, cells))
        return own, lon_send(to_x, to_s)

    def sides_of(from_a, from_b, reach, joined=()):
        side = side_shapes(reach)[1]
        if joined:
            side = joined_shape(reach)
        strip = shape(reach * lon_cells, levels)
        strip_a, strip_b, to_x, to_s = call(
            functools.partial(sides_kernel, dims, slots, reach, bool(joined)), "sides",
            (strip, strip, side, side), (*joined, from_a, from_b, *cells_near))
        return (strip_a, strip_b), lon_send(to_x, to_s)

    def halo(message, reach):
        from_a, from_b = lat_send(message, message, odd_pairs(n_lat))
        own, own_sides = scatter(message, reach)
        strips, corners = sides_of(from_a, from_b, reach)
        return (own, *strips, *own_sides, *corners), lat_sum(message[slots:], from_a, from_b)

    vmem = pl.BlockSpec(memory_space=pltpu.VMEM)
    smem = pl.BlockSpec(memory_space=pltpu.SMEM)
    hbm = pl.BlockSpec(memory_space=pl.ANY)
    params = pltpu.CompilerParams(vmem_limit_bytes=VMEM_LIMIT)
    shape = lambda *dims: jax.ShapeDtypeStruct(dims, f32)
    scratch = lambda *dims: pltpu.VMEM(dims, f32)
    rows_h = lat_cells + 2 * FRAME
    rows_v = lat_cells + 2 * REACH
    width = lon_cells + 2 * FRAME
    band_rows = n_lon * own_rows
    dims = (lat_cells, lon_cells)
    field = shape(cells_n, levels)
    msg = shape(obs + obs // 2 + 8, LANES)
    wide, tall = shape(rows_h, width, levels), shape(rows_v, width, levels)
    wide_vmem, tall_vmem = scratch(rows_h, width, levels), scratch(rows_v, width, levels)
    field_vmem = scratch(cells_n, levels)
    jac_vmem = scratch(slots, obs, levels)
    faces_vmem = [wide_vmem] * 2 + [tall_vmem] * 3
    sems = lambda count: pltpu.SemaphoreType.DMA((count,))

    def call(kernel, name, outs, ins, scalars=0, far_in=(), far_out=False, scratches=(), params=params):
        out_specs = jax.tree.map(lambda _: vmem, outs)
        if far_out:
            out_specs = (hbm,) * far_out + out_specs[far_out:]
        specs = [smem] * scalars + [vmem] * (len(ins) - scalars) + [hbm] * len(far_in)
        return pl.pallas_call(
            kernel, out_shape=outs, in_specs=specs, out_specs=out_specs,
            scratch_shapes=list(scratches), compiler_params=params, name=name,
        )(*ins, *far_in)

    strip = shape((FRAME + REACH) * lon_cells + 8, levels)
    start_in = (innovation, obs_weight, block_list,
                kappa_h.reshape(cells_n, levels), kappa_v.reshape(cells_n, levels))
    first, root_h, root_v, to_a, to_b = call(
        functools.partial(start_kernel, dims), "start", (shape(obs + 8, LANES), field, field, strip, strip),
        (), far_in=start_in, scratches=[pltpu.VMEM(v.shape, v.dtype) for v in start_in] + [sems(5)],
        params=pltpu.CompilerParams(vmem_limit_bytes=START_LIMIT))
    k_strips = lat_send(to_a, to_b, inner_pairs)
    band = gather_band(first)
    cells_near = [v[(FRAME + REACH) * lon_cells:] for v in k_strips]

    def place_of(row):
        row = row.astype(jnp.int32)
        key = (row // own_rows) ^ lon
        at = (key // 2 + parts * (key % 2)) * own_rows + row % own_rows
        return jnp.where((row >= 0) & (row < band_rows), at, -1)

    all_at = place_of(jnp.stack([piece[obs:obs + 2] for piece in band]).reshape(n_lon, 2 * LANES))
    row_iota = jnp.arange(band_rows, dtype=jnp.int32)
    row_hot = (all_at[:, :, None] == row_iota[None, None, :]).astype(jnp.bfloat16)
    own_at = jnp.pad(place_of(block_list[0]), (0, 2 * LANES - slots), constant_values=-1)
    own_hot = (row_iota[:, None] == own_at[None, :]).astype(jnp.bfloat16)
    cells = jnp.clip(block_list[1:], 0, cells_n - 1)
    cells_flat = cells.reshape(slots)

    adj_scratch = [jac_vmem, scratch(2, obs, LANES), sems(slots // 64)]
    message, weight = call(
        functools.partial(adjoint_kernel, True, parts), "adjoint_first",
        (shape(slots, levels), shape(obs, band_rows)), (*band, own_hot), far_in=(jacobian,),
        scratches=[scratch(obs, band_rows)] + adj_scratch)

    from_a, from_b = lat_send(message, message, inner_pairs)
    own = call(functools.partial(scatter_kernel, dims, slots, FRAME), "scatter", field, (message, cells))
    side = joined_shape(FRAME, REACH)
    k_messages = call(functools.partial(face_sides_kernel, dims), "face_sides", (side, side),
                      (root_h, root_v, *k_strips))
    k_sides = lon_send(*k_messages)
    k_messages, from_a, from_b = lax.optimization_barrier((k_messages, from_a, from_b))
    strips, sides = sides_of(from_a, from_b, FRAME, (own,))
    halos = (own, *strips, *sides)
    faces = call(
        functools.partial(faces_kernel, dims), "faces", (wide, wide, tall, tall, tall),
        (root_h, root_v, *k_strips, *k_sides), far_out=5,
        scratches=faces_vmem + [wide_vmem, scratch(rows_h + 1, width, levels), sems(5)])
    spread_scratch = faces_vmem + [jac_vmem] + [field_vmem] * 3 + [
        wide_vmem, wide_vmem, scratch(lat_cells, width, levels), sems(10)]
    grad, spread, message = call(
        functools.partial(spread_kernel, dims, True), "spread_first", (field, field, msg),
        (pass_counts, cells_flat, *halos), 2, (*faces, jacobian), 2, spread_scratch)

    def adjoint(message):
        return call(
            functools.partial(adjoint_kernel, False, parts), "adjoint_next",
            shape(slots + 16, levels), (*gather_band(message), row_hot, weight, own_hot),
            far_in=(jacobian,), scratches=adj_scratch)

    halos, scal0 = halo(adjoint(message), FRAME)
    image, spread_next, message = call(
        functools.partial(spread_kernel, dims, False), "spread_next", (field, field, msg),
        (pass_counts, cells_flat, *halos, scal0), 2, (*faces, jacobian, grad, spread), 2, spread_scratch)
    halos, scal1 = halo(adjoint(message), REACH)
    increment, residual = call(
        functools.partial(final_kernel, dims), "final", (field, field),
        (pass_counts, *halos, scal0, scal1), 1,
        (*faces, grad, spread, image, spread_next), 0,
        faces_vmem + [field_vmem] * 4 + [wide_vmem, wide_vmem, sems(9)])
    block = (lat_cells, lon_cells, levels)
    return increment.reshape(block), residual.reshape(block)


def solution(mesh):
    return jax.shard_map(
        local,
        mesh=mesh,
        in_specs=(
            P(None, ("lat", "lon")),
            P(None, ("lat", "lon")),
            P(("lat", "lon"), None, None),
            P(None, ("lat", "lon")),
            P(),
            P("lat", "lon", None),
            P("lat", "lon", None),
        ),
        out_specs=(P("lat", "lon", None), P("lat", "lon", None)),
        check_vma=False,
    )
```

```python
import functools

import jax
import jax.numpy as jnp
from jax import lax
from jax.experimental import pallas as pl
from jax.experimental.pallas import tpu as pltpu
from jax.sharding import PartitionSpec as P

LANES = 128
VMEM_LIMIT = 40 * 1024 * 1024
NEAR_LIMIT = 32 * 1024 * 1024
START_LIMIT = 60 * 1024 * 1024
REACH = 6
FRAME = 2 * REACH


def split3(x):
    high = x.astype(jnp.bfloat16)
    rest = x - high.astype(jnp.float32)
    mid = rest.astype(jnp.bfloat16)
    low = (rest - mid.astype(jnp.float32)).astype(jnp.bfloat16)
    return high, mid, low


def fold_sum(x):
    total = None
    for i in range(x.shape[0] // 8):
        for j in range(x.shape[1] // LANES):
            tile = x[8 * i:8 * i + 8, LANES * j:LANES * j + LANES]
            total = tile if total is None else total + tile
    return total


def copies(pairs, sems):
    started = [pltpu.make_async_copy(src, dst, sems.at[i]) for i, (src, dst) in enumerate(pairs)]
    for copy in started:
        copy.start()
    return started


def to_strided(natural, buf, rows):
    count = natural.shape[1] // 8
    for i in rows:
        for v in range(count):
            buf[i, 8 * v:8 * v + 8] = natural[i, pl.ds(v, 8, stride=count)]


def to_natural(buf, natural, rows, skip=0):
    count = natural.shape[1] // 8
    for i in rows:
        for v in range(count):
            natural[i - skip, pl.ds(v, 8, stride=count)] = buf[i, 8 * v:8 * v + 8]


def eastern(tiles):
    return tiles[1:] + [pltpu.roll(tiles[0], 7, 0)]


def western(tiles):
    return [pltpu.roll(tiles[-1], 1, 0)] + tiles[:-1]


def lateral_pass(buf, face_lat, face_lon, first, last):
    def tiles(ref, row):
        return [ref[row, 8 * v:8 * v + 8] for v in range(buf.shape[1] // 8)]

    def advance(row, carry):
        current, flux_above = carry
        below = tiles(buf, row + 1)
        flux = [f * (b - w) for f, b, w in zip(tiles(face_lat, row), below, current)]
        side = [f * (e - w) for f, e, w in zip(tiles(face_lon, row), eastern(current), current)]
        for v, (w, f, g, e, h) in enumerate(zip(current, flux, flux_above, side, western(side))):
            buf[row, 8 * v:8 * v + 8] = w + ((f - g) + (e - h))
        return below, flux

    def four(step, carry):
        for k in range(4):
            carry = advance(first + 4 * step + k, carry)
        return carry

    def two(step, carry):
        for k in range(2):
            carry = advance(last - 2 + k, carry)
        return carry

    start = tiles(buf, first)
    flux = [f * (w - a) for f, w, a in zip(tiles(face_lat, first - 1), start, tiles(buf, first - 1))]
    count = last - first
    carry = lax.fori_loop(0, count // 4, four, (start, flux))
    lax.fori_loop(0, (count % 4) // 2, two, carry)


def lateral_passes(buf, face_lat, face_lon, nh, begin, end):
    rows, lost = buf.shape[0], FRAME - 2 * nh

    def body(p, c):
        lateral_pass(buf, face_lat, face_lon, lost + p, rows - lost - p)
        return c

    lax.fori_loop(begin + 1, end + 1, body, 0)


def shift_matrix():
    source = lax.broadcasted_iota(jnp.int32, (2 * LANES, 2 * LANES), 0) % LANES
    target = lax.broadcasted_iota(jnp.int32, (2 * LANES, 2 * LANES), 1)
    wanted = jnp.where(target < LANES, target + 1, target - LANES - 1)
    return (source == wanted).astype(jnp.bfloat16)


def vertical_passes(buf, keep, up, down, first, last, offset, nv):
    width = buf.shape[1]
    shifts = shift_matrix()
    at = list(range(first, last))
    half = (last - first) // 2

    def sweep(p, c):
        values = [buf[i] for i in at]
        stack = jnp.concatenate(values[:half], axis=0)
        high = stack.astype(jnp.bfloat16)
        low = (stack - high.astype(jnp.float32)).astype(jnp.bfloat16)
        moved = jnp.dot(jnp.concatenate([high, low], axis=1), shifts, preferred_element_type=jnp.float32)
        for n, (i, w) in enumerate(zip(at, values)):
            if n < half:
                here = moved[width * n:width * n + width]
                above, below = here[:, :LANES], here[:, LANES:]
            else:
                above, below = pltpu.roll(w, LANES - 1, 1), pltpu.roll(w, 1, 1)
            buf[i] = keep[i - offset] * w + (up[i - offset] * above + down[i - offset] * below)
        return c

    lax.fori_loop(0, nv, sweep, 0)


def side_rows(reach, lat_cells):
    plan, first = [], 0
    for i in range(lat_cells + 2 * reach):
        outside = max(reach - i, i - (reach + lat_cells - 1), 0)
        if outside:
            plan.append((first, reach - outside))
            first += reach - outside
        else:
            plan.append(((i - reach) * reach, reach))
    return plan, (lat_cells * reach, -(-first // 8) * 8)


def even(axis):
    return lax.axis_index(axis) % 2 == 0


def place_halos(buf, own, strips, sides, reach, dims):
    lat_cells, lon_cells = dims
    (from_a, skip_a), (from_b, skip_b) = strips
    from_x, from_s = sides
    base = FRAME - reach
    lat_even, lon_even = even("lat"), even("lon")
    south = FRAME + lat_cells
    row_a = jnp.where(lat_even, south, base)
    row_b = jnp.where(lat_even, base, south)
    cols = slice(FRAME, FRAME + lon_cells)
    for i in range(lat_cells):
        buf[FRAME + i, cols] = own[i * lon_cells:(i + 1) * lon_cells]
    for i in range(reach):
        place = i * lon_cells
        buf[row_a + i, cols] = from_a[skip_a + place:skip_a + place + lon_cells]
        buf[row_b + i, cols] = from_b[skip_b + place:skip_b + place + lon_cells]

    def put_sides(west, east):
        for i, (first, count) in enumerate(side_rows(reach, lat_cells)[0]):
            part = 0 if reach <= i < reach + lat_cells else 1
            for (ref, skip), place in ((west[part], FRAME - count), (east[part], FRAME + lon_cells)):
                if count:
                    buf[base + i, place:place + count] = ref[skip + first:skip + first + count]

    pl.when(lon_even)(lambda: put_sides(from_s, from_x))
    pl.when(jnp.logical_not(lon_even))(lambda: put_sides(from_x, from_s))


def pack_own_sides(own, outs, reach, dims):
    lat_cells, lon_cells = dims

    def write(west, east):
        for i in range(lat_cells):
            row = i * lon_cells
            for (ref, skip), place in ((west, row), (east, row + lon_cells - reach)):
                ref[skip + i * reach:skip + (i + 1) * reach] = own[place:place + reach]

    to_x, to_s = outs
    pl.when(even("lon"))(lambda: write(to_s, to_x))
    pl.when(jnp.logical_not(even("lon")))(lambda: write(to_x, to_s))


def pack_corners(strips, outs, reach, dims):
    lat_cells, lon_cells = dims
    from_a, from_b = strips
    to_x, to_s = outs
    plan, _ = side_rows(reach, lat_cells)

    def write(north, south, west, east):
        for i, (first, count) in enumerate(plan):
            if reach <= i < reach + lat_cells or not count:
                continue
            ref, skip = north if i < reach else south
            row = skip + (i if i < reach else i - reach - lat_cells) * lon_cells
            for (out, base), place in ((west, row), (east, row + lon_cells - count)):
                out[base + first:base + first + count] = ref[place:place + count]

    for even_lat in (True, False):
        for even_lon in (True, False):
            poles = (from_b, from_a) if even_lat else (from_a, from_b)
            edges = (to_s, to_x) if even_lon else (to_x, to_s)
            pl.when((even("lat") == even_lat) & (even("lon") == even_lon))(
                functools.partial(write, *poles, *edges))


def cells_at(rows, slots):
    return jnp.concatenate([rows[0:1], rows[1:2, :slots - LANES]], axis=1).astype(jnp.int32)


def add_into(cells, parts, count):
    hot = lax.broadcasted_iota(jnp.int32, (count, cells.shape[1]), 0) == cells
    both = jnp.dot(hot.astype(jnp.bfloat16), jnp.concatenate(parts, axis=1),
                   preferred_element_type=jnp.float32)
    return both[:, :LANES] + (both[:, LANES:2 * LANES] + both[:, 2 * LANES:])


def scatter_kernel(dims, slots, reach, message, cells, own, *outs):
    own[...] = add_into(cells[...], split3(message[0:slots]), dims[0] * dims[1])
    if outs:
        pack_own_sides(own, [(out, 0) for out in outs], reach, dims)


def sides_kernel(dims, slots, reach, joined, *refs):
    lat_cells, lon_cells = dims
    own, refs = (refs[0], refs[1:]) if joined else (None, refs)
    from_a, from_b, cells_a, cells_b, strip_a, strip_b, to_x, to_s = refs
    skip = (lat_cells - reach) * lon_cells
    for message, cells, strip, north in (
        (from_a, cells_a, strip_a, jnp.logical_not(even("lat"))),
        (from_b, cells_b, strip_b, even("lat")),
    ):
        at = cells_at(cells, slots) - jnp.where(north, skip, 0)
        strip[...] = add_into(at, split3(message[0:slots]), reach * lon_cells)
    base = 0
    if joined:
        pack_own_sides(own, ((to_x, 0), (to_s, 0)), reach, dims)
        base = side_rows(reach, lat_cells)[1][0]
    pack_corners(((strip_a, 0), (strip_b, 0)), ((to_x, base), (to_s, base)), reach, dims)


def face_places(lat_cells):
    (own_h, corner_h), (own_v, _) = (side_rows(reach, lat_cells)[1] for reach in (FRAME, REACH))
    return (0, own_h + own_v), (own_h, own_h + own_v + corner_h)


def face_sides_kernel(dims, root_h, root_v, from_a, from_b, to_x, to_s):
    skip = 0
    for root, reach, (own, corner) in zip((root_h, root_v), (FRAME, REACH), face_places(dims[0])):
        pack_own_sides(root, ((to_x, own), (to_s, own)), reach, dims)
        pack_corners(((from_a, skip), (from_b, skip)), ((to_x, corner), (to_s, corner)), reach, dims)
        skip += reach * dims[1]


def start_kernel(dims, *refs):
    lat_cells, lon_cells = dims
    sources, (first, root_h, root_v, to_a, to_b), refs = refs[:5], refs[5:10], refs[10:]
    (innovation, obs_weight, block_list, kappa_h, kappa_v), sems = refs[:5], refs[5]
    loads = copies(list(zip(sources, refs[:5])), sems)
    obs, own = innovation.shape
    slots = block_list.shape[1]
    for load in loads:
        load.wait()
    weight = obs_weight[...]
    first[0:obs, 0:own] = weight * innovation[...]
    first[0:obs, own:2 * own] = weight
    places = block_list[...].astype(jnp.float32)
    tail = to_a.shape[0] - 8
    cells = jnp.clip(places[1:2], 0.0, lat_cells * lon_cells - 1.0)
    for ref, base, row in ((first, obs, places[0:1]), (to_a, tail, cells), (to_b, tail, cells)):
        ref[base:base + 8] = jnp.full((8, LANES), -1.0, jnp.float32)
        ref[base:base + 1] = row[:, :LANES]
        ref[base + 1:base + 2, 0:slots - LANES] = row[:, LANES:]
    root_h[...] = jnp.sqrt(kappa_h[...])
    root_v[...] = jnp.sqrt(kappa_v[...])

    def write(south, north):
        skip = 0
        for ref, reach in ((root_h, FRAME), (root_v, REACH)):
            count = reach * lon_cells
            north[skip:skip + count] = ref[0:count]
            south[skip:skip + count] = ref[lat_cells * lon_cells - count:]
            skip += count

    pl.when(even("lat"))(lambda: write(to_a, to_b))
    pl.when(jnp.logical_not(even("lat")))(lambda: write(to_b, to_a))


def faces_kernel(dims, root_h, root_v, from_a, from_b, from_x, from_s, *refs):
    lat_cells, lon_cells = dims
    out, (face_lat, face_lon, keep, up, down, natural, buf, sems) = refs[:5], refs[5:]
    rows = lat_cells + 2 * FRAME
    width = buf.shape[1]
    places = face_places(lat_cells)
    place_halos(
        natural, root_h, ((from_a, 0), (from_b, 0)),
        [[(ref, place) for place in places[0]] for ref in (from_x, from_s)], FRAME, dims,
    )

    def clear(first):
        def body(i, c):
            natural[first + i] = jnp.zeros((width, LANES), jnp.float32)
            return c
        lax.fori_loop(0, FRAME, body, 0)

    lat = lax.axis_index("lat")
    pl.when(lat == 0)(lambda: clear(0))
    pl.when(lat == lax.axis_size("lat") - 1)(lambda: clear(FRAME + lat_cells))

    to_strided(natural, buf, range(rows))
    buf[rows] = jnp.zeros((width, LANES), jnp.float32)

    def lateral(step, c):
        for k in range(4):
            i = 4 * step + k
            here = [buf[i, 8 * v:8 * v + 8] for v in range(width // 8)]
            face_lat[i] = buf[i] * buf[i + 1]
            for v, (w, e) in enumerate(zip(here, eastern(here))):
                face_lon[i, 8 * v:8 * v + 8] = w * e
        return c

    lax.fori_loop(0, rows // 4, lateral, 0)
    side = copies([(face_lat, out[0]), (face_lon, out[1])], sems)
    skip = FRAME * lon_cells
    place_halos(
        natural, root_v, ((from_a, skip), (from_b, skip)),
        [[(ref, place) for place in places[1]] for ref in (from_x, from_s)], REACH, dims,
    )
    to_strided(natural, buf, range(FRAME - REACH, rows - FRAME + REACH))
    top = lax.broadcasted_iota(jnp.int32, (width, LANES), 1) == LANES - 1

    def vertical(step, c):
        at = [4 * step + k for k in range(4)]
        here = [buf[FRAME - REACH + i] for i in at]
        face = [jnp.where(top, 0.0, v * pltpu.roll(v, LANES - 1, 1)) for v in here]
        below = [pltpu.roll(v, 1, 1) for v in face]
        for i, f, g in zip(at, face, below):
            up[i] = f
            down[i] = g
            keep[i] = 1.0 - (f + g)
        return c

    lax.fori_loop(0, (lat_cells + 2 * REACH) // 4, vertical, 0)
    level = copies([(keep, out[2]), (up, out[3]), (down, out[4])], sems.at[pl.ds(2, 3)])
    for copy in side + level:
        copy.wait()


def observe(cells, jac, field, out):
    slots, obs, _ = jac.shape
    lane = lax.broadcasted_iota(jnp.int32, (obs, LANES), 1)

    ones = jnp.ones((2 * LANES, LANES), jnp.bfloat16)
    group = 64

    def part(first, count):
        def body(step, acc):
            at = [first + step * group + k for k in range(group)]
            prods = [jac[slot] * field[pl.ds(cells[slot], 1), :] for slot in at]
            half = jnp.concatenate(prods[:group // 2], axis=0)
            high = half.astype(jnp.bfloat16)
            low = (half - high.astype(jnp.float32)).astype(jnp.bfloat16)
            sums = jnp.dot(jnp.concatenate([high, low], axis=1), ones, preferred_element_type=jnp.float32)
            for k in range(group):
                if k < group // 2:
                    value = sums[obs * k:obs * k + obs]
                else:
                    value = jnp.sum(prods[k], axis=1, keepdims=True)
                acc = jnp.where(lane == step * group + k, value, acc)
            return acc
        return lax.fori_loop(0, count // group, body, jnp.zeros((obs, LANES), jnp.float32))

    out[0:obs] = part(0, LANES)
    rest = part(LANES, slots - LANES)
    out[obs:obs + obs // 2] = rest[:obs // 2] + pltpu.roll(rest[obs // 2:], LANES // 2, 1)


def adjoint_kernel(first_call, parts, *refs):
    pieces, refs = refs[:2 * parts], refs[2 * parts:]
    if first_call:
        own_hot, jac_hbm, out, weight, band, jac, taken, sems = refs
    else:
        row_hot, weight, own_hot, jac, out, taken = refs
    slots, obs, _ = jac.shape
    group = 64
    groups = slots // group

    def chunk(g):
        place = pl.ds(g * group, group)
        return pltpu.make_async_copy(jac_hbm.at[place], jac.at[place], sems.at[g])

    for g in range(groups if first_call else 0):
        chunk(g).start()
    if first_call:
        own = weight.shape[1] // (2 * parts)
        for d, piece in enumerate(pieces):
            band[:, d * own:d * own + own] = piece[0:obs, 0:own]
            weight[:, d * own:d * own + own] = piece[0:obs, own:2 * own]
        weighted = band[...]
    else:
        total = None
        scal = None
        for d, piece in enumerate(pieces):
            fold = piece[obs:obs + obs // 2]
            rest = jnp.concatenate([fold, pltpu.roll(fold, LANES // 2, 1)], axis=0)
            values = jnp.concatenate([piece[0:obs], rest], axis=1)
            stack = jnp.concatenate(split3(values), axis=0)
            prod = jnp.dot(stack, row_hot[d], preferred_element_type=jnp.float32)
            total = prod if total is None else total + prod
            tail = piece[obs + obs // 2:obs + obs // 2 + 8]
            scal = tail if scal is None else scal + tail
        total = total[:obs] + (total[obs:2 * obs] + total[2 * obs:])
        weighted = weight[...] * total
        out[slots:slots + 8] = scal
        out[slots + 8:slots + 16] = fold_sum(weighted * total)
    stack = jnp.concatenate(split3(weighted), axis=0)
    picked = jnp.dot(stack, own_hot[...], preferred_element_type=jnp.float32)
    picked = picked[:obs] + (picked[obs:2 * obs] + picked[2 * obs:])
    taken[0] = picked[:, :LANES]
    taken[1] = picked[:, LANES:]

    ones = jnp.ones((2 * LANES, LANES), jnp.bfloat16)
    lane = lax.broadcasted_iota(jnp.int32, (obs, LANES), 1)

    def body(g, c):
        if first_call:
            chunk(g).wait()
        per = LANES // group
        base = (g % per) * group
        values = taken[g // per]
        high = values.astype(jnp.bfloat16)
        low = (values - high.astype(jnp.float32)).astype(jnp.bfloat16)
        none = jnp.zeros_like(high)
        stack = jnp.concatenate([
            jnp.concatenate([jnp.where(lane == base + k, high, none),
                             jnp.where(lane == base + k, low, none)], axis=1)
            for k in range(group // 2)
        ], axis=0)
        spread = jnp.dot(stack, ones, preferred_element_type=jnp.float32)
        values = pltpu.roll(values, LANES - base, 1)
        for k in range(group):
            slot = g * group + k
            wide = spread[obs * k:obs * k + obs] if k < group // 2 else values[:, k:k + 1]
            out[pl.ds(slot, 1), :] = jnp.sum(jac[slot] * wide, axis=0, keepdims=True)
        return c

    lax.fori_loop(0, groups, body, 0)


def spread_kernel(dims, first_call, *refs):
    lat_cells, lon_cells = dims
    counts, cells, own, from_a, from_b = refs[:5]
    if first_call:
        (from_x, from_s), refs = refs[5:7], refs[7:]
        corner = side_rows(FRAME, lat_cells)[1][0]
        sides = [[(ref, 0), (ref, corner)] for ref in (from_x, from_s)]
    else:
        (own_x, own_s, corner_x, corner_s), refs = refs[5:9], refs[9:]
        sides = [[(own_x, 0), (corner_x, 0)], [(own_s, 0), (corner_s, 0)]]
    if not first_call:
        scal, refs = refs[0], refs[1:]
    if first_call:
        faces_hbm, jac_hbm, refs = refs[:5], refs[5], refs[6:]
        one_hbm, two_hbm, message, jac = refs[:4]
        refs = refs[4:]
    else:
        jac, faces_hbm, grad_hbm, spread_hbm = refs[0], refs[1:6], refs[6], refs[7]
        one_hbm, two_hbm, message = refs[8:11]
        refs = refs[11:]
    face_lat, face_lon, keep, up, down, one, two, grad, natural, buf, mid, sems = refs
    loads = copies(list(zip(faces_hbm[:2], (face_lat, face_lon))), sems)
    nh, nv = counts[0], counts[1]
    rows = lat_cells + 2 * FRAME
    place_halos(
        natural, own, ((from_a, 0), (from_b, 0)), sides, FRAME, dims
    )
    to_strided(natural, buf, range(rows))
    for load in loads:
        load.wait()
    loads = copies(
        list(zip(faces_hbm[2:], (keep, up, down))) + ([(jac_hbm, jac)] if first_call else []),
        sems.at[pl.ds(2, 4)])
    if not first_call:
        old_loads = copies([(grad_hbm, grad), (spread_hbm, two)], sems.at[pl.ds(6, 2)])
    lateral_passes(buf, face_lat, face_lon, nh, 0, nh)
    border = FRAME - REACH
    tall = lat_cells + 2 * REACH
    vertical = functools.partial(
        vertical_passes, buf, keep, up, down, border, border + tall, border, nv
    )
    for load in loads[:3]:
        load.wait()
    vertical()

    block = range(FRAME, FRAME + lat_cells)
    to_natural(buf, mid, block, FRAME)
    vertical()
    lateral_passes(buf, face_lat, face_lon, nh, nh, 2 * nh)
    to_natural(buf, natural, block)
    cols = slice(FRAME, FRAME + lon_cells)
    if not first_call:
        rr = jnp.sum(scal[0:8])
        alpha = rr / (rr + jnp.sum(scal[8:16]))
        for load in old_loads:
            load.wait()

    def finish(i, acc):
        place = pl.ds(pl.multiple_of(i * lon_cells, lon_cells), lon_cells)
        vector = mid[i, cols]
        after = natural[FRAME + i, cols]
        if first_call:
            one[place] = vector
            two[place] = after
        else:
            old = two[place]
            base = grad[place]
            applied = base + vector
            one[place] = applied
            two[place] = old - alpha * (old + after)
            vector = base - alpha * applied
        square = vector * vector
        for j in range(lon_cells // 8):
            acc = acc + square[8 * j:8 * j + 8]
        return acc

    norm = lax.fori_loop(0, lat_cells, finish, jnp.zeros((8, LANES), jnp.float32))
    stores = copies([(one, one_hbm), (two, two_hbm)], sems.at[pl.ds(8, 2)])
    for load in loads[3:]:
        load.wait()
    obs = jac.shape[1]
    observe(cells, jac, two, message)
    message[obs + obs // 2:] = norm
    for store in stores:
        store.wait()


def combine_kernel(scal0, scal1, grad, spread, image, spread_next, increment, base, step):
    rr0 = jnp.sum(scal0[0:8])
    alpha0 = rr0 / (rr0 + jnp.sum(scal0[8:16]))
    rr1 = jnp.sum(scal1[0:8])
    beta = rr1 / rr0
    alpha1 = rr1 / ((rr1 + jnp.sum(scal1[8:16])) - beta * (rr1 / alpha0))
    step[...] = jnp.full(step.shape, 1.0, jnp.float32) * alpha1
    applied = image[...]
    rest = grad[...] - alpha0 * applied
    base[...] = rest - alpha1 * (rest + beta * applied)
    old = spread[...]
    increment[...] = alpha0 * old + alpha1 * (spread_next[...] + beta * old)


def final_kernel(dims, *refs):
    lat_cells, lon_cells = dims
    counts, own, from_a, from_b, own_x, own_s, corner_x, corner_s, base, alpha = refs[:10]
    hbm, residual, refs = refs[10:15], refs[15], refs[16:]
    face_lat, face_lon, keep, up, down, natural, buf, sems = refs
    inner = pl.ds(FRAME - REACH, lat_cells + 2 * REACH)
    block = pl.ds(REACH, lat_cells)
    loads = copies(
        [(src.at[inner], dst.at[inner]) for src, dst in zip(hbm[:2], refs[:2])]
        + [(src.at[block], dst.at[block]) for src, dst in zip(hbm[2:5], refs[2:5])], sems)
    nh, nv = counts[0], counts[1]
    place_halos(
        natural, own, ((from_a, 0), (from_b, 0)),
        (((own_x, 0), (corner_x, 0)), ((own_s, 0), (corner_s, 0))), REACH, dims,
    )
    to_strided(natural, buf, range(FRAME - REACH, FRAME + lat_cells + REACH))
    for load in loads[:2]:
        load.wait()
    lateral_passes(buf, face_lat, face_lon, nh, nh, 2 * nh)
    for load in loads[2:]:
        load.wait()
    vertical_passes(
        buf, keep, up, down, FRAME, FRAME + lat_cells, FRAME - REACH, nv
    )
    to_natural(buf, natural, range(FRAME, FRAME + lat_cells))
    cols = slice(FRAME, FRAME + lon_cells)
    step = jnp.concatenate([alpha[...]] * (lon_cells // 8), axis=0)
    for i in range(lat_cells):
        place = slice(i * lon_cells, i * lon_cells + lon_cells)
        residual[place] = base[place] - step * natural[FRAME + i, cols]


def local(innovation, obs_weight, jacobian, block_list, pass_counts, kappa_h, kappa_v):
    lat_cells, lon_cells, levels = kappa_h.shape
    cells_n = lat_cells * lon_cells
    slots, obs, _ = jacobian.shape
    own_rows = innovation.shape[1]
    n_lat, n_lon = lax.axis_size("lat"), lax.axis_size("lon")
    parts = n_lon // 2
    lon = lax.axis_index("lon")
    f32 = jnp.float32

    def swap(n, k):
        return [(i, i ^ k) for i in range(n)]

    def odd_pairs(n):
        return [(i, (i + 1) % n if i % 2 else (i - 1) % n) for i in range(n)]

    inner_pairs = [(0, 0), (n_lat - 1, n_lat - 1)] + [
        pair for i in range(1, n_lat - 1, 2) for pair in ((i, i + 1), (i + 1, i))]

    def send(x, axis, pairs):
        return lax.ppermute(x, axis, pairs)

    def gather_band(x):
        near = [x] + [send(x, "lon", swap(n_lon, 2 * k)) for k in range(1, parts)]
        return near + [send(piece, "lon", swap(n_lon, 1)) for piece in near]

    def lon_send(to_x, to_s):
        return send(to_x, "lon", swap(n_lon, 1)), send(to_s, "lon", odd_pairs(n_lon))

    def lat_send(to_a, to_b, pairs):
        return send(to_a, "lat", swap(n_lat, 1)), send(to_b, "lat", pairs)

    def lat_sum(tail, from_a, from_b):
        if n_lat != 4:
            return lax.psum(tail, "lat")
        return (tail + send(tail, "lat", swap(n_lat, 2))) + (from_a[slots:] + from_b[slots:])

    def side_shapes(reach):
        return [shape(size, levels) for size in side_rows(reach, lat_cells)[1]]

    def joined_shape(*reaches):
        return shape(sum(sum(side_rows(reach, lat_cells)[1]) for reach in reaches), levels)

    def scatter(message, reach):
        side = side_shapes(reach)[0]
        own, to_x, to_s = call(
            functools.partial(scatter_kernel, dims, slots, reach), "scatter", (field, side, side),
            (message, cells))
        return own, lon_send(to_x, to_s)

    def sides_of(from_a, from_b, reach, joined=()):
        side = side_shapes(reach)[1]
        if joined:
            side = joined_shape(reach)
        strip = shape(reach * lon_cells, levels)
        strip_a, strip_b, to_x, to_s = call(
            functools.partial(sides_kernel, dims, slots, reach, bool(joined)), "sides",
            (strip, strip, side, side), (*joined, from_a, from_b, *cells_near))
        return (strip_a, strip_b), lon_send(to_x, to_s)

    def halo(message, reach):
        from_a, from_b = lat_send(message, message, odd_pairs(n_lat))
        own, own_sides = scatter(message, reach)
        strips, corners = sides_of(from_a, from_b, reach)
        return (own, *strips, *own_sides, *corners), lat_sum(message[slots:], from_a, from_b)

    vmem = pl.BlockSpec(memory_space=pltpu.VMEM)
    smem = pl.BlockSpec(memory_space=pltpu.SMEM)
    hbm = pl.BlockSpec(memory_space=pl.ANY)
    params = pltpu.CompilerParams(vmem_limit_bytes=VMEM_LIMIT)
    shape = lambda *dims: jax.ShapeDtypeStruct(dims, f32)
    scratch = lambda *dims: pltpu.VMEM(dims, f32)
    rows_h = lat_cells + 2 * FRAME
    rows_v = lat_cells + 2 * REACH
    width = lon_cells + 2 * FRAME
    band_rows = n_lon * own_rows
    dims = (lat_cells, lon_cells)
    field = shape(cells_n, levels)
    msg = shape(obs + obs // 2 + 8, LANES)
    wide, tall = shape(rows_h, width, levels), shape(rows_v, width, levels)
    wide_vmem, tall_vmem = scratch(rows_h, width, levels), scratch(rows_v, width, levels)
    field_vmem = scratch(cells_n, levels)
    jac_vmem = scratch(slots, obs, levels)
    faces_vmem = [wide_vmem] * 2 + [tall_vmem] * 3
    sems = lambda count: pltpu.SemaphoreType.DMA((count,))

    def call(kernel, name, outs, ins, scalars=0, far_in=(), far_out=False, scratches=(), params=params):
        out_specs = jax.tree.map(lambda _: vmem, outs)
        if far_out:
            out_specs = (hbm,) * far_out + out_specs[far_out:]
        specs = [smem] * scalars + [vmem] * (len(ins) - scalars) + [hbm] * len(far_in)
        return pl.pallas_call(
            kernel, out_shape=outs, in_specs=specs, out_specs=out_specs,
            scratch_shapes=list(scratches), compiler_params=params, name=name,
        )(*ins, *far_in)

    strip = shape((FRAME + REACH) * lon_cells + 8, levels)
    start_in = (innovation, obs_weight, block_list,
                kappa_h.reshape(cells_n, levels), kappa_v.reshape(cells_n, levels))
    first, root_h, root_v, to_a, to_b = call(
        functools.partial(start_kernel, dims), "start", (shape(obs + 8, LANES), field, field, strip, strip),
        (), far_in=start_in, scratches=[pltpu.VMEM(v.shape, v.dtype) for v in start_in] + [sems(5)],
        params=pltpu.CompilerParams(vmem_limit_bytes=START_LIMIT))
    k_strips = lat_send(to_a, to_b, inner_pairs)
    band = gather_band(first)
    cells_near = [v[(FRAME + REACH) * lon_cells:] for v in k_strips]

    def place_of(row):
        row = row.astype(jnp.int32)
        key = (row // own_rows) ^ lon
        at = (key // 2 + parts * (key % 2)) * own_rows + row % own_rows
        return jnp.where((row >= 0) & (row < band_rows), at, -1)

    all_at = place_of(jnp.stack([piece[obs:obs + 2] for piece in band]).reshape(n_lon, 2 * LANES))
    row_iota = jnp.arange(band_rows, dtype=jnp.int32)
    row_hot = (all_at[:, :, None] == row_iota[None, None, :]).astype(jnp.bfloat16)
    own_at = jnp.pad(place_of(block_list[0]), (0, 2 * LANES - slots), constant_values=-1)
    own_hot = (row_iota[:, None] == own_at[None, :]).astype(jnp.bfloat16)
    cells = jnp.clip(block_list[1:], 0, cells_n - 1)
    cells_flat = cells.reshape(slots)

    adj_scratch = [jac_vmem, scratch(2, obs, LANES), sems(slots // 64)]
    message, weight = call(
        functools.partial(adjoint_kernel, True, parts), "adjoint_first",
        (shape(slots, levels), shape(obs, band_rows)), (*band, own_hot), far_in=(jacobian,),
        scratches=[scratch(obs, band_rows)] + adj_scratch)

    from_a, from_b = lat_send(message, message, inner_pairs)
    own = call(functools.partial(scatter_kernel, dims, slots, FRAME), "scatter", field, (message, cells))
    side = joined_shape(FRAME, REACH)
    k_messages = call(functools.partial(face_sides_kernel, dims), "face_sides", (side, side),
                      (root_h, root_v, *k_strips))
    k_sides = lon_send(*k_messages)
    k_messages, from_a, from_b = lax.optimization_barrier((k_messages, from_a, from_b))
    strips, sides = sides_of(from_a, from_b, FRAME, (own,))
    halos = (own, *strips, *sides)
    faces = call(
        functools.partial(faces_kernel, dims), "faces", (wide, wide, tall, tall, tall),
        (root_h, root_v, *k_strips, *k_sides), far_out=5,
        scratches=faces_vmem + [wide_vmem, scratch(rows_h + 1, width, levels), sems(5)])
    spread_scratch = faces_vmem + [field_vmem] * 3 + [
        wide_vmem, wide_vmem, scratch(lat_cells, width, levels), sems(10)]
    near_params = pltpu.CompilerParams(vmem_limit_bytes=NEAR_LIMIT)
    grad, spread, message, near_jac = call(
        functools.partial(spread_kernel, dims, True), "spread_first",
        (field, field, msg, shape(*jacobian.shape)),
        (pass_counts, cells_flat, *halos), 2, (*faces, jacobian), 2, spread_scratch)

    def adjoint(message):
        return call(
            functools.partial(adjoint_kernel, False, parts), "adjoint_next",
            shape(slots + 16, levels), (*gather_band(message), row_hot, weight, own_hot, near_jac),
            scratches=[scratch(2, obs, LANES)], params=near_params)

    halos, scal0 = halo(adjoint(message), FRAME)
    image, spread_next, message = call(
        functools.partial(spread_kernel, dims, False), "spread_next", (field, field, msg),
        (pass_counts, cells_flat, *halos, scal0, near_jac), 2, (*faces, grad, spread), 2, spread_scratch,
        near_params)
    halos, scal1 = halo(adjoint(message), REACH)
    increment, base, step = call(
        combine_kernel, "combine", (field, field, shape(8, LANES)),
        (scal0, scal1, grad, spread, image, spread_next))
    residual = call(
        functools.partial(final_kernel, dims), "final", field,
        (pass_counts, *halos, base, step), 1, faces, 0,
        faces_vmem + [wide_vmem, wide_vmem, sems(5)])
    block = (lat_cells, lon_cells, levels)
    return increment.reshape(block), residual.reshape(block)


def solution(mesh):
    return jax.shard_map(
        local,
        mesh=mesh,
        in_specs=(
            P(None, ("lat", "lon")),
            P(None, ("lat", "lon")),
            P(("lat", "lon"), None, None),
            P(None, ("lat", "lon")),
            P(),
            P("lat", "lon", None),
            P("lat", "lon", None),
        ),
        out_specs=(P("lat", "lon", None), P("lat", "lon", None)),
        check_vma=False,
    )
```

```python
import functools

import jax
import jax.numpy as jnp
from jax import lax
from jax.experimental import pallas as pl
from jax.experimental.pallas import tpu as pltpu
from jax.sharding import PartitionSpec as P

LANES = 128
VMEM_LIMIT = 40 * 1024 * 1024
NEAR_LIMIT = 32 * 1024 * 1024
FIRST_LIMIT = 48 * 1024 * 1024
START_LIMIT = 60 * 1024 * 1024
REACH = 6
FRAME = 2 * REACH


def split3(x):
    high = x.astype(jnp.bfloat16)
    rest = x - high.astype(jnp.float32)
    mid = rest.astype(jnp.bfloat16)
    low = (rest - mid.astype(jnp.float32)).astype(jnp.bfloat16)
    return high, mid, low


def fold_sum(x):
    total = None
    for i in range(x.shape[0] // 8):
        for j in range(x.shape[1] // LANES):
            tile = x[8 * i:8 * i + 8, LANES * j:LANES * j + LANES]
            total = tile if total is None else total + tile
    return total


def copies(pairs, sems):
    started = [pltpu.make_async_copy(src, dst, sems.at[i]) for i, (src, dst) in enumerate(pairs)]
    for copy in started:
        copy.start()
    return started


def to_strided(natural, buf, rows):
    count = natural.shape[1] // 8
    for i in rows:
        for v in range(count):
            buf[i, 8 * v:8 * v + 8] = natural[i, pl.ds(v, 8, stride=count)]


def to_natural(buf, natural, rows, skip=0):
    count = natural.shape[1] // 8
    for i in rows:
        for v in range(count):
            natural[i - skip, pl.ds(v, 8, stride=count)] = buf[i, 8 * v:8 * v + 8]


def eastern(tiles):
    return tiles[1:] + [pltpu.roll(tiles[0], 7, 0)]


def western(tiles):
    return [pltpu.roll(tiles[-1], 1, 0)] + tiles[:-1]


def lateral_pass(buf, face_lat, face_lon, first, last):
    def tiles(ref, row):
        return [ref[row, 8 * v:8 * v + 8] for v in range(buf.shape[1] // 8)]

    def advance(row, carry):
        current, flux_above = carry
        below = tiles(buf, row + 1)
        flux = [f * (b - w) for f, b, w in zip(tiles(face_lat, row), below, current)]
        side = [f * (e - w) for f, e, w in zip(tiles(face_lon, row), eastern(current), current)]
        for v, (w, f, g, e, h) in enumerate(zip(current, flux, flux_above, side, western(side))):
            buf[row, 8 * v:8 * v + 8] = w + ((f - g) + (e - h))
        return below, flux

    def four(step, carry):
        for k in range(4):
            carry = advance(first + 4 * step + k, carry)
        return carry

    def two(step, carry):
        for k in range(2):
            carry = advance(last - 2 + k, carry)
        return carry

    start = tiles(buf, first)
    flux = [f * (w - a) for f, w, a in zip(tiles(face_lat, first - 1), start, tiles(buf, first - 1))]
    count = last - first
    carry = lax.fori_loop(0, count // 4, four, (start, flux))
    lax.fori_loop(0, (count % 4) // 2, two, carry)


def lateral_passes(buf, face_lat, face_lon, nh, begin, end):
    rows, lost = buf.shape[0], FRAME - 2 * nh

    def body(p, c):
        lateral_pass(buf, face_lat, face_lon, lost + p, rows - lost - p)
        return c

    lax.fori_loop(begin + 1, end + 1, body, 0)


def shift_matrix():
    source = lax.broadcasted_iota(jnp.int32, (2 * LANES, 2 * LANES), 0) % LANES
    target = lax.broadcasted_iota(jnp.int32, (2 * LANES, 2 * LANES), 1)
    wanted = jnp.where(target < LANES, target + 1, target - LANES - 1)
    return (source == wanted).astype(jnp.bfloat16)


def vertical_passes(buf, keep, up, down, first, last, offset, nv):
    width = buf.shape[1]
    shifts = shift_matrix()
    at = list(range(first, last))
    half = (last - first) // 2

    def sweep(p, c):
        values = [buf[i] for i in at]
        stack = jnp.concatenate(values[:half], axis=0)
        high = stack.astype(jnp.bfloat16)
        low = (stack - high.astype(jnp.float32)).astype(jnp.bfloat16)
        moved = jnp.dot(jnp.concatenate([high, low], axis=1), shifts, preferred_element_type=jnp.float32)
        for n, (i, w) in enumerate(zip(at, values)):
            if n < half:
                here = moved[width * n:width * n + width]
                above, below = here[:, :LANES], here[:, LANES:]
            else:
                above, below = pltpu.roll(w, LANES - 1, 1), pltpu.roll(w, 1, 1)
            buf[i] = keep[i - offset] * w + (up[i - offset] * above + down[i - offset] * below)
        return c

    lax.fori_loop(0, nv, sweep, 0)


def side_rows(reach, lat_cells):
    plan, first = [], 0
    for i in range(lat_cells + 2 * reach):
        outside = max(reach - i, i - (reach + lat_cells - 1), 0)
        if outside:
            plan.append((first, reach - outside))
            first += reach - outside
        else:
            plan.append(((i - reach) * reach, reach))
    return plan, (lat_cells * reach, -(-first // 8) * 8)


def even(axis):
    return lax.axis_index(axis) % 2 == 0


def place_halos(buf, own, strips, sides, reach, dims):
    lat_cells, lon_cells = dims
    (from_a, skip_a), (from_b, skip_b) = strips
    from_x, from_s = sides
    base = FRAME - reach
    lat_even, lon_even = even("lat"), even("lon")
    south = FRAME + lat_cells
    row_a = jnp.where(lat_even, south, base)
    row_b = jnp.where(lat_even, base, south)
    cols = slice(FRAME, FRAME + lon_cells)
    for i in range(lat_cells):
        buf[FRAME + i, cols] = own[i * lon_cells:(i + 1) * lon_cells]
    for i in range(reach):
        place = i * lon_cells
        buf[row_a + i, cols] = from_a[skip_a + place:skip_a + place + lon_cells]
        buf[row_b + i, cols] = from_b[skip_b + place:skip_b + place + lon_cells]

    def put_sides(west, east):
        for i, (first, count) in enumerate(side_rows(reach, lat_cells)[0]):
            part = 0 if reach <= i < reach + lat_cells else 1
            for (ref, skip), place in ((west[part], FRAME - count), (east[part], FRAME + lon_cells)):
                if count:
                    buf[base + i, place:place + count] = ref[skip + first:skip + first + count]

    pl.when(lon_even)(lambda: put_sides(from_s, from_x))
    pl.when(jnp.logical_not(lon_even))(lambda: put_sides(from_x, from_s))


def pack_own_sides(own, outs, reach, dims):
    lat_cells, lon_cells = dims

    def write(west, east):
        for i in range(lat_cells):
            row = i * lon_cells
            for (ref, skip), place in ((west, row), (east, row + lon_cells - reach)):
                ref[skip + i * reach:skip + (i + 1) * reach] = own[place:place + reach]

    to_x, to_s = outs
    pl.when(even("lon"))(lambda: write(to_s, to_x))
    pl.when(jnp.logical_not(even("lon")))(lambda: write(to_x, to_s))


def pack_corners(strips, outs, reach, dims):
    lat_cells, lon_cells = dims
    from_a, from_b = strips
    to_x, to_s = outs
    plan, _ = side_rows(reach, lat_cells)

    def write(north, south, west, east):
        for i, (first, count) in enumerate(plan):
            if reach <= i < reach + lat_cells or not count:
                continue
            ref, skip = north if i < reach else south
            row = skip + (i if i < reach else i - reach - lat_cells) * lon_cells
            for (out, base), place in ((west, row), (east, row + lon_cells - count)):
                out[base + first:base + first + count] = ref[place:place + count]

    for even_lat in (True, False):
        for even_lon in (True, False):
            poles = (from_b, from_a) if even_lat else (from_a, from_b)
            edges = (to_s, to_x) if even_lon else (to_x, to_s)
            pl.when((even("lat") == even_lat) & (even("lon") == even_lon))(
                functools.partial(write, *poles, *edges))


def cells_at(rows, slots):
    return jnp.concatenate([rows[0:1], rows[1:2, :slots - LANES]], axis=1).astype(jnp.int32)


def add_into(cells, parts, count):
    hot = lax.broadcasted_iota(jnp.int32, (count, cells.shape[1]), 0) == cells
    both = jnp.dot(hot.astype(jnp.bfloat16), jnp.concatenate(parts, axis=1),
                   preferred_element_type=jnp.float32)
    return both[:, :LANES] + (both[:, LANES:2 * LANES] + both[:, 2 * LANES:])


def scatter_kernel(dims, slots, reach, message, cells, own, *outs):
    own[...] = add_into(cells[...], split3(message[0:slots]), dims[0] * dims[1])
    if outs:
        pack_own_sides(own, [(out, 0) for out in outs], reach, dims)


def sides_kernel(dims, slots, reach, joined, *refs):
    lat_cells, lon_cells = dims
    own, refs = (refs[0], refs[1:]) if joined else (None, refs)
    from_a, from_b, cells_a, cells_b, strip_a, strip_b, to_x, to_s = refs
    skip = (lat_cells - reach) * lon_cells
    for message, cells, strip, north in (
        (from_a, cells_a, strip_a, jnp.logical_not(even("lat"))),
        (from_b, cells_b, strip_b, even("lat")),
    ):
        at = cells_at(cells, slots) - jnp.where(north, skip, 0)
        strip[...] = add_into(at, split3(message[0:slots]), reach * lon_cells)
    base = 0
    if joined:
        pack_own_sides(own, ((to_x, 0), (to_s, 0)), reach, dims)
        base = side_rows(reach, lat_cells)[1][0]
    pack_corners(((strip_a, 0), (strip_b, 0)), ((to_x, base), (to_s, base)), reach, dims)


def face_places(lat_cells):
    (own_h, corner_h), (own_v, _) = (side_rows(reach, lat_cells)[1] for reach in (FRAME, REACH))
    return (0, own_h + own_v), (own_h, own_h + own_v + corner_h)


def face_sides_kernel(dims, root_h, root_v, from_a, from_b, to_x, to_s):
    skip = 0
    for root, reach, (own, corner) in zip((root_h, root_v), (FRAME, REACH), face_places(dims[0])):
        pack_own_sides(root, ((to_x, own), (to_s, own)), reach, dims)
        pack_corners(((from_a, skip), (from_b, skip)), ((to_x, corner), (to_s, corner)), reach, dims)
        skip += reach * dims[1]


def start_kernel(dims, *refs):
    lat_cells, lon_cells = dims
    sources, (first, root_h, root_v, to_a, to_b), refs = refs[:5], refs[5:10], refs[10:]
    (innovation, obs_weight, block_list, kappa_h, kappa_v), sems = refs[:5], refs[5]
    loads = copies(list(zip(sources, refs[:5])), sems)
    obs, own = innovation.shape
    slots = block_list.shape[1]
    for load in loads:
        load.wait()
    weight = obs_weight[...]
    first[0:obs, 0:own] = weight * innovation[...]
    first[0:obs, own:2 * own] = weight
    places = block_list[...].astype(jnp.float32)
    tail = to_a.shape[0] - 8
    cells = jnp.clip(places[1:2], 0.0, lat_cells * lon_cells - 1.0)
    for ref, base, row in ((first, obs, places[0:1]), (to_a, tail, cells), (to_b, tail, cells)):
        ref[base:base + 8] = jnp.full((8, LANES), -1.0, jnp.float32)
        ref[base:base + 1] = row[:, :LANES]
        ref[base + 1:base + 2, 0:slots - LANES] = row[:, LANES:]
    root_h[...] = jnp.sqrt(kappa_h[...])
    root_v[...] = jnp.sqrt(kappa_v[...])

    def write(south, north):
        skip = 0
        for ref, reach in ((root_h, FRAME), (root_v, REACH)):
            count = reach * lon_cells
            north[skip:skip + count] = ref[0:count]
            south[skip:skip + count] = ref[lat_cells * lon_cells - count:]
            skip += count

    pl.when(even("lat"))(lambda: write(to_a, to_b))
    pl.when(jnp.logical_not(even("lat")))(lambda: write(to_b, to_a))


def faces_kernel(dims, root_h, root_v, from_a, from_b, from_x, from_s, *refs):
    lat_cells, lon_cells = dims
    face_lat, face_lon, keep, up, down, natural, buf = refs
    rows = lat_cells + 2 * FRAME
    width = buf.shape[1]
    places = face_places(lat_cells)
    place_halos(
        natural, root_h, ((from_a, 0), (from_b, 0)),
        [[(ref, place) for place in places[0]] for ref in (from_x, from_s)], FRAME, dims,
    )

    def clear(first):
        def body(i, c):
            natural[first + i] = jnp.zeros((width, LANES), jnp.float32)
            return c
        lax.fori_loop(0, FRAME, body, 0)

    lat = lax.axis_index("lat")
    pl.when(lat == 0)(lambda: clear(0))
    pl.when(lat == lax.axis_size("lat") - 1)(lambda: clear(FRAME + lat_cells))

    to_strided(natural, buf, range(rows))
    buf[rows] = jnp.zeros((width, LANES), jnp.float32)

    def lateral(step, c):
        for k in range(4):
            i = 4 * step + k
            here = [buf[i, 8 * v:8 * v + 8] for v in range(width // 8)]
            face_lat[i] = buf[i] * buf[i + 1]
            for v, (w, e) in enumerate(zip(here, eastern(here))):
                face_lon[i, 8 * v:8 * v + 8] = w * e
        return c

    lax.fori_loop(0, rows // 4, lateral, 0)
    skip = FRAME * lon_cells
    place_halos(
        natural, root_v, ((from_a, skip), (from_b, skip)),
        [[(ref, place) for place in places[1]] for ref in (from_x, from_s)], REACH, dims,
    )
    to_strided(natural, buf, range(FRAME - REACH, rows - FRAME + REACH))
    top = lax.broadcasted_iota(jnp.int32, (width, LANES), 1) == LANES - 1

    def vertical(step, c):
        at = [4 * step + k for k in range(4)]
        here = [buf[FRAME - REACH + i] for i in at]
        face = [jnp.where(top, 0.0, v * pltpu.roll(v, LANES - 1, 1)) for v in here]
        below = [pltpu.roll(v, 1, 1) for v in face]
        for i, f, g in zip(at, face, below):
            up[i] = f
            down[i] = g
            keep[i] = 1.0 - (f + g)
        return c

    lax.fori_loop(0, (lat_cells + 2 * REACH) // 4, vertical, 0)


def observe(cells, jac, field, out):
    slots, obs, _ = jac.shape
    lane = lax.broadcasted_iota(jnp.int32, (obs, LANES), 1)

    ones = jnp.ones((2 * LANES, LANES), jnp.bfloat16)
    group = 64

    def part(first, count):
        def body(step, acc):
            at = [first + step * group + k for k in range(group)]
            prods = [jac[slot] * field[pl.ds(cells[slot], 1), :] for slot in at]
            half = jnp.concatenate(prods[:group // 2], axis=0)
            high = half.astype(jnp.bfloat16)
            low = (half - high.astype(jnp.float32)).astype(jnp.bfloat16)
            sums = jnp.dot(jnp.concatenate([high, low], axis=1), ones, preferred_element_type=jnp.float32)
            for k in range(group):
                if k < group // 2:
                    value = sums[obs * k:obs * k + obs]
                else:
                    value = jnp.sum(prods[k], axis=1, keepdims=True)
                acc = jnp.where(lane == step * group + k, value, acc)
            return acc
        return lax.fori_loop(0, count // group, body, jnp.zeros((obs, LANES), jnp.float32))

    out[0:obs] = part(0, LANES)
    rest = part(LANES, slots - LANES)
    out[obs:obs + obs // 2] = rest[:obs // 2] + pltpu.roll(rest[obs // 2:], LANES // 2, 1)


def adjoint_kernel(first_call, parts, *refs):
    pieces, refs = refs[:2 * parts], refs[2 * parts:]
    if first_call:
        own_hot, jac_hbm, out, weight, band, jac, taken, sems = refs
    else:
        row_hot, weight, own_hot, jac, out, taken = refs
    slots, obs, _ = jac.shape
    group = 64
    groups = slots // group

    def chunk(g):
        place = pl.ds(g * group, group)
        return pltpu.make_async_copy(jac_hbm.at[place], jac.at[place], sems.at[g])

    for g in range(groups if first_call else 0):
        chunk(g).start()
    if first_call:
        own = weight.shape[1] // (2 * parts)
        for d, piece in enumerate(pieces):
            band[:, d * own:d * own + own] = piece[0:obs, 0:own]
            weight[:, d * own:d * own + own] = piece[0:obs, own:2 * own]
        weighted = band[...]
    else:
        total = None
        scal = None
        for d, piece in enumerate(pieces):
            fold = piece[obs:obs + obs // 2]
            rest = jnp.concatenate([fold, pltpu.roll(fold, LANES // 2, 1)], axis=0)
            values = jnp.concatenate([piece[0:obs], rest], axis=1)
            stack = jnp.concatenate(split3(values), axis=0)
            prod = jnp.dot(stack, row_hot[d], preferred_element_type=jnp.float32)
            total = prod if total is None else total + prod
            tail = piece[obs + obs // 2:obs + obs // 2 + 8]
            scal = tail if scal is None else scal + tail
        total = total[:obs] + (total[obs:2 * obs] + total[2 * obs:])
        weighted = weight[...] * total
        out[slots:slots + 8] = scal
        out[slots + 8:slots + 16] = fold_sum(weighted * total)
    stack = jnp.concatenate(split3(weighted), axis=0)
    picked = jnp.dot(stack, own_hot[...], preferred_element_type=jnp.float32)
    picked = picked[:obs] + (picked[obs:2 * obs] + picked[2 * obs:])
    taken[0] = picked[:, :LANES]
    taken[1] = picked[:, LANES:]

    ones = jnp.ones((2 * LANES, LANES), jnp.bfloat16)
    lane = lax.broadcasted_iota(jnp.int32, (obs, LANES), 1)

    def body(g, c):
        if first_call:
            chunk(g).wait()
        per = LANES // group
        base = (g % per) * group
        values = taken[g // per]
        high = values.astype(jnp.bfloat16)
        low = (values - high.astype(jnp.float32)).astype(jnp.bfloat16)
        none = jnp.zeros_like(high)
        stack = jnp.concatenate([
            jnp.concatenate([jnp.where(lane == base + k, high, none),
                             jnp.where(lane == base + k, low, none)], axis=1)
            for k in range(group // 2)
        ], axis=0)
        spread = jnp.dot(stack, ones, preferred_element_type=jnp.float32)
        values = pltpu.roll(values, LANES - base, 1)
        for k in range(group):
            slot = g * group + k
            wide = spread[obs * k:obs * k + obs] if k < group // 2 else values[:, k:k + 1]
            out[pl.ds(slot, 1), :] = jnp.sum(jac[slot] * wide, axis=0, keepdims=True)
        return c

    lax.fori_loop(0, groups, body, 0)


def spread_kernel(dims, first_call, *refs):
    lat_cells, lon_cells = dims
    counts, cells, own, from_a, from_b = refs[:5]
    if first_call:
        (from_x, from_s), refs = refs[5:7], refs[7:]
        corner = side_rows(FRAME, lat_cells)[1][0]
        sides = [[(ref, 0), (ref, corner)] for ref in (from_x, from_s)]
    else:
        (own_x, own_s, corner_x, corner_s), refs = refs[5:9], refs[9:]
        sides = [[(own_x, 0), (corner_x, 0)], [(own_s, 0), (corner_s, 0)]]
    if not first_call:
        scal, refs = refs[0], refs[1:]
    if first_call:
        faces, jac_hbm, refs = refs[:5], refs[5], refs[6:]
        one_hbm, two_hbm, message, jac = refs[:4]
        refs = refs[4:]
    else:
        jac, faces, grad_hbm, spread_hbm = refs[0], refs[1:6], refs[6], refs[7]
        one_hbm, two_hbm, message = refs[8:11]
        refs = refs[11:]
    face_lat, face_lon, keep, up, down = faces
    one, two, grad, natural, buf, mid, sems = refs
    if first_call:
        loads = copies([(jac_hbm, jac)], sems)
    else:
        loads = copies([(grad_hbm, grad), (spread_hbm, two)], sems)
    nh, nv = counts[0], counts[1]
    rows = lat_cells + 2 * FRAME
    place_halos(
        natural, own, ((from_a, 0), (from_b, 0)), sides, FRAME, dims
    )
    to_strided(natural, buf, range(rows))
    lateral_passes(buf, face_lat, face_lon, nh, 0, nh)
    border = FRAME - REACH
    tall = lat_cells + 2 * REACH
    vertical = functools.partial(
        vertical_passes, buf, keep, up, down, border, border + tall, border, nv
    )
    vertical()

    block = range(FRAME, FRAME + lat_cells)
    to_natural(buf, mid, block, FRAME)
    vertical()
    lateral_passes(buf, face_lat, face_lon, nh, nh, 2 * nh)
    to_natural(buf, natural, block)
    cols = slice(FRAME, FRAME + lon_cells)
    if not first_call:
        rr = jnp.sum(scal[0:8])
        alpha = rr / (rr + jnp.sum(scal[8:16]))
        for load in loads:
            load.wait()

    def finish(i, acc):
        place = pl.ds(pl.multiple_of(i * lon_cells, lon_cells), lon_cells)
        vector = mid[i, cols]
        after = natural[FRAME + i, cols]
        if first_call:
            one[place] = vector
            two[place] = after
        else:
            old = two[place]
            base = grad[place]
            applied = base + vector
            one[place] = applied
            two[place] = old - alpha * (old + after)
            vector = base - alpha * applied
        square = vector * vector
        for j in range(lon_cells // 8):
            acc = acc + square[8 * j:8 * j + 8]
        return acc

    norm = lax.fori_loop(0, lat_cells, finish, jnp.zeros((8, LANES), jnp.float32))
    stores = copies([(one, one_hbm), (two, two_hbm)], sems.at[pl.ds(2, 2)])
    if first_call:
        loads[0].wait()
    obs = jac.shape[1]
    observe(cells, jac, two, message)
    message[obs + obs // 2:] = norm
    for store in stores:
        store.wait()


def combine_kernel(scal0, scal1, grad, spread, image, spread_next, increment, base, step):
    rr0 = jnp.sum(scal0[0:8])
    alpha0 = rr0 / (rr0 + jnp.sum(scal0[8:16]))
    rr1 = jnp.sum(scal1[0:8])
    beta = rr1 / rr0
    alpha1 = rr1 / ((rr1 + jnp.sum(scal1[8:16])) - beta * (rr1 / alpha0))
    step[...] = jnp.full(step.shape, 1.0, jnp.float32) * alpha1
    applied = image[...]
    rest = grad[...] - alpha0 * applied
    base[...] = rest - alpha1 * (rest + beta * applied)
    old = spread[...]
    increment[...] = alpha0 * old + alpha1 * (spread_next[...] + beta * old)


def final_kernel(dims, *refs):
    lat_cells, lon_cells = dims
    counts, own, from_a, from_b, own_x, own_s, corner_x, corner_s, base, alpha = refs[:10]
    face_lat, face_lon, keep, up, down, residual, natural, buf = refs[10:]
    nh, nv = counts[0], counts[1]
    place_halos(
        natural, own, ((from_a, 0), (from_b, 0)),
        (((own_x, 0), (corner_x, 0)), ((own_s, 0), (corner_s, 0))), REACH, dims,
    )
    to_strided(natural, buf, range(FRAME - REACH, FRAME + lat_cells + REACH))
    lateral_passes(buf, face_lat, face_lon, nh, nh, 2 * nh)
    vertical_passes(
        buf, keep, up, down, FRAME, FRAME + lat_cells, FRAME - REACH, nv
    )
    to_natural(buf, natural, range(FRAME, FRAME + lat_cells))
    cols = slice(FRAME, FRAME + lon_cells)
    step = jnp.concatenate([alpha[...]] * (lon_cells // 8), axis=0)
    for i in range(lat_cells):
        place = slice(i * lon_cells, i * lon_cells + lon_cells)
        residual[place] = base[place] - step * natural[FRAME + i, cols]


def local(innovation, obs_weight, jacobian, block_list, pass_counts, kappa_h, kappa_v):
    lat_cells, lon_cells, levels = kappa_h.shape
    cells_n = lat_cells * lon_cells
    slots, obs, _ = jacobian.shape
    own_rows = innovation.shape[1]
    n_lat, n_lon = lax.axis_size("lat"), lax.axis_size("lon")
    parts = n_lon // 2
    lon = lax.axis_index("lon")
    f32 = jnp.float32

    def swap(n, k):
        return [(i, i ^ k) for i in range(n)]

    def odd_pairs(n):
        return [(i, (i + 1) % n if i % 2 else (i - 1) % n) for i in range(n)]

    inner_pairs = [(0, 0), (n_lat - 1, n_lat - 1)] + [
        pair for i in range(1, n_lat - 1, 2) for pair in ((i, i + 1), (i + 1, i))]

    def send(x, axis, pairs):
        return lax.ppermute(x, axis, pairs)

    def gather_band(x):
        near = [x] + [send(x, "lon", swap(n_lon, 2 * k)) for k in range(1, parts)]
        return near + [send(piece, "lon", swap(n_lon, 1)) for piece in near]

    def lon_send(to_x, to_s):
        return send(to_x, "lon", swap(n_lon, 1)), send(to_s, "lon", odd_pairs(n_lon))

    def lat_send(to_a, to_b, pairs):
        return send(to_a, "lat", swap(n_lat, 1)), send(to_b, "lat", pairs)

    def lat_sum(tail, from_a, from_b):
        if n_lat != 4:
            return lax.psum(tail, "lat")
        return (tail + send(tail, "lat", swap(n_lat, 2))) + (from_a[slots:] + from_b[slots:])

    def side_shapes(reach):
        return [shape(size, levels) for size in side_rows(reach, lat_cells)[1]]

    def joined_shape(*reaches):
        return shape(sum(sum(side_rows(reach, lat_cells)[1]) for reach in reaches), levels)

    def scatter(message, reach):
        side = side_shapes(reach)[0]
        own, to_x, to_s = call(
            functools.partial(scatter_kernel, dims, slots, reach), "scatter", (field, side, side),
            (message, cells))
        return own, lon_send(to_x, to_s)

    def sides_of(from_a, from_b, reach, joined=()):
        side = side_shapes(reach)[1]
        if joined:
            side = joined_shape(reach)
        strip = shape(reach * lon_cells, levels)
        strip_a, strip_b, to_x, to_s = call(
            functools.partial(sides_kernel, dims, slots, reach, bool(joined)), "sides",
            (strip, strip, side, side), (*joined, from_a, from_b, *cells_near))
        return (strip_a, strip_b), lon_send(to_x, to_s)

    def halo(message, reach):
        from_a, from_b = lat_send(message, message, odd_pairs(n_lat))
        own, own_sides = scatter(message, reach)
        strips, corners = sides_of(from_a, from_b, reach)
        return (own, *strips, *own_sides, *corners), lat_sum(message[slots:], from_a, from_b)

    vmem = pl.BlockSpec(memory_space=pltpu.VMEM)
    smem = pl.BlockSpec(memory_space=pltpu.SMEM)
    hbm = pl.BlockSpec(memory_space=pl.ANY)
    params = pltpu.CompilerParams(vmem_limit_bytes=VMEM_LIMIT)
    shape = lambda *dims: jax.ShapeDtypeStruct(dims, f32)
    scratch = lambda *dims: pltpu.VMEM(dims, f32)
    rows_h = lat_cells + 2 * FRAME
    rows_v = lat_cells + 2 * REACH
    width = lon_cells + 2 * FRAME
    band_rows = n_lon * own_rows
    dims = (lat_cells, lon_cells)
    field = shape(cells_n, levels)
    msg = shape(obs + obs // 2 + 8, LANES)
    wide, tall = shape(rows_h, width, levels), shape(rows_v, width, levels)
    wide_vmem, tall_vmem = scratch(rows_h, width, levels), scratch(rows_v, width, levels)
    field_vmem = scratch(cells_n, levels)
    jac_vmem = scratch(slots, obs, levels)
    faces_vmem = [wide_vmem] * 2 + [tall_vmem] * 3
    sems = lambda count: pltpu.SemaphoreType.DMA((count,))

    def call(kernel, name, outs, ins, scalars=0, far_in=(), far_out=False, scratches=(), params=params):
        out_specs = jax.tree.map(lambda _: vmem, outs)
        if far_out:
            out_specs = (hbm,) * far_out + out_specs[far_out:]
        specs = [smem] * scalars + [vmem] * (len(ins) - scalars) + [hbm] * len(far_in)
        return pl.pallas_call(
            kernel, out_shape=outs, in_specs=specs, out_specs=out_specs,
            scratch_shapes=list(scratches), compiler_params=params, name=name,
        )(*ins, *far_in)

    strip = shape((FRAME + REACH) * lon_cells + 8, levels)
    start_in = (innovation, obs_weight, block_list,
                kappa_h.reshape(cells_n, levels), kappa_v.reshape(cells_n, levels))
    first, root_h, root_v, to_a, to_b = call(
        functools.partial(start_kernel, dims), "start", (shape(obs + 8, LANES), field, field, strip, strip),
        (), far_in=start_in, scratches=[pltpu.VMEM(v.shape, v.dtype) for v in start_in] + [sems(5)],
        params=pltpu.CompilerParams(vmem_limit_bytes=START_LIMIT))
    k_strips = lat_send(to_a, to_b, inner_pairs)
    band = gather_band(first)
    cells_near = [v[(FRAME + REACH) * lon_cells:] for v in k_strips]

    def place_of(row):
        row = row.astype(jnp.int32)
        key = (row // own_rows) ^ lon
        at = (key // 2 + parts * (key % 2)) * own_rows + row % own_rows
        return jnp.where((row >= 0) & (row < band_rows), at, -1)

    all_at = place_of(jnp.stack([piece[obs:obs + 2] for piece in band]).reshape(n_lon, 2 * LANES))
    row_iota = jnp.arange(band_rows, dtype=jnp.int32)
    row_hot = (all_at[:, :, None] == row_iota[None, None, :]).astype(jnp.bfloat16)
    own_at = jnp.pad(place_of(block_list[0]), (0, 2 * LANES - slots), constant_values=-1)
    own_hot = (row_iota[:, None] == own_at[None, :]).astype(jnp.bfloat16)
    cells = jnp.clip(block_list[1:], 0, cells_n - 1)
    cells_flat = cells.reshape(slots)

    adj_scratch = [jac_vmem, scratch(2, obs, LANES), sems(slots // 64)]
    message, weight = call(
        functools.partial(adjoint_kernel, True, parts), "adjoint_first",
        (shape(slots, levels), shape(obs, band_rows)), (*band, own_hot), far_in=(jacobian,),
        scratches=[scratch(obs, band_rows)] + adj_scratch)

    from_a, from_b = lat_send(message, message, inner_pairs)
    own = call(functools.partial(scatter_kernel, dims, slots, FRAME), "scatter", field, (message, cells))
    side = joined_shape(FRAME, REACH)
    k_messages = call(functools.partial(face_sides_kernel, dims), "face_sides", (side, side),
                      (root_h, root_v, *k_strips))
    k_sides = lon_send(*k_messages)
    k_messages, from_a, from_b = lax.optimization_barrier((k_messages, from_a, from_b))
    strips, sides = sides_of(from_a, from_b, FRAME, (own,))
    halos = (own, *strips, *sides)
    faces = call(
        functools.partial(faces_kernel, dims), "faces", (wide, wide, tall, tall, tall),
        (root_h, root_v, *k_strips, *k_sides),
        scratches=[wide_vmem, scratch(rows_h + 1, width, levels)])
    spread_scratch = [field_vmem] * 3 + [
        wide_vmem, wide_vmem, scratch(lat_cells, width, levels), sems(4)]
    near_params = pltpu.CompilerParams(vmem_limit_bytes=NEAR_LIMIT)
    grad, spread, message, near_jac = call(
        functools.partial(spread_kernel, dims, True), "spread_first",
        (field, field, msg, shape(*jacobian.shape)),
        (pass_counts, cells_flat, *halos, *faces), 2, (jacobian,), 2, spread_scratch)

    def adjoint(message):
        return call(
            functools.partial(adjoint_kernel, False, parts), "adjoint_next",
            shape(slots + 16, levels), (*gather_band(message), row_hot, weight, own_hot, near_jac),
            scratches=[scratch(2, obs, LANES)], params=near_params)

    halos, scal0 = halo(adjoint(message), FRAME)
    image, spread_next, message = call(
        functools.partial(spread_kernel, dims, False), "spread_next", (field, field, msg),
        (pass_counts, cells_flat, *halos, scal0, near_jac, *faces), 2, (grad, spread), 2, spread_scratch,
        near_params)
    halos, scal1 = halo(adjoint(message), REACH)
    increment, base, step = call(
        combine_kernel, "combine", (field, field, shape(8, LANES)),
        (scal0, scal1, grad, spread, image, spread_next))
    residual = call(
        functools.partial(final_kernel, dims), "final", field,
        (pass_counts, *halos, base, step, *faces), 1, scratches=[wide_vmem, wide_vmem], params=near_params)
    block = (lat_cells, lon_cells, levels)
    return increment.reshape(block), residual.reshape(block)


def solution(mesh):
    return jax.shard_map(
        local,
        mesh=mesh,
        in_specs=(
            P(None, ("lat", "lon")),
            P(None, ("lat", "lon")),
            P(("lat", "lon"), None, None),
            P(None, ("lat", "lon")),
            P(),
            P("lat", "lon", None),
            P("lat", "lon", None),
        ),
        out_specs=(P("lat", "lon", None), P("lat", "lon", None)),
        check_vma=False,
    )
```

```python
import functools

import jax
import jax.numpy as jnp
from jax import lax
from jax.experimental import pallas as pl
from jax.experimental.pallas import tpu as pltpu
from jax.sharding import PartitionSpec as P

LANES = 128
VMEM_LIMIT = 40 * 1024 * 1024
NEAR_LIMIT = 32 * 1024 * 1024
FIRST_LIMIT = 48 * 1024 * 1024
START_LIMIT = 60 * 1024 * 1024
REACH = 6
FRAME = 2 * REACH


def split3(x):
    high = x.astype(jnp.bfloat16)
    rest = x - high.astype(jnp.float32)
    mid = rest.astype(jnp.bfloat16)
    low = (rest - mid.astype(jnp.float32)).astype(jnp.bfloat16)
    return high, mid, low


def fold_sum(x):
    total = None
    for i in range(x.shape[0] // 8):
        for j in range(x.shape[1] // LANES):
            tile = x[8 * i:8 * i + 8, LANES * j:LANES * j + LANES]
            total = tile if total is None else total + tile
    return total


def copies(pairs, sems):
    started = [pltpu.make_async_copy(src, dst, sems.at[i]) for i, (src, dst) in enumerate(pairs)]
    for copy in started:
        copy.start()
    return started


def to_strided(natural, buf, rows):
    count = natural.shape[1] // 8
    for i in rows:
        for v in range(count):
            buf[i, 8 * v:8 * v + 8] = natural[i, pl.ds(v, 8, stride=count)]


def to_natural(buf, natural, rows, skip=0):
    count = natural.shape[1] // 8
    for i in rows:
        for v in range(count):
            natural[i - skip, pl.ds(v, 8, stride=count)] = buf[i, 8 * v:8 * v + 8]


def eastern(tiles):
    return tiles[1:] + [pltpu.roll(tiles[0], 7, 0)]


def western(tiles):
    return [pltpu.roll(tiles[-1], 1, 0)] + tiles[:-1]


def lateral_pass(buf, face_lat, face_lon, first, last):
    def tiles(ref, row):
        return [ref[row, 8 * v:8 * v + 8] for v in range(buf.shape[1] // 8)]

    def advance(row, carry):
        current, flux_above = carry
        below = tiles(buf, row + 1)
        flux = [f * (b - w) for f, b, w in zip(tiles(face_lat, row), below, current)]
        side = [f * (e - w) for f, e, w in zip(tiles(face_lon, row), eastern(current), current)]
        for v, (w, f, g, e, h) in enumerate(zip(current, flux, flux_above, side, western(side))):
            buf[row, 8 * v:8 * v + 8] = w + ((f - g) + (e - h))
        return below, flux

    def six(step, carry):
        for k in range(6):
            carry = advance(first + 6 * step + k, carry)
        return carry

    def two(step, carry):
        for k in range(2):
            carry = advance(first + count // 6 * 6 + 2 * step + k, carry)
        return carry

    start = tiles(buf, first)
    flux = [f * (w - a) for f, w, a in zip(tiles(face_lat, first - 1), start, tiles(buf, first - 1))]
    count = last - first
    carry = lax.fori_loop(0, count // 6, six, (start, flux))
    lax.fori_loop(0, (count % 6) // 2, two, carry)


def lateral_passes(buf, face_lat, face_lon, nh, begin, end):
    rows, lost = buf.shape[0], FRAME - 2 * nh

    def body(p, c):
        lateral_pass(buf, face_lat, face_lon, lost + p, rows - lost - p)
        return c

    lax.fori_loop(begin + 1, end + 1, body, 0)


def shift_matrix():
    source = lax.broadcasted_iota(jnp.int32, (2 * LANES, 2 * LANES), 0) % LANES
    target = lax.broadcasted_iota(jnp.int32, (2 * LANES, 2 * LANES), 1)
    wanted = jnp.where(target < LANES, target + 1, target - LANES - 1)
    return (source == wanted).astype(jnp.bfloat16)


def vertical_passes(buf, keep, up, down, first, last, offset, nv):
    width = buf.shape[1]
    shifts = shift_matrix()
    at = list(range(first, last))
    half = (last - first) // 2

    def sweep(p, c):
        values = [buf[i] for i in at]
        stack = jnp.concatenate(values[:half], axis=0)
        high = stack.astype(jnp.bfloat16)
        low = (stack - high.astype(jnp.float32)).astype(jnp.bfloat16)
        moved = jnp.dot(jnp.concatenate([high, low], axis=1), shifts, preferred_element_type=jnp.float32)
        for n, (i, w) in enumerate(zip(at, values)):
            if n < half:
                here = moved[width * n:width * n + width]
                above, below = here[:, :LANES], here[:, LANES:]
            else:
                above, below = pltpu.roll(w, LANES - 1, 1), pltpu.roll(w, 1, 1)
            buf[i] = keep[i - offset] * w + (up[i - offset] * above + down[i - offset] * below)
        return c

    lax.fori_loop(0, nv, sweep, 0)


def side_rows(reach, lat_cells):
    plan, first = [], 0
    for i in range(lat_cells + 2 * reach):
        outside = max(reach - i, i - (reach + lat_cells - 1), 0)
        if outside:
            plan.append((first, reach - outside))
            first += reach - outside
        else:
            plan.append(((i - reach) * reach, reach))
    return plan, (lat_cells * reach, -(-first // 8) * 8)


def even(axis):
    return lax.axis_index(axis) % 2 == 0


def place_halos(buf, own, strips, sides, reach, dims):
    lat_cells, lon_cells = dims
    (from_a, skip_a), (from_b, skip_b) = strips
    from_x, from_s = sides
    base = FRAME - reach
    lat_even, lon_even = even("lat"), even("lon")
    south = FRAME + lat_cells
    row_a = jnp.where(lat_even, south, base)
    row_b = jnp.where(lat_even, base, south)
    cols = slice(FRAME, FRAME + lon_cells)
    for i in range(lat_cells):
        buf[FRAME + i, cols] = own[i * lon_cells:(i + 1) * lon_cells]
    for i in range(reach):
        place = i * lon_cells
        buf[row_a + i, cols] = from_a[skip_a + place:skip_a + place + lon_cells]
        buf[row_b + i, cols] = from_b[skip_b + place:skip_b + place + lon_cells]

    def put_sides(west, east):
        for i, (first, count) in enumerate(side_rows(reach, lat_cells)[0]):
            part = 0 if reach <= i < reach + lat_cells else 1
            for (ref, skip), place in ((west[part], FRAME - count), (east[part], FRAME + lon_cells)):
                if count:
                    buf[base + i, place:place + count] = ref[skip + first:skip + first + count]

    pl.when(lon_even)(lambda: put_sides(from_s, from_x))
    pl.when(jnp.logical_not(lon_even))(lambda: put_sides(from_x, from_s))


def pack_own_sides(own, outs, reach, dims):
    lat_cells, lon_cells = dims

    def write(west, east):
        for i in range(lat_cells):
            row = i * lon_cells
            for (ref, skip), place in ((west, row), (east, row + lon_cells - reach)):
                ref[skip + i * reach:skip + (i + 1) * reach] = own[place:place + reach]

    to_x, to_s = outs
    pl.when(even("lon"))(lambda: write(to_s, to_x))
    pl.when(jnp.logical_not(even("lon")))(lambda: write(to_x, to_s))


def pack_corners(strips, outs, reach, dims):
    lat_cells, lon_cells = dims
    from_a, from_b = strips
    to_x, to_s = outs
    plan, _ = side_rows(reach, lat_cells)

    def write(north, south, west, east):
        for i, (first, count) in enumerate(plan):
            if reach <= i < reach + lat_cells or not count:
                continue
            ref, skip = north if i < reach else south
            row = skip + (i if i < reach else i - reach - lat_cells) * lon_cells
            for (out, base), place in ((west, row), (east, row + lon_cells - count)):
                out[base + first:base + first + count] = ref[place:place + count]

    for even_lat in (True, False):
        for even_lon in (True, False):
            poles = (from_b, from_a) if even_lat else (from_a, from_b)
            edges = (to_s, to_x) if even_lon else (to_x, to_s)
            pl.when((even("lat") == even_lat) & (even("lon") == even_lon))(
                functools.partial(write, *poles, *edges))


def cells_at(rows, slots):
    return jnp.concatenate([rows[0:1], rows[1:2, :slots - LANES]], axis=1).astype(jnp.int32)


def add_into(cells, parts, count):
    hot = lax.broadcasted_iota(jnp.int32, (count, cells.shape[1]), 0) == cells
    both = jnp.dot(hot.astype(jnp.bfloat16), jnp.concatenate(parts, axis=1),
                   preferred_element_type=jnp.float32)
    return both[:, :LANES] + (both[:, LANES:2 * LANES] + both[:, 2 * LANES:])


def scatter_kernel(dims, slots, reach, message, cells, own, *outs):
    own[...] = add_into(cells[...], split3(message[0:slots]), dims[0] * dims[1])
    if outs:
        pack_own_sides(own, [(out, 0) for out in outs], reach, dims)


def sides_kernel(dims, slots, reach, joined, *refs):
    lat_cells, lon_cells = dims
    own, refs = (refs[0], refs[1:]) if joined else (None, refs)
    from_a, from_b, cells_a, cells_b, strip_a, strip_b, to_x, to_s = refs
    skip = (lat_cells - reach) * lon_cells
    for message, cells, strip, north in (
        (from_a, cells_a, strip_a, jnp.logical_not(even("lat"))),
        (from_b, cells_b, strip_b, even("lat")),
    ):
        at = cells_at(cells, slots) - jnp.where(north, skip, 0)
        strip[...] = add_into(at, split3(message[0:slots]), reach * lon_cells)
    base = 0
    if joined:
        pack_own_sides(own, ((to_x, 0), (to_s, 0)), reach, dims)
        base = side_rows(reach, lat_cells)[1][0]
    pack_corners(((strip_a, 0), (strip_b, 0)), ((to_x, base), (to_s, base)), reach, dims)


def face_places(lat_cells):
    (own_h, corner_h), (own_v, _) = (side_rows(reach, lat_cells)[1] for reach in (FRAME, REACH))
    return (0, own_h + own_v), (own_h, own_h + own_v + corner_h)


def face_sides_kernel(dims, root_h, root_v, from_a, from_b, to_x, to_s):
    skip = 0
    for root, reach, (own, corner) in zip((root_h, root_v), (FRAME, REACH), face_places(dims[0])):
        pack_own_sides(root, ((to_x, own), (to_s, own)), reach, dims)
        pack_corners(((from_a, skip), (from_b, skip)), ((to_x, corner), (to_s, corner)), reach, dims)
        skip += reach * dims[1]


def start_kernel(dims, *refs):
    lat_cells, lon_cells = dims
    sources, (first, root_h, root_v, to_a, to_b), refs = refs[:5], refs[5:10], refs[10:]
    (innovation, obs_weight, block_list, kappa_h, kappa_v), sems = refs[:5], refs[5]
    loads = copies(list(zip(sources, refs[:5])), sems)
    obs, own = innovation.shape
    slots = block_list.shape[1]
    for load in loads:
        load.wait()
    weight = obs_weight[...]
    first[0:obs, 0:own] = weight * innovation[...]
    first[0:obs, own:2 * own] = weight
    places = block_list[...].astype(jnp.float32)
    tail = to_a.shape[0] - 8
    cells = jnp.clip(places[1:2], 0.0, lat_cells * lon_cells - 1.0)
    for ref, base, row in ((first, obs, places[0:1]), (to_a, tail, cells), (to_b, tail, cells)):
        ref[base:base + 8] = jnp.full((8, LANES), -1.0, jnp.float32)
        ref[base:base + 1] = row[:, :LANES]
        ref[base + 1:base + 2, 0:slots - LANES] = row[:, LANES:]
    root_h[...] = jnp.sqrt(kappa_h[...])
    root_v[...] = jnp.sqrt(kappa_v[...])

    def write(south, north):
        skip = 0
        for ref, reach in ((root_h, FRAME), (root_v, REACH)):
            count = reach * lon_cells
            north[skip:skip + count] = ref[0:count]
            south[skip:skip + count] = ref[lat_cells * lon_cells - count:]
            skip += count

    pl.when(even("lat"))(lambda: write(to_a, to_b))
    pl.when(jnp.logical_not(even("lat")))(lambda: write(to_b, to_a))


def faces_kernel(dims, root_h, root_v, from_a, from_b, from_x, from_s, *refs):
    lat_cells, lon_cells = dims
    face_lat, face_lon, keep, up, down, natural, buf = refs
    rows = lat_cells + 2 * FRAME
    width = buf.shape[1]
    places = face_places(lat_cells)
    place_halos(
        natural, root_h, ((from_a, 0), (from_b, 0)),
        [[(ref, place) for place in places[0]] for ref in (from_x, from_s)], FRAME, dims,
    )

    def clear(first):
        def body(i, c):
            natural[first + i] = jnp.zeros((width, LANES), jnp.float32)
            return c
        lax.fori_loop(0, FRAME, body, 0)

    lat = lax.axis_index("lat")
    pl.when(lat == 0)(lambda: clear(0))
    pl.when(lat == lax.axis_size("lat") - 1)(lambda: clear(FRAME + lat_cells))

    to_strided(natural, buf, range(rows))
    buf[rows] = jnp.zeros((width, LANES), jnp.float32)

    def lateral(step, c):
        for k in range(4):
            i = 4 * step + k
            here = [buf[i, 8 * v:8 * v + 8] for v in range(width // 8)]
            face_lat[i] = buf[i] * buf[i + 1]
            for v, (w, e) in enumerate(zip(here, eastern(here))):
                face_lon[i, 8 * v:8 * v + 8] = w * e
        return c

    lax.fori_loop(0, rows // 4, lateral, 0)
    skip = FRAME * lon_cells
    place_halos(
        natural, root_v, ((from_a, skip), (from_b, skip)),
        [[(ref, place) for place in places[1]] for ref in (from_x, from_s)], REACH, dims,
    )
    to_strided(natural, buf, range(FRAME - REACH, rows - FRAME + REACH))
    top = lax.broadcasted_iota(jnp.int32, (width, LANES), 1) == LANES - 1

    def vertical(step, c):
        at = [4 * step + k for k in range(4)]
        here = [buf[FRAME - REACH + i] for i in at]
        face = [jnp.where(top, 0.0, v * pltpu.roll(v, LANES - 1, 1)) for v in here]
        below = [pltpu.roll(v, 1, 1) for v in face]
        for i, f, g in zip(at, face, below):
            up[i] = f
            down[i] = g
            keep[i] = 1.0 - (f + g)
        return c

    lax.fori_loop(0, (lat_cells + 2 * REACH) // 4, vertical, 0)


def observe(cells, jac, field, out):
    slots, obs, _ = jac.shape
    lane = lax.broadcasted_iota(jnp.int32, (obs, LANES), 1)

    ones = jnp.ones((2 * LANES, LANES), jnp.bfloat16)
    group = 64

    def part(first, count):
        def body(step, acc):
            at = [first + step * group + k for k in range(group)]
            prods = [jac[slot] * field[pl.ds(cells[slot], 1), :] for slot in at]
            half = jnp.concatenate(prods[:group // 2], axis=0)
            high = half.astype(jnp.bfloat16)
            low = (half - high.astype(jnp.float32)).astype(jnp.bfloat16)
            sums = jnp.dot(jnp.concatenate([high, low], axis=1), ones, preferred_element_type=jnp.float32)
            for k in range(group):
                if k < group // 2:
                    value = sums[obs * k:obs * k + obs]
                else:
                    value = jnp.sum(prods[k], axis=1, keepdims=True)
                acc = jnp.where(lane == step * group + k, value, acc)
            return acc
        return lax.fori_loop(0, count // group, body, jnp.zeros((obs, LANES), jnp.float32))

    out[0:obs] = part(0, LANES)
    rest = part(LANES, slots - LANES)
    out[obs:obs + obs // 2] = rest[:obs // 2] + pltpu.roll(rest[obs // 2:], LANES // 2, 1)


def adjoint_kernel(first_call, parts, *refs):
    pieces, refs = refs[:2 * parts], refs[2 * parts:]
    if first_call:
        own_hot, jac_hbm, out, weight, band, jac, taken, sems = refs
    else:
        row_hot, weight, own_hot, jac, out, taken = refs
    slots, obs, _ = jac.shape
    group = 64
    groups = slots // group

    def chunk(g):
        place = pl.ds(g * group, group)
        return pltpu.make_async_copy(jac_hbm.at[place], jac.at[place], sems.at[g])

    for g in range(groups if first_call else 0):
        chunk(g).start()
    if first_call:
        own = weight.shape[1] // (2 * parts)
        for d, piece in enumerate(pieces):
            band[:, d * own:d * own + own] = piece[0:obs, 0:own]
            weight[:, d * own:d * own + own] = piece[0:obs, own:2 * own]
        weighted = band[...]
    else:
        total = None
        scal = None
        for d, piece in enumerate(pieces):
            fold = piece[obs:obs + obs // 2]
            rest = jnp.concatenate([fold, pltpu.roll(fold, LANES // 2, 1)], axis=0)
            values = jnp.concatenate([piece[0:obs], rest], axis=1)
            stack = jnp.concatenate(split3(values), axis=0)
            prod = jnp.dot(stack, row_hot[d], preferred_element_type=jnp.float32)
            total = prod if total is None else total + prod
            tail = piece[obs + obs // 2:obs + obs // 2 + 8]
            scal = tail if scal is None else scal + tail
        total = total[:obs] + (total[obs:2 * obs] + total[2 * obs:])
        weighted = weight[...] * total
        out[slots:slots + 8] = scal
        out[slots + 8:slots + 16] = fold_sum(weighted * total)
    stack = jnp.concatenate(split3(weighted), axis=0)
    picked = jnp.dot(stack, own_hot[...], preferred_element_type=jnp.float32)
    picked = picked[:obs] + (picked[obs:2 * obs] + picked[2 * obs:])
    taken[0] = picked[:, :LANES]
    taken[1] = picked[:, LANES:]

    ones = jnp.ones((2 * LANES, LANES), jnp.bfloat16)
    lane = lax.broadcasted_iota(jnp.int32, (obs, LANES), 1)

    def body(g, c):
        if first_call:
            chunk(g).wait()
        per = LANES // group
        base = (g % per) * group
        values = taken[g // per]
        high = values.astype(jnp.bfloat16)
        low = (values - high.astype(jnp.float32)).astype(jnp.bfloat16)
        none = jnp.zeros_like(high)
        stack = jnp.concatenate([
            jnp.concatenate([jnp.where(lane == base + k, high, none),
                             jnp.where(lane == base + k, low, none)], axis=1)
            for k in range(group // 2)
        ], axis=0)
        spread = jnp.dot(stack, ones, preferred_element_type=jnp.float32)
        values = pltpu.roll(values, LANES - base, 1)
        for k in range(group):
            slot = g * group + k
            wide = spread[obs * k:obs * k + obs] if k < group // 2 else values[:, k:k + 1]
            out[pl.ds(slot, 1), :] = jnp.sum(jac[slot] * wide, axis=0, keepdims=True)
        return c

    lax.fori_loop(0, groups, body, 0)


def spread_kernel(dims, first_call, *refs):
    lat_cells, lon_cells = dims
    counts, cells, own, from_a, from_b = refs[:5]
    if first_call:
        (from_x, from_s), refs = refs[5:7], refs[7:]
        corner = side_rows(FRAME, lat_cells)[1][0]
        sides = [[(ref, 0), (ref, corner)] for ref in (from_x, from_s)]
    else:
        (own_x, own_s, corner_x, corner_s), refs = refs[5:9], refs[9:]
        sides = [[(own_x, 0), (corner_x, 0)], [(own_s, 0), (corner_s, 0)]]
    if not first_call:
        scal, refs = refs[0], refs[1:]
    if first_call:
        faces, jac_hbm, refs = refs[:5], refs[5], refs[6:]
        one_hbm, two_hbm, message, jac = refs[:4]
        refs = refs[4:]
    else:
        jac, faces, grad_hbm, spread_hbm = refs[0], refs[1:6], refs[6], refs[7]
        one_hbm, two_hbm, message = refs[8:11]
        refs = refs[11:]
    face_lat, face_lon, keep, up, down = faces
    one, two, grad, natural, buf, mid, sems = refs
    if first_call:
        loads = copies([(jac_hbm, jac)], sems)
    else:
        loads = copies([(grad_hbm, grad), (spread_hbm, two)], sems)
    nh, nv = counts[0], counts[1]
    rows = lat_cells + 2 * FRAME
    place_halos(
        natural, own, ((from_a, 0), (from_b, 0)), sides, FRAME, dims
    )
    to_strided(natural, buf, range(rows))
    lateral_passes(buf, face_lat, face_lon, nh, 0, nh)
    border = FRAME - REACH
    tall = lat_cells + 2 * REACH
    vertical = functools.partial(
        vertical_passes, buf, keep, up, down, border, border + tall, border, nv
    )
    vertical()

    block = range(FRAME, FRAME + lat_cells)
    to_natural(buf, mid, block, FRAME)
    vertical()
    lateral_passes(buf, face_lat, face_lon, nh, nh, 2 * nh)
    to_natural(buf, natural, block)
    cols = slice(FRAME, FRAME + lon_cells)
    if not first_call:
        rr = jnp.sum(scal[0:8])
        alpha = rr / (rr + jnp.sum(scal[8:16]))
        for load in loads:
            load.wait()

    norm = jnp.zeros((8, LANES), jnp.float32)
    for i in range(lat_cells):
        place = slice(i * lon_cells, (i + 1) * lon_cells)
        vector = mid[i, cols]
        after = natural[FRAME + i, cols]
        if first_call:
            one[place] = vector
            two[place] = after
        else:
            old = two[place]
            base = grad[place]
            applied = base + vector
            one[place] = applied
            two[place] = old - alpha * (old + after)
            vector = base - alpha * applied
        square = vector * vector
        for j in range(lon_cells // 8):
            norm = norm + square[8 * j:8 * j + 8]
    stores = copies([(one, one_hbm), (two, two_hbm)], sems.at[pl.ds(2, 2)])
    if first_call:
        loads[0].wait()
    obs = jac.shape[1]
    observe(cells, jac, two, message)
    message[obs + obs // 2:] = norm
    for store in stores:
        store.wait()


def combine_kernel(scal0, scal1, grad, spread, image, spread_next, increment, base, step):
    rr0 = jnp.sum(scal0[0:8])
    alpha0 = rr0 / (rr0 + jnp.sum(scal0[8:16]))
    rr1 = jnp.sum(scal1[0:8])
    beta = rr1 / rr0
    alpha1 = rr1 / ((rr1 + jnp.sum(scal1[8:16])) - beta * (rr1 / alpha0))
    step[...] = jnp.full(step.shape, 1.0, jnp.float32) * alpha1
    applied = image[...]
    rest = grad[...] - alpha0 * applied
    base[...] = rest - alpha1 * (rest + beta * applied)
    old = spread[...]
    increment[...] = alpha0 * old + alpha1 * (spread_next[...] + beta * old)


def final_kernel(dims, *refs):
    lat_cells, lon_cells = dims
    counts, own, from_a, from_b, own_x, own_s, corner_x, corner_s, base, alpha = refs[:10]
    face_lat, face_lon, keep, up, down, residual, natural, buf = refs[10:]
    nh, nv = counts[0], counts[1]
    place_halos(
        natural, own, ((from_a, 0), (from_b, 0)),
        (((own_x, 0), (corner_x, 0)), ((own_s, 0), (corner_s, 0))), REACH, dims,
    )
    to_strided(natural, buf, range(FRAME - REACH, FRAME + lat_cells + REACH))
    lateral_passes(buf, face_lat, face_lon, nh, nh, 2 * nh)
    vertical_passes(
        buf, keep, up, down, FRAME, FRAME + lat_cells, FRAME - REACH, nv
    )
    to_natural(buf, natural, range(FRAME, FRAME + lat_cells))
    cols = slice(FRAME, FRAME + lon_cells)
    step = jnp.concatenate([alpha[...]] * (lon_cells // 8), axis=0)
    for i in range(lat_cells):
        place = slice(i * lon_cells, i * lon_cells + lon_cells)
        residual[place] = base[place] - step * natural[FRAME + i, cols]


def local(innovation, obs_weight, jacobian, block_list, pass_counts, kappa_h, kappa_v):
    lat_cells, lon_cells, levels = kappa_h.shape
    cells_n = lat_cells * lon_cells
    slots, obs, _ = jacobian.shape
    own_rows = innovation.shape[1]
    n_lat, n_lon = lax.axis_size("lat"), lax.axis_size("lon")
    parts = n_lon // 2
    lon = lax.axis_index("lon")
    f32 = jnp.float32

    def swap(n, k):
        return [(i, i ^ k) for i in range(n)]

    def odd_pairs(n):
        return [(i, (i + 1) % n if i % 2 else (i - 1) % n) for i in range(n)]

    inner_pairs = [(0, 0), (n_lat - 1, n_lat - 1)] + [
        pair for i in range(1, n_lat - 1, 2) for pair in ((i, i + 1), (i + 1, i))]

    def send(x, axis, pairs):
        return lax.ppermute(x, axis, pairs)

    def gather_band(x):
        near = [x] + [send(x, "lon", swap(n_lon, 2 * k)) for k in range(1, parts)]
        return near + [send(piece, "lon", swap(n_lon, 1)) for piece in near]

    def lon_send(to_x, to_s):
        return send(to_x, "lon", swap(n_lon, 1)), send(to_s, "lon", odd_pairs(n_lon))

    def lat_send(to_a, to_b, pairs):
        return send(to_a, "lat", swap(n_lat, 1)), send(to_b, "lat", pairs)

    def lat_sum(tail, from_a, from_b):
        if n_lat != 4:
            return lax.psum(tail, "lat")
        return (tail + send(tail, "lat", swap(n_lat, 2))) + (from_a[slots:] + from_b[slots:])

    def side_shapes(reach):
        return [shape(size, levels) for size in side_rows(reach, lat_cells)[1]]

    def joined_shape(*reaches):
        return shape(sum(sum(side_rows(reach, lat_cells)[1]) for reach in reaches), levels)

    def scatter(message, reach):
        side = side_shapes(reach)[0]
        own, to_x, to_s = call(
            functools.partial(scatter_kernel, dims, slots, reach), "scatter", (field, side, side),
            (message, cells))
        return own, lon_send(to_x, to_s)

    def sides_of(from_a, from_b, reach, joined=()):
        side = side_shapes(reach)[1]
        if joined:
            side = joined_shape(reach)
        strip = shape(reach * lon_cells, levels)
        strip_a, strip_b, to_x, to_s = call(
            functools.partial(sides_kernel, dims, slots, reach, bool(joined)), "sides",
            (strip, strip, side, side), (*joined, from_a, from_b, *cells_near))
        return (strip_a, strip_b), lon_send(to_x, to_s)

    def halo(message, reach):
        from_a, from_b = lat_send(message, message, odd_pairs(n_lat))
        own, own_sides = scatter(message, reach)
        strips, corners = sides_of(from_a, from_b, reach)
        return (own, *strips, *own_sides, *corners), lat_sum(message[slots:], from_a, from_b)

    vmem = pl.BlockSpec(memory_space=pltpu.VMEM)
    smem = pl.BlockSpec(memory_space=pltpu.SMEM)
    hbm = pl.BlockSpec(memory_space=pl.ANY)
    params = pltpu.CompilerParams(vmem_limit_bytes=VMEM_LIMIT)
    shape = lambda *dims: jax.ShapeDtypeStruct(dims, f32)
    scratch = lambda *dims: pltpu.VMEM(dims, f32)
    rows_h = lat_cells + 2 * FRAME
    rows_v = lat_cells + 2 * REACH
    width = lon_cells + 2 * FRAME
    band_rows = n_lon * own_rows
    dims = (lat_cells, lon_cells)
    field = shape(cells_n, levels)
    msg = shape(obs + obs // 2 + 8, LANES)
    wide, tall = shape(rows_h, width, levels), shape(rows_v, width, levels)
    wide_vmem, tall_vmem = scratch(rows_h, width, levels), scratch(rows_v, width, levels)
    field_vmem = scratch(cells_n, levels)
    jac_vmem = scratch(slots, obs, levels)
    faces_vmem = [wide_vmem] * 2 + [tall_vmem] * 3
    sems = lambda count: pltpu.SemaphoreType.DMA((count,))

    def call(kernel, name, outs, ins, scalars=0, far_in=(), far_out=False, scratches=(), params=params):
        out_specs = jax.tree.map(lambda _: vmem, outs)
        if far_out:
            out_specs = (hbm,) * far_out + out_specs[far_out:]
        specs = [smem] * scalars + [vmem] * (len(ins) - scalars) + [hbm] * len(far_in)
        return pl.pallas_call(
            kernel, out_shape=outs, in_specs=specs, out_specs=out_specs,
            scratch_shapes=list(scratches), compiler_params=params, name=name,
        )(*ins, *far_in)

    strip = shape((FRAME + REACH) * lon_cells + 8, levels)
    start_in = (innovation, obs_weight, block_list,
                kappa_h.reshape(cells_n, levels), kappa_v.reshape(cells_n, levels))
    first, root_h, root_v, to_a, to_b = call(
        functools.partial(start_kernel, dims), "start", (shape(obs + 8, LANES), field, field, strip, strip),
        (), far_in=start_in, scratches=[pltpu.VMEM(v.shape, v.dtype) for v in start_in] + [sems(5)],
        params=pltpu.CompilerParams(vmem_limit_bytes=START_LIMIT))
    k_strips = lat_send(to_a, to_b, inner_pairs)
    band = gather_band(first)
    cells_near = [v[(FRAME + REACH) * lon_cells:] for v in k_strips]

    def place_of(row):
        row = row.astype(jnp.int32)
        key = (row // own_rows) ^ lon
        at = (key // 2 + parts * (key % 2)) * own_rows + row % own_rows
        return jnp.where((row >= 0) & (row < band_rows), at, -1)

    all_at = place_of(jnp.stack([piece[obs:obs + 2] for piece in band]).reshape(n_lon, 2 * LANES))
    row_iota = jnp.arange(band_rows, dtype=jnp.int32)
    row_hot = (all_at[:, :, None] == row_iota[None, None, :]).astype(jnp.bfloat16)
    own_at = jnp.pad(place_of(block_list[0]), (0, 2 * LANES - slots), constant_values=-1)
    own_hot = (row_iota[:, None] == own_at[None, :]).astype(jnp.bfloat16)
    cells = jnp.clip(block_list[1:], 0, cells_n - 1)
    cells_flat = cells.reshape(slots)

    adj_scratch = [jac_vmem, scratch(2, obs, LANES), sems(slots // 64)]
    message, weight = call(
        functools.partial(adjoint_kernel, True, parts), "adjoint_first",
        (shape(slots, levels), shape(obs, band_rows)), (*band, own_hot), far_in=(jacobian,),
        scratches=[scratch(obs, band_rows)] + adj_scratch)

    from_a, from_b = lat_send(message, message, inner_pairs)
    own = call(functools.partial(scatter_kernel, dims, slots, FRAME), "scatter", field, (message, cells))
    side = joined_shape(FRAME, REACH)
    k_messages = call(functools.partial(face_sides_kernel, dims), "face_sides", (side, side),
                      (root_h, root_v, *k_strips))
    k_sides = lon_send(*k_messages)
    k_messages, from_a, from_b = lax.optimization_barrier((k_messages, from_a, from_b))
    strips, sides = sides_of(from_a, from_b, FRAME, (own,))
    halos = (own, *strips, *sides)
    faces = call(
        functools.partial(faces_kernel, dims), "faces", (wide, wide, tall, tall, tall),
        (root_h, root_v, *k_strips, *k_sides),
        scratches=[wide_vmem, scratch(rows_h + 1, width, levels)])
    spread_scratch = [field_vmem] * 3 + [
        wide_vmem, wide_vmem, scratch(lat_cells, width, levels), sems(4)]
    near_params = pltpu.CompilerParams(vmem_limit_bytes=NEAR_LIMIT)
    grad, spread, message, near_jac = call(
        functools.partial(spread_kernel, dims, True), "spread_first",
        (field, field, msg, shape(*jacobian.shape)),
        (pass_counts, cells_flat, *halos, *faces), 2, (jacobian,), 2, spread_scratch)

    def adjoint(message):
        return call(
            functools.partial(adjoint_kernel, False, parts), "adjoint_next",
            shape(slots + 16, levels), (*gather_band(message), row_hot, weight, own_hot, near_jac),
            scratches=[scratch(2, obs, LANES)], params=near_params)

    halos, scal0 = halo(adjoint(message), FRAME)
    image, spread_next, message = call(
        functools.partial(spread_kernel, dims, False), "spread_next", (field, field, msg),
        (pass_counts, cells_flat, *halos, scal0, near_jac, *faces), 2, (grad, spread), 2, spread_scratch,
        near_params)
    halos, scal1 = halo(adjoint(message), REACH)
    increment, base, step = call(
        combine_kernel, "combine", (field, field, shape(8, LANES)),
        (scal0, scal1, grad, spread, image, spread_next))
    residual = call(
        functools.partial(final_kernel, dims), "final", field,
        (pass_counts, *halos, base, step, *faces), 1, scratches=[wide_vmem, wide_vmem], params=near_params)
    block = (lat_cells, lon_cells, levels)
    return increment.reshape(block), residual.reshape(block)


def solution(mesh):
    return jax.shard_map(
        local,
        mesh=mesh,
        in_specs=(
            P(None, ("lat", "lon")),
            P(None, ("lat", "lon")),
            P(("lat", "lon"), None, None),
            P(None, ("lat", "lon")),
            P(),
            P("lat", "lon", None),
            P("lat", "lon", None),
        ),
        out_specs=(P("lat", "lon", None), P("lat", "lon", None)),
        check_vma=False,
    )
```
